32 devices in a mesh: dp: 16 (over z, y, x), tensor: 2 (over core).
Axes of the slice: x: 2, y: 2, z: 4, core: 2. Of those that a mesh axis runs over, the one named last changes fastest.
Arguments:
- layer_in: bfloat16 [2, 16, 1024, 1024], P(None, 'dp', 'tensor'), may hold values from -6 to 6
- segment_ids: int32 [2, 16, 1024], P(None, 'dp'), may hold values from 0 to 7, never falling along the last dimension, each value on 1 to 768 neighbouring positions
- w_mix_in: bfloat16 [1024, 1024], P('dp', 'tensor'), may hold values from -0.1875 to 0.1875
- w_query: bfloat16 [1024, 1024], P('dp', 'tensor'), may hold values from -0.1875 to 0.1875
- w_key: bfloat16 [1024, 1024], P('dp', 'tensor'), may hold values from -0.1875 to 0.1875
- w_value: bfloat16 [1024, 1024], P('dp', 'tensor'), may hold values from -0.1875 to 0.1875
- w_attn_out: bfloat16 [1024, 1024], P('tensor', 'dp'), may hold values from -0.5 to 0.5
- w_up: bfloat16 [1024, 4096], P('dp', 'tensor'), may hold values from -0.1875 to 0.1875
- w_down: bfloat16 [4096, 1024], P('tensor', 'dp'), may hold values from -0.09375 to 0.09375
- norm1_gain: bfloat16 [1024], P('dp'), may hold values from 0.5 to 1.5
- norm1_bias: bfloat16 [1024], P('dp'), may hold values from -1.75 to 1.75
- norm2_gain: bfloat16 [1024], P('dp'), may hold values from 0.5 to 1.5
- norm2_bias: bfloat16 [1024], P('dp'), may hold values from -1.75 to 1.75
- ssm_decay: float32 [16, 1024], P(None, 'tensor'), may hold values from 0.9 to 0.995
- ssm_inject: float32 [16, 1024], P(None, 'tensor'), may hold values from -0.875 to 0.875
- ssm_readout: float32 [16, 1024], P(None, 'tensor'), may hold values from -1.5 to 1.5
- out_grad: bfloat16 [2, 16, 1024, 1024], P(None, 'dp', 'tensor'), may hold values from -6 to 6
Outputs:
- layer_out: float32 [2, 16, 1024, 1024], P(None, 'dp', 'tensor')
- in_grad: float32 [2, 16, 1024, 1024], P(None, 'dp', 'tensor')
- grad_w_mix_in: float32 [1024, 1024], P('dp', 'tensor')
- grad_w_query: float32 [1024, 1024], P('dp', 'tensor')
- grad_w_key: float32 [1024, 1024], P('dp', 'tensor')
- grad_w_value: float32 [1024, 1024], P('dp', 'tensor')
- grad_w_attn_out: float32 [1024, 1024], P('tensor', 'dp')
- grad_w_up: float32 [1024, 4096], P('dp', 'tensor')
- grad_w_down: float32 [4096, 1024], P('tensor', 'dp')
- grad_norm1_gain: float32 [1024], P('dp')
- grad_norm1_bias: float32 [1024], P('dp')
- grad_norm2_gain: float32 [1024], P('dp')
- grad_norm2_bias: float32 [1024], P('dp')
- grad_decay: float32 [16, 1024], P(None, 'tensor')
- grad_inject: float32 [16, 1024], P(None, 'tensor')
- grad_readout: float32 [16, 1024], P(None, 'tensor')
The draws below stay inside these ranges and needn't reach their ends.
Inputs may be any that keep to these rules, and one draw needn't show every extreme that they name: `segment_ids`: ids never decrease along a sequence; a document holds at most 768 tokens, and some document holds exactly 768.
All inputs are finite; a program needn't handle non-finite values.
Results may differ from the reference program's by a relative error of at most 0.015.
Values may be sent and summed in bfloat16 or wider, within the bound.
No kernel may reach another device: no remote copies, remote signals or barrier semaphores. Data moves between devices by JAX's collectives and lax.ppermute only.
A program may use at most 256 MiB of HBM per device.

```python
import math
import jax
import jax.numpy as jnp
import numpy as np
from jax import lax

D = 1024
HEADS = 8
HEAD_DIM = 128
FF = 4096
NSTATE = 16
BLOCK = 512
CTX = 128
SCAN_BLOCK = 64
SEQ_LEN = 1024
MICRO = 2
SEQS = 16
DOCS = 8
DOC_MAX = 768


def level_of(key, shape, pieces, smallest, top_value):
    def one(axis_at, shards_of):
        steps = jax.random.uniform(jax.random.fold_in(jax.random.fold_in(key, 6), axis_at), (shards_of,), jnp.float32, smallest / len(pieces), top_value / len(pieces))
        return jnp.repeat(jnp.exp(steps), shape[axis_at] // shards_of).reshape((-1,) + (1,) * (len(shape) - axis_at - 1))

    level = one(*pieces[0])
    for cut in pieces[1:]:
        level = level * one(*cut)
    return level


def profile(count, total, reach, lean):
    weights = [(1 << 20) // math.isqrt(standing ** lean) + 1 for standing in range(2, count + 1)]
    surplus, counts = total - reach - (count - 1), [1] * (count - 1)
    while surplus > 0:
        free = [i for i in range(count - 1) if counts[i] < reach]
        mass, remaining = sum([weights[i] for i in free]), surplus
        for i in free:
            extra = min(reach - counts[i], max(1, remaining * weights[i] // mass), surplus)
            counts[i] = counts[i] + extra
            surplus = surplus - extra
    return np.array([reach] + counts)


def uneven(rng, amount, total, bound, lean):
    if amount == 2:
        one = jax.random.randint(rng, (), max(1, total - bound), min(bound, total - 1) + 1)
        return jnp.stack([one, total - one])
    lengths = jnp.asarray(profile(amount, total, bound, lean), jnp.int32)
    pairs = (amount - 1) // 2
    donor, taker = lengths[1:1 + 2 * pairs:2], lengths[2:2 + 2 * pairs:2]
    slack = jnp.minimum(donor - 1, bound - taker)
    shifted = jax.random.randint(jax.random.fold_in(rng, 1), (pairs,), 0, 1 << 20) % (slack + 1)
    lengths = lengths.at[1:1 + 2 * pairs:2].set(donor - shifted).at[2:2 + 2 * pairs:2].set(taker + shifted)
    return lengths[jax.random.permutation(jax.random.fold_in(rng, 2), amount)]


def normal_values(rng, extent, width, bound, split=(), kind=jnp.bfloat16):
    values = jax.random.normal(rng, extent, jnp.float32) * width
    if len(split) > 0:
        values = level_of(rng, extent, split, -0.22, 0.18) * values
    return jnp.clip(values, min=-bound, max=bound).astype(kind)


def setup_inputs(seed: int = 0) -> dict:
    key_list = jax.random.split(jax.random.key(seed), 18)
    layer_in = normal_values(key_list[0], (MICRO, SEQS, SEQ_LEN, D), 1.0, 6.0, ((1, 16), (2, 2)))
    segment_ids = jax.vmap(lambda own: jnp.searchsorted(jnp.cumsum(uneven(own, DOCS, SEQ_LEN, DOC_MAX, 1)), jnp.arange(SEQ_LEN), side="right"))(jax.random.split(key_list[1], MICRO * SEQS)).reshape((MICRO, SEQS, SEQ_LEN)).astype(jnp.int32)
    w_mix_in = normal_values(key_list[2], (D, D), D ** -0.5, 0.1875, ((0, 16), (1, 2)))
    w_query = normal_values(key_list[3], (D, D), D ** -0.5, 0.1875, ((0, 16), (1, 2)))
    w_key = normal_values(key_list[4], (D, D), D ** -0.5, 0.1875, ((0, 16), (1, 2)))
    w_value = normal_values(key_list[5], (D, D), D ** -0.5, 0.1875, ((0, 16), (1, 2)))
    w_attn_out = normal_values(key_list[6], (D, D), (D // 8) ** -0.5, 0.5, ((0, 2), (1, 16)))
    w_up = normal_values(key_list[7], (D, FF), D ** -0.5, 0.1875, ((0, 16), (1, 2)))
    w_down = normal_values(key_list[8], (FF, D), FF ** -0.5, 0.09375, ((0, 2), (1, 16)))
    norm1_gain = jnp.clip(1.0 + 0.1 * jax.random.normal(key_list[9], (D,), jnp.float32), 0.5, 1.5).astype(jnp.bfloat16)
    norm1_bias = normal_values(key_list[10], (D,), 0.3, 1.75, ((0, 16),))
    norm2_gain = jnp.clip(1.0 + 0.1 * jax.random.normal(key_list[11], (D,), jnp.float32), 0.5, 1.5).astype(jnp.bfloat16)
    norm2_bias = normal_values(key_list[12], (D,), 0.3, 1.75, ((0, 16),))
    ssm_decay = jnp.clip(0.9 + 0.09500003 * jax.random.uniform(key_list[13], (NSTATE, D), jnp.float32) ** level_of(key_list[13], (NSTATE, D), ((1, 2),), -0.2, 0.2), 0.9, 0.995)
    ssm_inject = normal_values(key_list[14], (NSTATE, D), 0.15, 0.875, ((1, 2),), jnp.float32)
    ssm_readout = normal_values(key_list[15], (NSTATE, D), NSTATE ** -0.5, 1.5, ((1, 2),), jnp.float32)
    out_grad = normal_values(key_list[16], (MICRO, SEQS, SEQ_LEN, D), 1.0, 6.0, ((1, 16), (2, 2)))
    return {"layer_in": layer_in, "segment_ids": segment_ids, "w_mix_in": w_mix_in, "w_query": w_query, "w_key": w_key, "w_value": w_value, "w_attn_out": w_attn_out, "w_up": w_up, "w_down": w_down, "norm1_gain": norm1_gain, "norm1_bias": norm1_bias, "norm2_gain": norm2_gain, "norm2_bias": norm2_bias, "ssm_decay": ssm_decay, "ssm_inject": ssm_inject, "ssm_readout": ssm_readout, "out_grad": out_grad}


norm_eps = 1e-05
masked_score = -1e+30

@jax.custom_vjp
def low(v):
    return lax.optimization_barrier(v.astype(jnp.bfloat16)).astype(jnp.float32)

@jax.custom_vjp
def low_back(v):
    return v

def low_keep(v):
    return (low(v), None)

def low_pass(kept, grad):
    return (grad,)

def back_keep(v):
    return (v, None)

def back_low(kept, grad):
    return (low(grad),)
low.defvjp(low_keep, low_pass)
low_back.defvjp(back_keep, back_low)

def product(left_op, right_op):
    return jnp.dot(left_op, right_op, precision=lax.Precision.HIGHEST)

def norm_rows(values, gain_vec, bias_vec):
    centred = values - lax.optimization_barrier(jnp.mean(values, axis=-1, keepdims=True))
    inverse = lax.rsqrt(lax.optimization_barrier(jnp.mean(centred * centred, axis=-1, keepdims=True)) + norm_eps)
    return centred * inverse * gain_vec + bias_vec

def state_blocks(driving, carry_keep, decay_rate, inject, readout):
    length, channels = driving.shape
    span = SCAN_BLOCK
    count_blocks = length // span
    states_count = decay_rate.shape[0]
    log_rate = jnp.log(decay_rate)
    offsets = jnp.arange(span, dtype=jnp.float32)
    power_up = jnp.exp(offsets[:, None, None] * log_rate[None])
    power_next = jnp.exp((offsets + 1.0)[:, None, None] * log_rate[None])
    power_down = jnp.exp(-offsets[:, None, None] * log_rate[None])
    position = jnp.arange(span, dtype=jnp.int32)
    ordered = position[:, None] >= position[None, :]

    def one_block(carry_state, parts):
        block_in, block_keep = parts
        breaks = jnp.cumsum(1.0 - block_keep)
        same_run = jnp.where(ordered & (breaks[:, None] == breaks[None, :]), 1.0, 0.0).astype(driving.dtype)
        alive = jnp.where(breaks == 0.0, 1.0, 0.0).astype(driving.dtype)
        scaled = power_down * inject[None] * block_in[:, None, :]
        summed = jnp.dot(same_run, scaled.reshape(span, states_count * channels), precision=lax.Precision.HIGHEST).reshape(span, states_count, channels)
        states = power_up * summed + alive[:, None, None] * power_next * carry_state[None]
        return (states[span - 1], lax.optimization_barrier(jnp.sum(states * readout[None], axis=1)))
    blocks_in = driving.reshape(count_blocks, span, channels)
    blocks_keep = carry_keep.reshape(count_blocks, span)
    start_state = jnp.zeros(decay_rate.shape, driving.dtype)
    outputs = lax.scan(jax.checkpoint(one_block), start_state, (blocks_in, blocks_keep))[1]
    return outputs.reshape(length, channels)

def block_attention(query_rows, key_all, value_all, segment_row):
    length = query_rows.shape[0]
    query_heads = query_rows.reshape(length, HEADS, HEAD_DIM)
    key_pad = jnp.concatenate([jnp.zeros((CTX, HEADS, HEAD_DIM), jnp.float32), key_all.reshape(length, HEADS, HEAD_DIM)], axis=0)
    value_pad = jnp.concatenate([jnp.zeros((CTX, HEADS, HEAD_DIM), jnp.float32), value_all.reshape(length, HEADS, HEAD_DIM)], axis=0)
    segment_pad = jnp.concatenate([jnp.full((CTX,), -1, jnp.int32), segment_row.astype(jnp.int32)])
    score_scale = HEAD_DIM ** (-0.5)

    def one_block(block_index):
        block_first = (block_index * BLOCK).astype(jnp.int32)
        query_block = lax.dynamic_slice_in_dim(query_heads, block_first, BLOCK, 0)
        key_block = lax.dynamic_slice_in_dim(key_pad, block_first, BLOCK + CTX, 0)
        value_block = lax.dynamic_slice_in_dim(value_pad, block_first, BLOCK + CTX, 0)
        segment_query = lax.dynamic_slice_in_dim(segment_pad, block_first + CTX, BLOCK, 0)
        segment_key = lax.dynamic_slice_in_dim(segment_pad, block_first, BLOCK + CTX, 0)
        query_pos = jnp.arange(BLOCK, dtype=jnp.int32)[:, None] + CTX
        key_pos = jnp.arange(BLOCK + CTX, dtype=jnp.int32)[None, :]
        allowed = (key_pos <= query_pos) & (segment_key[None, :] == segment_query[:, None])
        scores = low_back(jnp.einsum('ihd,jhd->hij', query_block, key_block, precision=lax.Precision.HIGHEST) * score_scale)
        scores = jnp.where(allowed[None], scores, masked_score)
        attn_probs = low(jax.nn.softmax(scores, axis=-1))
        return jnp.einsum('hij,jhd->ihd', attn_probs, value_block, precision=lax.Precision.HIGHEST)
    blocks = lax.map(jax.checkpoint(one_block), jnp.arange(length // BLOCK, dtype=jnp.int32))
    return blocks.reshape(length, HEADS * HEAD_DIM)

def layer_forward(weights_now, rows_now, segment_row):
    w_mix_in, w_query, w_key, w_value, w_attn_out, w_up, w_down, gain_one, bias_one, gain_two, bias_two, decay_rate, inject, readout = weights_now
    carry_keep = jnp.concatenate([jnp.zeros((1,), jnp.float32), (segment_row[1:] == segment_row[:-1]).astype(jnp.float32)])
    normed = low(norm_rows(rows_now, gain_one, bias_one))
    mixed_in = low_back(product(normed, w_mix_in))
    ssm_out = low(state_blocks(mixed_in, carry_keep, decay_rate, inject, readout))
    query_rows = low(low_back(product(normed, w_query)))
    key_all = low(low_back(product(ssm_out, w_key)))
    value_all = low(low_back(product(ssm_out, w_value)))
    attended = low(low_back(block_attention(query_rows, key_all, value_all, segment_row)))
    middle = rows_now + low_back(product(attended, w_attn_out))
    normed_two = low(norm_rows(middle, gain_two, bias_two))
    hidden_pre = low_back(product(normed_two, w_up))
    hidden = low(jax.nn.gelu(hidden_pre, approximate=False))
    return middle + low_back(product(hidden, w_down))

def reference(layer_in, segment_ids, w_mix_in, w_query, w_key, w_value, w_attn_out, w_up, w_down, norm1_gain, norm1_bias, norm2_gain, norm2_bias, ssm_decay, ssm_inject, ssm_readout, out_grad):
    weights_all = tuple((member.astype(jnp.float32) for member in (w_mix_in, w_query, w_key, w_value, w_attn_out, w_up, w_down, norm1_gain, norm1_bias, norm2_gain, norm2_bias, ssm_decay, ssm_inject, ssm_readout)))
    count_seqs = MICRO * SEQS
    rows_all = layer_in.astype(jnp.float32).reshape(count_seqs, SEQ_LEN, D)
    segment_all = segment_ids.astype(jnp.int32).reshape(count_seqs, SEQ_LEN)
    cot_all = out_grad.astype(jnp.float32).reshape(count_seqs, SEQ_LEN, D)

    def one_sequence(totals, inputs_now):
        rows_now, segment_row, cot_now = inputs_now

        def forward_fn(weights_now, rows_given):
            return layer_forward(weights_now, rows_given, segment_row)
        result, pullback = jax.vjp(forward_fn, weights_all, rows_now)
        grad_weights, grad_rows = pullback(cot_now)
        totals = tuple((a + b for a, b in zip(totals, grad_weights)))
        return (totals, (result, grad_rows))
    zeros_all = tuple((jnp.zeros_like(member) for member in weights_all))
    totals, (outputs, grad_in) = lax.scan(one_sequence, zeros_all, (rows_all, segment_all, cot_all))
    shape_out = (MICRO, SEQS, SEQ_LEN, D)
    return (outputs.reshape(shape_out), grad_in.reshape(shape_out), totals[0], totals[1], totals[2], totals[3], totals[4], totals[5], totals[6], totals[7], totals[8], totals[9], totals[10], totals[11], totals[12], totals[13])
```

```python
import functools
import math

import jax
import jax.numpy as jnp
from jax import lax
from jax.experimental import pallas as pl
from jax.experimental.pallas import tpu as pltpu
from jax.sharding import PartitionSpec as P

HEAD_DIM = 128
BLOCK = 512
CTX = 128
NDOCS = 8
LANES = 128
QTILE = 256

norm_eps = 1e-05
masked_score = -1e30
VMEM = 56 * 1024 * 1024
BF = jnp.bfloat16
F32 = jnp.float32


def dot_plain(left_op, right_op):
    return jnp.dot(left_op, right_op, preferred_element_type=F32)


def dot_last(left_op, right_op):
    return lax.dot_general(left_op, right_op, (((1,), (1,)), ((), ())), preferred_element_type=F32)


def dot_first(left_op, right_op):
    return lax.dot_general(left_op, right_op, (((0,), (0,)), ((), ())), preferred_element_type=F32)


def params(count=1):
    return pltpu.CompilerParams(
        dimension_semantics=("arbitrary",) * count, vmem_limit_bytes=VMEM
    )


def bits_of(count):
    out = []
    bit = 1
    while bit < count:
        out.append(bit)
        bit *= 2
    return out


def gather_order(count, flip):
    bits = bits_of(count)
    low = bits[:2]
    return bits[2:] + (low[::-1] if flip else low)


def swap(values, axis_name, count, bit):
    return lax.ppermute(values, axis_name, [(i, i ^ bit) for i in range(count)])


def after(values, earlier):
    return lax.optimization_barrier((values, earlier))[0]


def gather_rows(shard, count, index, flip):
    values = shard
    present = []
    half_way = None
    for bit in gather_order(count, flip):
        other = swap(values, "dp", count, bit)
        place = sum(1 for p in present if p > bit)
        upper = (index // bit) % 2 == 1
        first = jnp.where(upper, other, values)
        second = jnp.where(upper, values, other)
        values = jnp.stack([first, second], axis=place)
        present.append(bit)
        if len(present) == 2:
            half_way = values
    return values.reshape((count * shard.shape[0],) + shard.shape[1:]), half_way


def scatter_rows(full, count, index, flip):
    bits = bits_of(count)
    rows = full.shape[0] // count
    values = full.reshape((2,) * len(bits) + (rows,) + full.shape[1:])
    present = sorted(bits, reverse=True)
    for bit in gather_order(count, flip)[::-1]:
        place = present.index(bit)
        upper = (index // bit) % 2
        send = lax.dynamic_index_in_dim(values, 1 - upper, place, keepdims=False)
        keep = lax.dynamic_index_in_dim(values, upper, place, keepdims=False)
        got = swap(send, "dp", count, bit)
        present.remove(bit)
        values = keep.astype(F32) + got.astype(F32)
        if present:
            values = values.astype(BF)
    return values


def sum_all(values, count):
    for bit in bits_of(count):
        values = values + swap(values, "dp", count, bit)
    return values


def join_pair(own, other, side, axis):
    return jnp.where(
        side == 0,
        jnp.concatenate([own, other], axis=axis),
        jnp.concatenate([other, own], axis=axis),
    )


def pair(values):
    return lax.ppermute(values, "tensor", [(0, 1), (1, 0)])


def norm_of(values, gain_vec, bias_vec):
    centred = values - jnp.mean(values, axis=-1, keepdims=True)
    inverse = lax.rsqrt(jnp.mean(centred * centred, axis=-1, keepdims=True) + norm_eps)
    return centred * inverse * gain_vec + bias_vec


def to_steps(steps_ref, row_first, values, col_first):
    rows, cols = values.shape
    tiles = steps_ref.shape[1]
    for j in range(cols // LANES):
        steps_ref[pl.ds(row_first, rows), col_first // LANES + j, :] = values[
            :, j * LANES : (j + 1) * LANES
        ]


def run_docs(starts_ref, step, make_start, finish, backward, unroll=8):
    for doc in range(NDOCS):
        d = NDOCS - 1 - doc if backward else doc
        first = starts_ref[d]
        last = starts_ref[d + 1]
        length = last - first
        groups = length // unroll
        carry = make_start(doc)

        def group_body(g, carry):
            base = last - 1 - g * unroll if backward else first + g * unroll
            for i in range(unroll):
                carry = step(base - i if backward else base + i, carry)
            return carry

        carry = lax.fori_loop(0, groups, group_body, carry)
        done = groups * unroll

        def one_body(i, carry):
            return step(last - 1 - done - i if backward else first + done + i, carry)

        carry = lax.fori_loop(0, length - done, one_body, carry)
        finish(carry)


def ssm_forward_kernel(
    starts_ref, rows_ref, gain_ref, bias_ref, mix_ref, decay_ref, coef_ref,
    normed_ref, drive_ref, out_ref, y_ref,
):
    length, width = rows_ref.shape
    states = decay_ref.shape[0]
    chunk = 256

    def project(i, _):
        r = pl.multiple_of(i * chunk, chunk)
        normed = norm_of(
            rows_ref[pl.ds(r, chunk), :].astype(F32), gain_ref[...], bias_ref[...]
        ).astype(BF)
        normed_ref[pl.ds(r, chunk), :] = normed
        for c in range(0, width, 256):
            to_steps(drive_ref, r, dot_plain(normed, mix_ref[:, c : c + 256]), c)
        return 0

    lax.fori_loop(0, length // chunk, project, 0)

    def step(t, state):
        u = drive_ref[t]
        new = []
        parts = []
        for n in range(states):
            s = decay_ref[n] * state[n] + u
            new.append(s)
            parts.append(coef_ref[n] * s)
        while len(parts) > 1:
            parts = [parts[k] + parts[k + 1] for k in range(0, len(parts), 2)]
        y_ref[t] = parts[0]
        return tuple(new)

    zero = jnp.zeros(decay_ref.shape[1:], F32)
    run_docs(starts_ref, step, lambda doc: (zero,) * states, lambda carry: None, False)

    def write(i, _):
        r = pl.multiple_of(i * chunk, chunk)
        for j in range(width // LANES):
            out_ref[pl.ds(r, chunk), j * LANES : (j + 1) * LANES] = y_ref[
                pl.ds(r, chunk), j, :
            ].astype(BF)
        return 0

    lax.fori_loop(0, length // chunk, write, 0)


def ssm_forward(starts, rows, gain_vec, bias_vec, mix, decay, coef):
    length, width = rows.shape
    tiles = width // LANES
    vm = pl.BlockSpec(memory_space=pltpu.VMEM)
    return pl.pallas_call(
        ssm_forward_kernel,
        out_shape=(
            jax.ShapeDtypeStruct((length, width), BF),
            jax.ShapeDtypeStruct((length, tiles, LANES), F32),
            jax.ShapeDtypeStruct((length, width), BF),
        ),
        in_specs=[pl.BlockSpec(memory_space=pltpu.SMEM)] + [vm] * 6,
        out_specs=(vm,) * 3,
        scratch_shapes=[pltpu.VMEM((length, tiles, LANES), F32)],
        compiler_params=pltpu.CompilerParams(vmem_limit_bytes=VMEM),
        cost_estimate=pl.CostEstimate(
            flops=2 * length * width * width + 40 * 16 * length * width,
            bytes_accessed=16 * length * width,
            transcendentals=0,
        ),
        name="ssm_forward",
    )(starts, rows, gain_vec, bias_vec, mix, decay, coef)


def ssm_backward_kernel(
    starts_ref, gkey_ref, gvalue_ref, wkey_ref, wvalue_ref, drive_ref, decay_ref, coef_ref,
    gmixed_ref, sum_ref, dsum_ref, g_ref, gm_ref,
):
    length, width = gkey_ref.shape
    states = decay_ref.shape[0]
    chunk = 256

    def project(i, _):
        r = pl.multiple_of(i * chunk, chunk)
        gkey = gkey_ref[pl.ds(r, chunk), :]
        gvalue = gvalue_ref[pl.ds(r, chunk), :]
        for c in range(0, width, 256):
            to_steps(
                g_ref,
                r,
                dot_last(gkey, wkey_ref[c : c + 256, :])
                + dot_last(gvalue, wvalue_ref[c : c + 256, :]),
                c,
            )
        return 0

    lax.fori_loop(0, length // chunk, project, 0)

    zero = jnp.zeros(decay_ref.shape[1:], F32)
    part = states // 2
    for half in range(2):
        base = half * part

        def step(t, carry, half=half, base=base):
            mu, rho, total, dtotal = carry
            u = drive_ref[t]
            g = g_ref[t]
            new_mu, new_rho, new_total, new_dtotal, parts = [], [], [], [], []
            for n in range(part):
                a = decay_ref[base + n]
                r = a * rho[n] + mu[n]
                m = a * mu[n] + g
                new_mu.append(m)
                new_rho.append(r)
                new_total.append(total[n] + u * m)
                new_dtotal.append(dtotal[n] + u * r)
                parts.append(coef_ref[base + n] * m)
            while len(parts) > 1:
                parts = [parts[k] + parts[k + 1] for k in range(0, len(parts), 2)]
            if half == 0:
                gm_ref[t] = parts[0]
            else:
                gm_ref[t] = gm_ref[t] + parts[0]
            return tuple(new_mu), tuple(new_rho), tuple(new_total), tuple(new_dtotal)

        for n in range(part):
            sum_ref[base + n] = zero
            dsum_ref[base + n] = zero

        def make_start(doc):
            zeros = (zero,) * part
            return zeros, zeros, zeros, zeros

        def finish(carry, base=base):
            for n in range(part):
                sum_ref[base + n] = sum_ref[base + n] + carry[2][n]
                dsum_ref[base + n] = dsum_ref[base + n] + carry[3][n]

        run_docs(starts_ref, step, make_start, finish, True)

    def write(i, _):
        r = pl.multiple_of(i * chunk, chunk)
        for j in range(width // LANES):
            gmixed_ref[pl.ds(r, chunk), j * LANES : (j + 1) * LANES] = gm_ref[
                pl.ds(r, chunk), j, :
            ].astype(BF)
        return 0

    lax.fori_loop(0, length // chunk, write, 0)


def ssm_backward(starts, gkey, gvalue, wkey, wvalue, drive, decay, coef):
    length, width = gkey.shape
    tiles = width // LANES
    vm = pl.BlockSpec(memory_space=pltpu.VMEM)
    return pl.pallas_call(
        ssm_backward_kernel,
        out_shape=(
            jax.ShapeDtypeStruct((length, width), BF),
            jax.ShapeDtypeStruct(decay.shape, F32),
            jax.ShapeDtypeStruct(decay.shape, F32),
        ),
        in_specs=[pl.BlockSpec(memory_space=pltpu.SMEM)] + [vm] * 7,
        out_specs=(vm,) * 3,
        scratch_shapes=[
            pltpu.VMEM((length, tiles, LANES), F32),
            pltpu.VMEM((length, tiles, LANES), F32),
        ],
        compiler_params=pltpu.CompilerParams(vmem_limit_bytes=VMEM),
        cost_estimate=pl.CostEstimate(
            flops=4 * length * width * width + 100 * 16 * length * width,
            bytes_accessed=16 * length * width,
            transcendentals=0,
        ),
        name="ssm_backward",
    )(starts, gkey, gvalue, wkey, wvalue, drive, decay, coef)


def attention_tiles(length):
    tiles = []
    for first in range(0, length, QTILE):
        block_first = first // BLOCK * BLOCK
        key_first = max(0, block_first - CTX)
        tiles.append((first, key_first, first + QTILE - key_first))
    return tiles


def fill_bias(seg_col_ref, seg_row_ref, bias_ref, tiles):
    at = 0
    for first, key_first, count in tiles:
        same = seg_col_ref[first : first + QTILE, :] == seg_row_ref[:, key_first : key_first + count]
        query_pos = lax.broadcasted_iota(jnp.int32, (QTILE, count), 0) + first
        key_pos = lax.broadcasted_iota(jnp.int32, (QTILE, count), 1) + key_first
        bias_ref[:, at : at + count] = jnp.where(
            same & (key_pos <= query_pos), 0.0, masked_score
        ).astype(F32)
        at += count


EXP_SCALE = HEAD_DIM ** (-0.5) * math.log2(math.e)


def attention_forward_kernel(
    seg_col_ref, seg_row_ref, query_ref, key_ref, value_ref, out_ref, lse_ref, bias_ref
):
    tiles = attention_tiles(query_ref.shape[0])

    @pl.when(pl.program_id(0) == 0)
    def _():
        fill_bias(seg_col_ref, seg_row_ref, bias_ref, tiles)

    at = 0
    for first, key_first, count in tiles:
        keys = slice(key_first, key_first + count)
        scores = dot_last(query_ref[first : first + QTILE, :], key_ref[keys, :])
        scores = scores * EXP_SCALE + bias_ref[:, at : at + count]
        top = jnp.max(scores, axis=-1, keepdims=True)
        raised = jnp.exp2(scores - top)
        total = jnp.sum(raised, axis=-1, keepdims=True)
        probs = (raised * (1.0 / total)).astype(BF)
        out_ref[first : first + QTILE, :] = dot_plain(probs, value_ref[keys, :]).astype(BF)
        lse_ref[0, first : first + QTILE, :] = top + jnp.log2(total)
        at += count


def attention_forward(seg_col, seg_row, query, key, value):
    length, width = query.shape
    heads = width // HEAD_DIM
    tiles = attention_tiles(length)
    cols = sum(t[2] for t in tiles)
    head = pl.BlockSpec((length, HEAD_DIM), lambda h: (0, h))
    whole = lambda shape: pl.BlockSpec(shape, lambda h: (0, 0))
    return pl.pallas_call(
        attention_forward_kernel,
        grid=(heads,),
        out_shape=(
            jax.ShapeDtypeStruct((length, width), BF),
            jax.ShapeDtypeStruct((heads, length, 1), F32),
        ),
        in_specs=[whole((length, 1)), whole((1, length)), head, head, head],
        out_specs=(head, pl.BlockSpec((1, length, 1), lambda h: (h, 0, 0))),
        scratch_shapes=[pltpu.VMEM((QTILE, cols), F32)],
        compiler_params=params(),
        cost_estimate=pl.CostEstimate(
            flops=4 * QTILE * cols * width,
            bytes_accessed=8 * length * width,
            transcendentals=QTILE * cols * heads,
        ),
        name="attention_forward",
    )(seg_col, seg_row, query, key, value)


def attention_backward_kernel(
    seg_col_ref, seg_row_ref, query_ref, key_ref, value_ref, lse_ref, gout_ref,
    gquery_ref, gkey_ref, gvalue_ref, bias_ref, gk_ref, gv_ref,
):
    tiles = attention_tiles(query_ref.shape[0])
    scale = HEAD_DIM ** (-0.5)

    @pl.when(pl.program_id(0) == 0)
    def _():
        fill_bias(seg_col_ref, seg_row_ref, bias_ref, tiles)

    gk_ref[...] = jnp.zeros_like(gk_ref)
    gv_ref[...] = jnp.zeros_like(gv_ref)
    at = 0
    for first, key_first, count in tiles:
        keys = slice(key_first, key_first + count)
        query = query_ref[first : first + QTILE, :]
        gout = gout_ref[first : first + QTILE, :]
        scores = dot_last(query, key_ref[keys, :]) * EXP_SCALE + bias_ref[:, at : at + count]
        probs = jnp.exp2(scores - lse_ref[0, first : first + QTILE, :])
        gv_ref[keys, :] = gv_ref[keys, :] + dot_first(probs.astype(BF), gout)
        gprobs = dot_last(gout, value_ref[keys, :])
        inner = jnp.sum(probs * gprobs, axis=-1, keepdims=True)
        gscores = (probs * (gprobs - inner)).astype(BF)
        gquery_ref[first : first + QTILE, :] = (
            dot_plain(gscores, key_ref[keys, :]) * scale
        ).astype(BF)
        gk_ref[keys, :] = gk_ref[keys, :] + dot_first(gscores, query)
        at += count
    gkey_ref[...] = (gk_ref[...] * scale).astype(BF)
    gvalue_ref[...] = gv_ref[...].astype(BF)


def attention_backward(seg_col, seg_row, query, key, value, lse, gout):
    length, width = query.shape
    heads = width // HEAD_DIM
    tiles = attention_tiles(length)
    cols = sum(t[2] for t in tiles)
    head = pl.BlockSpec((length, HEAD_DIM), lambda h: (0, h))
    whole = lambda shape: pl.BlockSpec(shape, lambda h: (0, 0))
    return pl.pallas_call(
        attention_backward_kernel,
        grid=(heads,),
        out_shape=(jax.ShapeDtypeStruct((length, width), BF),) * 3,
        in_specs=[whole((length, 1)), whole((1, length)), head, head, head]
        + [pl.BlockSpec((1, length, 1), lambda h: (h, 0, 0)), head],
        out_specs=(head,) * 3,
        scratch_shapes=[
            pltpu.VMEM((QTILE, cols), F32),
            pltpu.VMEM((length, HEAD_DIM), F32),
            pltpu.VMEM((length, HEAD_DIM), F32),
        ],
        compiler_params=params(),
        cost_estimate=pl.CostEstimate(
            flops=10 * QTILE * cols * width,
            bytes_accessed=14 * length * width,
            transcendentals=QTILE * cols * heads,
        ),
        name="attention_backward",
    )(seg_col, seg_row, query, key, value, lse, gout)


def norm_backward(grad, values, gain_vec):
    centred = values - jnp.mean(values, axis=-1, keepdims=True)
    inverse = lax.rsqrt(jnp.mean(centred * centred, axis=-1, keepdims=True) + norm_eps)
    xhat = centred * inverse
    dxhat = grad * gain_vec
    back = (
        dxhat
        - jnp.mean(dxhat, axis=-1, keepdims=True)
        - xhat * jnp.mean(dxhat * xhat, axis=-1, keepdims=True)
    ) * inverse
    return back, jnp.sum(grad * xhat, axis=0), jnp.sum(grad, axis=0)


def gelu_parts(values):
    below = 0.5 * lax.erfc(values * (-(2.0**-0.5)))
    density = jnp.exp(-0.5 * values * values) * ((2.0 * math.pi) ** -0.5)
    return values * below, below + values * density


def per_device(
    count,
    layer_in,
    segment_ids,
    w_mix_in,
    w_query,
    w_key,
    w_value,
    w_attn_out,
    w_up,
    w_down,
    norm1_gain,
    norm1_bias,
    norm2_gain,
    norm2_bias,
    ssm_decay,
    ssm_inject,
    ssm_readout,
    out_grad,
):
    index = lax.axis_index("dp")
    side = lax.axis_index("tensor")
    half = layer_in.shape[2]
    width = layer_in.shape[3]
    length = 2 * half
    tiles = width // LANES
    states = ssm_decay.shape[0]

    def whole_sequence(halves):
        own = lax.dynamic_index_in_dim(halves, side, 0, keepdims=False)
        other = pair(lax.dynamic_index_in_dim(halves, 1 - side, 0, keepdims=False))
        return join_pair(own, other, side, 0)

    def both_halves(sequence):
        own = lax.dynamic_slice_in_dim(sequence, side * half, half, 0)
        other = pair(lax.dynamic_slice_in_dim(sequence, (1 - side) * half, half, 0))
        return jnp.where(side == 0, jnp.stack([own, other]), jnp.stack([other, own]))

    norms = jnp.stack([norm1_gain, norm1_bias, norm2_gain, norm2_bias])[None]
    norms_all, _ = gather_rows(norms, count, index, False)
    mix_half, mark = gather_rows(w_mix_in, count, index, False)
    attn_shard = jnp.concatenate([w_query, w_key, w_value, w_attn_out.T], axis=1)
    attn_half, mark = gather_rows(after(attn_shard, mark), count, index, True)
    up_half, mark = gather_rows(after(w_up, mark), count, index, False)
    down_half, mark = gather_rows(after(w_down.T, mark), count, index, True)
    norms_all = norms_all.astype(F32).transpose(1, 0, 2).reshape(4, width)
    gain_one, bias_one, gain_two, bias_two = (norms_all[i : i + 1] for i in range(4))
    mix_full = join_pair(mix_half, pair(mix_half), side, 1)
    attn_other = pair(attn_half)
    cols = w_query.shape[1]
    query_full, key_full, value_full, out_full = (
        join_pair(
            attn_half[:, i * cols : (i + 1) * cols],
            attn_other[:, i * cols : (i + 1) * cols],
            side,
            1,
        )
        for i in range(4)
    )

    coefs = jnp.stack([ssm_decay, ssm_inject, ssm_readout])
    coefs = join_pair(coefs, pair(coefs), side, 2)
    decay, inject, readout = coefs.reshape(3, states, tiles, LANES)
    coef = inject * readout

    rows = whole_sequence(layer_in[:, 0])
    cot = whole_sequence(out_grad[:, 0])
    cot_both = jnp.concatenate([cot, pair(cot)], axis=0)
    segments = lax.dynamic_index_in_dim(segment_ids[:, 0], side, 0, keepdims=False)
    starts = jnp.sum(
        (segments[None, :] < jnp.arange(16, dtype=jnp.int32)[:, None]).astype(jnp.int32), axis=1
    )
    seg_col, seg_row = segments[:, None], segments[None, :]

    normed, drive, ssm_out = ssm_forward(
        starts, rows, gain_one, bias_one, mix_full, decay, coef
    )
    query = dot_plain(normed, query_full).astype(BF)
    key = dot_plain(ssm_out, key_full).astype(BF)
    value = dot_plain(ssm_out, value_full).astype(BF)
    attended, lse = attention_forward(seg_col, seg_row, query, key, value)
    middle = rows.astype(F32) + dot_last(attended, out_full)
    normed_two = norm_of(middle, gain_two, bias_two).astype(BF)

    normed_both = jnp.concatenate([normed_two, pair(normed_two)], axis=0)
    hidden_pre = dot_plain(normed_both, up_half)
    hidden, slope = gelu_parts(hidden_pre)
    hidden = hidden.astype(BF)
    grad_pre = (dot_plain(cot_both, down_half) * slope).astype(BF)
    grad_two_part = dot_last(grad_pre, up_half)
    grad_two = grad_two_part[:length] + pair(grad_two_part[length:].astype(BF)).astype(F32)
    grad_up = dot_first(normed_both, grad_pre).astype(BF)
    grad_down = dot_first(cot_both, hidden).astype(BF)
    branch = dot_last(hidden, down_half)
    layer_out = middle + branch[:length] + pair(branch[length:].astype(BF)).astype(F32)
    layer_out = both_halves(layer_out)
    shard_up = scatter_rows(grad_up, count, index, False)
    shard_down = scatter_rows(grad_down, count, index, True)

    back_two, grad_gain_two, grad_bias_two = norm_backward(grad_two, middle, gain_two)
    grad_middle = cot.astype(F32) + back_two
    grad_branch = grad_middle.astype(BF)
    grad_attended = dot_plain(grad_branch, out_full).astype(BF)
    grad_query, grad_key, grad_value = attention_backward(
        seg_col, seg_row, query, key, value, lse, grad_attended
    )

    def pair_sum(grad):
        mine = lax.dynamic_slice_in_dim(grad, side * cols, cols, 1)
        theirs = lax.dynamic_slice_in_dim(grad, (1 - side) * cols, cols, 1)
        return (mine.astype(F32) + pair(theirs).astype(F32)).astype(BF)

    grad_attn = jnp.concatenate(
        [
            pair_sum(dot_first(normed, grad_query).astype(BF)),
            pair_sum(dot_first(ssm_out, grad_key).astype(BF)),
            pair_sum(dot_first(ssm_out, grad_value).astype(BF)),
            pair_sum(dot_first(grad_branch, attended).astype(BF)),
        ],
        axis=1,
    )
    shard_attn = scatter_rows(grad_attn, count, index, False)
    grad_mixed, state_sum, state_dsum = ssm_backward(
        starts, grad_key, grad_value, key_full, value_full, drive, decay, coef
    )
    grad_mix = pair_sum(dot_first(normed, grad_mixed).astype(BF))
    shard_mix = scatter_rows(grad_mix, count, index, True)
    grad_normed = dot_last(grad_query, query_full) + dot_last(grad_mixed, mix_full)
    back_one, grad_gain_one, grad_bias_one = norm_backward(
        grad_normed, rows.astype(F32), gain_one
    )
    in_grad = both_halves(grad_middle + back_one)

    norm_sums = jnp.stack([grad_gain_one, grad_bias_one, grad_gain_two, grad_bias_two])
    norm_sums = norm_sums + pair(norm_sums)
    state_sums = jnp.stack([state_sum, state_dsum]).reshape(2 * states, width)
    mine = lax.dynamic_slice_in_dim(state_sums, side * cols, cols, 1)
    theirs = lax.dynamic_slice_in_dim(state_sums, (1 - side) * cols, cols, 1)
    state_sums = mine + pair(theirs)
    small = jnp.concatenate([state_sums, norm_sums.reshape(-1, cols)], axis=0)
    small = sum_all(small, count)
    total, dtotal = small[:states], small[states : 2 * states]
    norm_sums = small[2 * states :].reshape(4, width)
    norm_sums = lax.dynamic_slice_in_dim(
        norm_sums, index * norm1_gain.shape[0], norm1_gain.shape[0], 1
    )
    return (
        layer_out[:, None],
        in_grad[:, None],
        shard_mix,
        shard_attn[:, :cols],
        shard_attn[:, cols : 2 * cols],
        shard_attn[:, 2 * cols : 3 * cols],
        shard_attn[:, 3 * cols :].T,
        shard_up,
        shard_down.T,
        norm_sums[0],
        norm_sums[1],
        norm_sums[2],
        norm_sums[3],
        ssm_inject * ssm_readout * dtotal,
        ssm_readout * total,
        ssm_inject * total,
    )


def solution(mesh):
    return jax.shard_map(
        functools.partial(per_device, mesh.shape["dp"]),
        mesh=mesh,
        in_specs=(
            P(None, "dp", "tensor", None),
            P(None, "dp", None),
            P("dp", "tensor"),
            P("dp", "tensor"),
            P("dp", "tensor"),
            P("dp", "tensor"),
            P("tensor", "dp"),
            P("dp", "tensor"),
            P("tensor", "dp"),
            P("dp"),
            P("dp"),
            P("dp"),
            P("dp"),
            P(None, "tensor"),
            P(None, "tensor"),
            P(None, "tensor"),
            P(None, "dp", "tensor", None),
        ),
        out_specs=(
            P(None, "dp", "tensor", None),
            P(None, "dp", "tensor", None),
            P("dp", "tensor"),
            P("dp", "tensor"),
            P("dp", "tensor"),
            P("dp", "tensor"),
            P("tensor", "dp"),
            P("dp", "tensor"),
            P("tensor", "dp"),
            P("dp"),
            P("dp"),
            P("dp"),
            P("dp"),
            P(None, "tensor"),
            P(None, "tensor"),
            P(None, "tensor"),
        ),
        check_vma=False,
    )
```

```python
import functools
import math

import jax
import jax.numpy as jnp
from jax import lax
from jax.experimental import pallas as pl
from jax.experimental.pallas import tpu as pltpu
from jax.sharding import PartitionSpec as P

HEAD_DIM = 128
BLOCK = 512
CTX = 128
NDOCS = 8
LANES = 128
QTILE = 256

norm_eps = 1e-05
masked_score = -1e30
VMEM = 56 * 1024 * 1024
BF = jnp.bfloat16
F32 = jnp.float32


def dot_plain(left_op, right_op):
    return jnp.dot(left_op, right_op, preferred_element_type=F32)


def dot_last(left_op, right_op):
    return lax.dot_general(left_op, right_op, (((1,), (1,)), ((), ())), preferred_element_type=F32)


def dot_first(left_op, right_op):
    return lax.dot_general(left_op, right_op, (((0,), (0,)), ((), ())), preferred_element_type=F32)


def params(count=1):
    return pltpu.CompilerParams(
        dimension_semantics=("arbitrary",) * count, vmem_limit_bytes=VMEM
    )


def bits_of(count):
    out = []
    bit = 1
    while bit < count:
        out.append(bit)
        bit *= 2
    return out


def gather_order(count, flip):
    bits = bits_of(count)
    low = bits[:2]
    return bits[2:] + (low[::-1] if flip else low)


def swap(values, axis_name, count, bit):
    return lax.ppermute(values, axis_name, [(i, i ^ bit) for i in range(count)])


def tie(*trees):
    return lax.optimization_barrier(trees)


class Gather:
    def __init__(self, shard, count, index, flip):
        self.values, self.count, self.index = shard, count, index
        self.shape = (count * shard.shape[0],) + shard.shape[1:]
        self.left = gather_order(count, flip)
        self.present = []

    def send(self):
        self.got = swap(self.values, "dp", self.count, self.left[0])

    def merge(self):
        bit = self.left.pop(0)
        place = sum(1 for p in self.present if p > bit)
        self.present.append(bit)
        upper = (self.index // bit) % 2 == 1
        self.values = jnp.where(
            upper,
            jnp.stack([self.got, self.values], axis=place),
            jnp.stack([self.values, self.got], axis=place),
        )

    def result(self):
        return self.values.reshape(self.shape)


class Scatter:
    def __init__(self, full, count, index, flip):
        bits = bits_of(count)
        self.values = full.reshape((2,) * len(bits) + (full.shape[0] // count,) + full.shape[1:])
        self.count, self.index = count, index
        self.present = sorted(bits, reverse=True)
        self.left = gather_order(count, flip)[::-1]

    def send(self):
        bit = self.left[0]
        place = self.present.index(bit)
        upper = (self.index // bit) % 2
        send = lax.dynamic_index_in_dim(self.values, 1 - upper, place, keepdims=False)
        self.got = swap(send, "dp", self.count, bit)

    def merge(self):
        bit = self.left.pop(0)
        place = self.present.index(bit)
        upper = (self.index // bit) % 2
        keep = lax.dynamic_index_in_dim(self.values, upper, place, keepdims=False)
        self.present.remove(bit)
        self.values = keep.astype(F32) + self.got.astype(F32)
        if self.present:
            self.values = self.values.astype(BF)

    def result(self):
        return self.values


class Total:
    def __init__(self, values, count):
        self.values, self.count, self.left = values, count, bits_of(count)

    def send(self):
        self.got = swap(self.values, "dp", self.count, self.left[0])

    def merge(self):
        self.left.pop(0)
        self.values = self.values + self.got


def send(chains, *gates):
    chains = [c for c in chains if c.left]
    held = tie([c.values for c in chains], gates)[0]
    for c, v in zip(chains, held):
        c.values = v
    for c in chains:
        c.send()


def fence(chains, *values):
    chains = [c for c in chains if c.left]
    held, values = tie([(c.values, c.got) for c in chains], values)
    for c, (v, g) in zip(chains, held):
        c.values, c.got = v, g
        c.merge()
    held, values = tie(marks(chains), values)
    for c, v in zip(chains, held):
        c.values = v
    return values if len(values) != 1 else values[0]


def step(chains, *gates):
    send(chains, *gates)
    fence(chains)


def complete(chains):
    while any(c.left for c in chains):
        step(chains)


def join_chains(chains):
    chains[0].values = jnp.concatenate([c.values for c in chains], axis=-1)
    del chains[1:]


def marks(chains):
    return [c.values for c in chains]


def join_pair(own, other, side, axis):
    return jnp.where(
        side == 0,
        jnp.concatenate([own, other], axis=axis),
        jnp.concatenate([other, own], axis=axis),
    )


def pair(values):
    return lax.ppermute(values, "tensor", [(0, 1), (1, 0)])


def norm_of(values, gain_vec, bias_vec):
    centred = values - jnp.mean(values, axis=-1, keepdims=True)
    inverse = lax.rsqrt(jnp.mean(centred * centred, axis=-1, keepdims=True) + norm_eps)
    return centred * inverse * gain_vec + bias_vec


def to_steps(steps_ref, row_first, values, col_first):
    rows, cols = values.shape
    tiles = steps_ref.shape[1]
    for j in range(cols // LANES):
        steps_ref[pl.ds(row_first, rows), col_first // LANES + j, :] = values[
            :, j * LANES : (j + 1) * LANES
        ]


def run_docs(starts_ref, low, high, one_step, make_start, finish, backward, unroll=8):
    for doc in range(NDOCS):
        d = NDOCS - 1 - doc if backward else doc
        first = jnp.minimum(jnp.maximum(starts_ref[d], low), high)
        last = jnp.minimum(jnp.maximum(starts_ref[d + 1], low), high)
        length = last - first
        groups = length // unroll
        carry = make_start(d)

        def group_body(g, carry):
            base = last - 1 - g * unroll if backward else first + g * unroll
            for i in range(unroll):
                carry = one_step(base - i if backward else base + i, carry)
            return carry

        carry = lax.fori_loop(0, groups, group_body, carry)
        done = groups * unroll

        def one_body(i, carry):
            return one_step(last - 1 - done - i if backward else first + done + i, carry)

        carry = lax.fori_loop(0, length - done, one_body, carry)
        finish(d, length, carry)


def add_up(parts):
    while len(parts) > 1:
        parts = [parts[k] + parts[k + 1] for k in range(0, len(parts), 2)]
    return parts[0]


def scan_states(starts_ref, low, high, drive_ref, decay_ref, coef_ref, y_ref, start_ref, end_ref):
    states = decay_ref.shape[0]
    zero = jnp.zeros(decay_ref.shape[1:], F32)

    def one_step(t, state):
        u = drive_ref[t]
        new = [decay_ref[n] * state[n] + u for n in range(states)]
        y_ref[t - low] = add_up([coef_ref[n] * new[n] for n in range(states)])
        return tuple(new)

    def make_start(d):
        if start_ref is None:
            return (zero,) * states
        going = starts_ref[d] < low
        return tuple(jnp.where(going, start_ref[n], zero) for n in range(states))

    def finish(d, length, carry):
        if end_ref is not None:

            @pl.when(length > 0)
            def _():
                for n in range(states):
                    end_ref[n] = carry[n]

    run_docs(starts_ref, low, high, one_step, make_start, finish, False)


def from_steps(steps_ref, out_ref):
    length, tiles, _ = steps_ref.shape
    chunk = 256

    def write(i, _):
        r = pl.multiple_of(i * chunk, chunk)
        for j in range(tiles):
            out_ref[pl.ds(r, chunk), j * LANES : (j + 1) * LANES] = steps_ref[
                pl.ds(r, chunk), j, :
            ].astype(BF)
        return 0

    lax.fori_loop(0, length // chunk, write, 0)


def ssm_forward_kernel(
    starts_ref, rows_ref, gain_ref, bias_ref, mix_ref, decay_ref, coef_ref,
    normed_ref, drive_ref, out_ref, end_ref, y_ref,
):
    length, width = rows_ref.shape
    chunk = 256

    def project(i, _):
        r = pl.multiple_of(i * chunk, chunk)
        normed = norm_of(
            rows_ref[pl.ds(r, chunk), :].astype(F32), gain_ref[...], bias_ref[...]
        ).astype(BF)
        normed_ref[pl.ds(r, chunk), :] = normed
        for c in range(0, width, 256):
            to_steps(drive_ref, r, dot_plain(normed, mix_ref[:, c : c + 256]), c)
        return 0

    lax.fori_loop(0, length // chunk, project, 0)
    scan_states(
        starts_ref, 0, length // 2, drive_ref, decay_ref, coef_ref, y_ref, None, end_ref
    )
    from_steps(y_ref, out_ref)


def ssm_rest_kernel(
    starts_ref, drive_ref, decay_ref, coef_ref, start_ref, first_ref, out_ref, y_ref
):
    length = drive_ref.shape[0]
    half = length // 2
    scan_states(
        starts_ref, half, length, drive_ref, decay_ref, coef_ref, y_ref, start_ref, None
    )
    out_ref[:half, :] = first_ref[...]
    from_steps(y_ref, out_ref.at[half:])


def ssm_forward(starts, rows, gain_vec, bias_vec, mix, decay, coef):
    length, width = rows.shape
    tiles = width // LANES
    vm = pl.BlockSpec(memory_space=pltpu.VMEM)
    return pl.pallas_call(
        ssm_forward_kernel,
        out_shape=(
            jax.ShapeDtypeStruct((length, width), BF),
            jax.ShapeDtypeStruct((length, tiles, LANES), F32),
            jax.ShapeDtypeStruct((length // 2, width), BF),
            jax.ShapeDtypeStruct(decay.shape, F32),
        ),
        in_specs=[pl.BlockSpec(memory_space=pltpu.SMEM)] + [vm] * 6,
        out_specs=(vm,) * 4,
        scratch_shapes=[pltpu.VMEM((length // 2, tiles, LANES), F32)],
        compiler_params=pltpu.CompilerParams(vmem_limit_bytes=VMEM),
        cost_estimate=pl.CostEstimate(
            flops=12 * length * width * width,
            bytes_accessed=16 * length * width,
            transcendentals=0,
        ),
        name="ssm_forward",
    )(starts, rows, gain_vec, bias_vec, mix, decay, coef)


def ssm_rest(starts, drive, decay, coef, start, first):
    length, tiles, _ = drive.shape
    width = tiles * LANES
    vm = pl.BlockSpec(memory_space=pltpu.VMEM)
    return pl.pallas_call(
        ssm_rest_kernel,
        out_shape=jax.ShapeDtypeStruct((length, width), BF),
        in_specs=[pl.BlockSpec(memory_space=pltpu.SMEM)] + [vm] * 5,
        out_specs=vm,
        scratch_shapes=[pltpu.VMEM((length // 2, tiles, LANES), F32)],
        compiler_params=pltpu.CompilerParams(vmem_limit_bytes=VMEM),
        cost_estimate=pl.CostEstimate(
            flops=10 * length * width * width,
            bytes_accessed=16 * length * width,
            transcendentals=0,
        ),
        name="ssm_rest",
    )(starts, drive, decay, coef, start, first)


def adjoint_states(starts_ref, low, drive_ref, g_ref, decay_ref, coef_ref, gm_ref, sum_ref, dsum_ref, given_ref):
    length = g_ref.shape[0]
    part = sum_ref.shape[0]
    zero = jnp.zeros(decay_ref.shape[1:], F32)

    def one_step(t, carry):
        mu, rho, total, dtotal = carry
        u = drive_ref[t]
        g = g_ref[t]
        new_mu, new_rho, new_total, new_dtotal, parts = [], [], [], [], []
        for n in range(part):
            a = decay_ref[low + n]
            r = a * rho[n] + mu[n]
            m = a * mu[n] + g
            new_mu.append(m)
            new_rho.append(r)
            new_total.append(total[n] + u * m)
            new_dtotal.append(dtotal[n] + u * r)
            parts.append(coef_ref[low + n] * m)
        gm = add_up(parts)
        gm_ref[t] = gm if given_ref is None else gm + given_ref[t]
        return tuple(new_mu), tuple(new_rho), tuple(new_total), tuple(new_dtotal)

    for n in range(part):
        sum_ref[n] = zero
        dsum_ref[n] = zero

    def make_start(d):
        zeros = (zero,) * part
        return zeros, zeros, zeros, zeros

    def finish(d, count, carry):
        for n in range(part):
            sum_ref[n] = sum_ref[n] + carry[2][n]
            dsum_ref[n] = dsum_ref[n] + carry[3][n]

    run_docs(starts_ref, 0, length, one_step, make_start, finish, True)


def ssm_backward_kernel(
    starts_ref, gkey_ref, gvalue_ref, wkey_ref, wvalue_ref, drive_ref, decay_ref, coef_ref,
    g_ref, gm_ref, sum_ref, dsum_ref,
):
    length, width = gkey_ref.shape
    chunk = 256

    def project(i, _):
        r = pl.multiple_of(i * chunk, chunk)
        gkey = gkey_ref[pl.ds(r, chunk), :]
        gvalue = gvalue_ref[pl.ds(r, chunk), :]
        for c in range(0, width, 256):
            to_steps(
                g_ref,
                r,
                dot_last(gkey, wkey_ref[c : c + 256, :])
                + dot_last(gvalue, wvalue_ref[c : c + 256, :]),
                c,
            )
        return 0

    lax.fori_loop(0, length // chunk, project, 0)
    adjoint_states(
        starts_ref, 0, drive_ref, g_ref, decay_ref, coef_ref, gm_ref, sum_ref, dsum_ref, None
    )


def ssm_backward_rest_kernel(
    starts_ref, g_ref, given_ref, drive_ref, decay_ref, coef_ref,
    gmixed_ref, sum_ref, dsum_ref, gm_ref,
):
    adjoint_states(
        starts_ref, decay_ref.shape[0] // 2, drive_ref, g_ref, decay_ref, coef_ref, gm_ref,
        sum_ref, dsum_ref, given_ref,
    )
    from_steps(gm_ref, gmixed_ref)


def ssm_backward(starts, gkey, gvalue, wkey, wvalue, drive, decay, coef):
    length, width = gkey.shape
    tiles = width // LANES
    vm = pl.BlockSpec(memory_space=pltpu.VMEM)
    half = (decay.shape[0] // 2,) + decay.shape[1:]
    return pl.pallas_call(
        ssm_backward_kernel,
        out_shape=(
            jax.ShapeDtypeStruct((length, tiles, LANES), F32),
            jax.ShapeDtypeStruct((length, tiles, LANES), F32),
            jax.ShapeDtypeStruct(half, F32),
            jax.ShapeDtypeStruct(half, F32),
        ),
        in_specs=[pl.BlockSpec(memory_space=pltpu.SMEM)] + [vm] * 7,
        out_specs=(vm,) * 4,
        compiler_params=pltpu.CompilerParams(vmem_limit_bytes=VMEM),
        cost_estimate=pl.CostEstimate(
            flops=20 * length * width * width,
            bytes_accessed=20 * length * width,
            transcendentals=0,
        ),
        name="ssm_backward",
    )(starts, gkey, gvalue, wkey, wvalue, drive, decay, coef)


def ssm_backward_rest(starts, g, given, drive, decay, coef):
    length, tiles, _ = drive.shape
    width = tiles * LANES
    vm = pl.BlockSpec(memory_space=pltpu.VMEM)
    half = (decay.shape[0] // 2,) + decay.shape[1:]
    return pl.pallas_call(
        ssm_backward_rest_kernel,
        out_shape=(
            jax.ShapeDtypeStruct((length, width), BF),
            jax.ShapeDtypeStruct(half, F32),
            jax.ShapeDtypeStruct(half, F32),
        ),
        in_specs=[pl.BlockSpec(memory_space=pltpu.SMEM)] + [vm] * 5,
        out_specs=(vm,) * 3,
        scratch_shapes=[pltpu.VMEM((length, tiles, LANES), F32)],
        compiler_params=pltpu.CompilerParams(vmem_limit_bytes=VMEM),
        cost_estimate=pl.CostEstimate(
            flops=20 * length * width * width,
            bytes_accessed=20 * length * width,
            transcendentals=0,
        ),
        name="ssm_backward_rest",
    )(starts, g, given, drive, decay, coef)


def attention_tiles(length):
    tiles = []
    for first in range(0, length, QTILE):
        block_first = first // BLOCK * BLOCK
        key_first = max(0, block_first - CTX)
        tiles.append((first, key_first, first + QTILE - key_first))
    return tiles


def fill_bias(seg_col_ref, seg_row_ref, bias_ref, tiles):
    at = 0
    for first, key_first, count in tiles:
        same = seg_col_ref[first : first + QTILE, :] == seg_row_ref[:, key_first : key_first + count]
        query_pos = lax.broadcasted_iota(jnp.int32, (QTILE, count), 0) + first
        key_pos = lax.broadcasted_iota(jnp.int32, (QTILE, count), 1) + key_first
        bias_ref[:, at : at + count] = jnp.where(
            same & (key_pos <= query_pos), 0.0, masked_score
        ).astype(F32)
        at += count


EXP_SCALE = HEAD_DIM ** (-0.5) * math.log2(math.e)


def attention_forward_kernel(
    seg_col_ref, seg_row_ref, query_ref, key_ref, value_ref, out_ref, lse_ref, bias_ref
):
    tiles = attention_tiles(query_ref.shape[0])

    @pl.when(pl.program_id(0) == 0)
    def _():
        fill_bias(seg_col_ref, seg_row_ref, bias_ref, tiles)

    at = 0
    for first, key_first, count in tiles:
        keys = slice(key_first, key_first + count)
        scores = dot_last(query_ref[first : first + QTILE, :], key_ref[keys, :])
        scores = scores * EXP_SCALE + bias_ref[:, at : at + count]
        top = jnp.max(scores, axis=-1, keepdims=True)
        raised = jnp.exp2(scores - top)
        total = jnp.sum(raised, axis=-1, keepdims=True)
        probs = (raised * (1.0 / total)).astype(BF)
        out_ref[first : first + QTILE, :] = dot_plain(probs, value_ref[keys, :]).astype(BF)
        lse_ref[0, first : first + QTILE, :] = top + jnp.log2(total)
        at += count


def attention_forward(seg_col, seg_row, query, key, value):
    length, width = query.shape
    heads = width // HEAD_DIM
    tiles = attention_tiles(length)
    cols = sum(t[2] for t in tiles)
    head = pl.BlockSpec((length, HEAD_DIM), lambda h: (0, h))
    whole = lambda shape: pl.BlockSpec(shape, lambda h: (0, 0))
    return pl.pallas_call(
        attention_forward_kernel,
        grid=(heads,),
        out_shape=(
            jax.ShapeDtypeStruct((length, width), BF),
            jax.ShapeDtypeStruct((heads, length, 1), F32),
        ),
        in_specs=[whole((length, 1)), whole((1, length)), head, head, head],
        out_specs=(head, pl.BlockSpec((1, length, 1), lambda h: (h, 0, 0))),
        scratch_shapes=[pltpu.VMEM((QTILE, cols), F32)],
        compiler_params=params(),
        cost_estimate=pl.CostEstimate(
            flops=4 * QTILE * cols * width,
            bytes_accessed=8 * length * width,
            transcendentals=QTILE * cols * heads,
        ),
        name="attention_forward",
    )(seg_col, seg_row, query, key, value)


def attention_backward_kernel(
    seg_col_ref, seg_row_ref, query_ref, key_ref, value_ref, lse_ref, gout_ref,
    gquery_ref, gkey_ref, gvalue_ref, bias_ref, gk_ref, gv_ref,
):
    tiles = attention_tiles(query_ref.shape[0])
    scale = HEAD_DIM ** (-0.5)

    @pl.when(pl.program_id(0) == 0)
    def _():
        fill_bias(seg_col_ref, seg_row_ref, bias_ref, tiles)

    gk_ref[...] = jnp.zeros_like(gk_ref)
    gv_ref[...] = jnp.zeros_like(gv_ref)
    at = 0
    for first, key_first, count in tiles:
        keys = slice(key_first, key_first + count)
        query = query_ref[first : first + QTILE, :]
        gout = gout_ref[first : first + QTILE, :]
        scores = dot_last(query, key_ref[keys, :]) * EXP_SCALE + bias_ref[:, at : at + count]
        probs = jnp.exp2(scores - lse_ref[0, first : first + QTILE, :])
        gv_ref[keys, :] = gv_ref[keys, :] + dot_first(probs.astype(BF), gout)
        gprobs = dot_last(gout, value_ref[keys, :])
        inner = jnp.sum(probs * gprobs, axis=-1, keepdims=True)
        gscores = (probs * (gprobs - inner)).astype(BF)
        gquery_ref[first : first + QTILE, :] = (
            dot_plain(gscores, key_ref[keys, :]) * scale
        ).astype(BF)
        gk_ref[keys, :] = gk_ref[keys, :] + dot_first(gscores, query)
        at += count
    gkey_ref[...] = (gk_ref[...] * scale).astype(BF)
    gvalue_ref[...] = gv_ref[...].astype(BF)


def attention_backward(seg_col, seg_row, query, key, value, lse, gout):
    length, width = query.shape
    heads = width // HEAD_DIM
    tiles = attention_tiles(length)
    cols = sum(t[2] for t in tiles)
    head = pl.BlockSpec((length, HEAD_DIM), lambda h: (0, h))
    whole = lambda shape: pl.BlockSpec(shape, lambda h: (0, 0))
    return pl.pallas_call(
        attention_backward_kernel,
        grid=(heads,),
        out_shape=(jax.ShapeDtypeStruct((length, width), BF),) * 3,
        in_specs=[whole((length, 1)), whole((1, length)), head, head, head]
        + [pl.BlockSpec((1, length, 1), lambda h: (h, 0, 0)), head],
        out_specs=(head,) * 3,
        scratch_shapes=[
            pltpu.VMEM((QTILE, cols), F32),
            pltpu.VMEM((length, HEAD_DIM), F32),
            pltpu.VMEM((length, HEAD_DIM), F32),
        ],
        compiler_params=params(),
        cost_estimate=pl.CostEstimate(
            flops=10 * QTILE * cols * width,
            bytes_accessed=14 * length * width,
            transcendentals=QTILE * cols * heads,
        ),
        name="attention_backward",
    )(seg_col, seg_row, query, key, value, lse, gout)


def norm_backward(grad, values, gain_vec):
    centred = values - jnp.mean(values, axis=-1, keepdims=True)
    inverse = lax.rsqrt(jnp.mean(centred * centred, axis=-1, keepdims=True) + norm_eps)
    xhat = centred * inverse
    dxhat = grad * gain_vec
    back = (
        dxhat
        - jnp.mean(dxhat, axis=-1, keepdims=True)
        - xhat * jnp.mean(dxhat * xhat, axis=-1, keepdims=True)
    ) * inverse
    return back, jnp.sum(grad * xhat, axis=0, keepdims=True), jnp.sum(grad, axis=0, keepdims=True)


ERF_RATE = 0.3275911 * 2.0**-0.5
ERF_TERMS = (0.254829592, -0.284496736, 1.421413741, -1.453152027, 1.061405429)


def gelu_parts(values):
    near = 1.0 / (1.0 + ERF_RATE * jnp.abs(values))
    bell = jnp.exp2((-0.5 * math.log2(math.e)) * (values * values))
    poly = 0.5 * ERF_TERMS[4]
    for term in ERF_TERMS[3::-1]:
        poly = 0.5 * term + near * poly
    tail = near * poly * bell
    below = jnp.where(values < 0, tail, 1.0 - tail)
    return values * below, below + values * bell * ((2.0 * math.pi) ** -0.5)


def feed_forward_kernel(part, *refs):
    ins, refs = refs[: 6 + 6 * (part > 0)], refs[6 + 6 * (part > 0) :]
    own_ref, other_ref, cot_own_ref, cot_other_ref, up_ref, down_ref = ins[:6]
    earlier = ins[6:10]
    outs, (gup_ref, gdown_ref) = refs[:4], refs[4:6]
    hidden_ref, gpre_ref, up_sum_ref, down_sum_ref, sems = refs[6:]
    length, width = own_ref.shape
    units = up_ref.shape[1]
    tile = 512

    for s, (normed_ref, cot_ref) in enumerate(
        ((own_ref, cot_own_ref), (other_ref, cot_other_ref))
    ):

        def one(i, _, s=s, normed_ref=normed_ref, cot_ref=cot_ref):
            rows = pl.ds(pl.multiple_of(i * tile, tile), tile)
            held = pl.ds(pl.multiple_of(s * length + i * tile, tile), tile)
            for n in range(0, units, tile):
                pre = dot_plain(normed_ref[rows, :], up_ref[:, n : n + tile])
                ghidden = dot_plain(cot_ref[rows, :], down_ref[:, n : n + tile])
                hidden, slope = gelu_parts(pre)
                hidden_ref[held, n : n + tile] = hidden.astype(BF)
                gpre_ref[held, n : n + tile] = (ghidden * slope).astype(BF)
            return 0

        lax.fori_loop(0, length // tile, one, 0)

    copies = []
    for k, (first_ref, second_ref, held_ref, sum_ref, out_ref) in enumerate(
        (
            (own_ref, other_ref, gpre_ref, up_sum_ref, gup_ref),
            (cot_own_ref, cot_other_ref, hidden_ref, down_sum_ref, gdown_ref),
        )
    ):

        def three(i, _, first_ref=first_ref, second_ref=second_ref, held_ref=held_ref, sum_ref=sum_ref):
            cols = pl.ds(pl.multiple_of(i * tile, tile), tile)
            total = dot_first(first_ref[:, cols], held_ref[:length, :])
            total = total + dot_first(second_ref[:, cols], held_ref[length:, :])
            sum_ref[cols, :] = total.astype(BF)
            return 0

        lax.fori_loop(0, width // tile, three, 0)
        copy = pltpu.make_async_copy(
            sum_ref, out_ref.at[:, pl.ds(part * units, units)], sems.at[k]
        )
        copy.start()
        copies.append(copy)

    for s in range(2):

        def two(i, _, s=s):
            rows = pl.ds(pl.multiple_of(i * tile, tile), tile)
            held = pl.ds(pl.multiple_of(s * length + i * tile, tile), tile)
            for k, (held_ref, weight_ref) in enumerate(
                ((hidden_ref, down_ref), (gpre_ref, up_ref))
            ):
                total = dot_last(held_ref[held, :], weight_ref[...])
                if earlier:
                    total = total + earlier[2 * k + s][rows, :].astype(F32)
                outs[2 * k + s][rows, :] = total.astype(BF)
            return 0

        lax.fori_loop(0, length // tile, two, 0)

    for copy in copies:
        copy.wait()


def feed_forward(part, parts, own, other, cot_own, cot_other, up, down, earlier):
    length, width = own.shape
    units = up.shape[1]
    vm = pl.BlockSpec(memory_space=pltpu.VMEM)
    anywhere = pl.BlockSpec(memory_space=pl.ANY)
    return pl.pallas_call(
        functools.partial(feed_forward_kernel, part),
        out_shape=(jax.ShapeDtypeStruct((length, width), BF),) * 4
        + (jax.ShapeDtypeStruct((width, parts * units), BF),) * 2,
        in_specs=[vm] * 6 + ([vm] * 4 + [anywhere] * 2 if part else []),
        out_specs=(vm,) * 4 + (anywhere,) * 2,
        scratch_shapes=[pltpu.VMEM((2 * length, units), BF)] * 2
        + [pltpu.VMEM((width, units), BF)] * 2
        + [pltpu.SemaphoreType.DMA((2,))],
        input_output_aliases={10: 4, 11: 5} if part else {},
        compiler_params=pltpu.CompilerParams(vmem_limit_bytes=VMEM),
        cost_estimate=pl.CostEstimate(
            flops=28 * length * width * units,
            bytes_accessed=48 * length * width,
            transcendentals=4 * length * units,
        ),
        name="feed_forward",
    )(own, other, cot_own, cot_other, up, down, *earlier)


def middle_kernel(attended_ref, out_ref, rows_ref, gain_ref, bias_ref, middle_ref, normed_ref):
    middle = rows_ref[...].astype(F32) + dot_last(attended_ref[...], out_ref[...])
    middle_ref[...] = middle
    normed_ref[...] = norm_of(middle, gain_ref[...], bias_ref[...]).astype(BF)


def row_spec(width, tile=256):
    return pl.BlockSpec((tile, width), lambda i: (i, 0))


def fixed(*shape):
    return pl.BlockSpec(shape, lambda i: (0,) * len(shape))


def middle_of(attended, out_full, rows, gain_vec, bias_vec):
    length, width = rows.shape
    row = row_spec(width)
    return pl.pallas_call(
        middle_kernel,
        grid=(length // 256,),
        out_shape=(
            jax.ShapeDtypeStruct((length, width), F32),
            jax.ShapeDtypeStruct((length, width), BF),
        ),
        in_specs=[row, fixed(width, width), row, fixed(1, width), fixed(1, width)],
        out_specs=(row, row),
        compiler_params=params(),
        cost_estimate=pl.CostEstimate(
            flops=2 * length * width * width, bytes_accessed=12 * length * width, transcendentals=0
        ),
        name="middle",
    )(attended, out_full, rows, gain_vec, bias_vec)


def norm_two_kernel(
    mine_ref, theirs_ref, middle_ref, cot_ref, gain_ref, out_ref,
    gmiddle_ref, gbranch_ref, gattended_ref, sums_ref,
):
    grad = mine_ref[...].astype(F32) + theirs_ref[...].astype(F32)
    back, gain_sum, bias_sum = norm_backward(grad, middle_ref[...], gain_ref[...])
    gmiddle = cot_ref[...].astype(F32) + back
    gmiddle_ref[...] = gmiddle
    gbranch = gmiddle.astype(BF)
    gbranch_ref[...] = gbranch
    gattended_ref[...] = dot_plain(gbranch, out_ref[...]).astype(BF)
    add_sums(sums_ref, gain_sum, bias_sum)


def add_sums(sums_ref, gain_sum, bias_sum):
    @pl.when(pl.program_id(0) == 0)
    def _():
        sums_ref[...] = jnp.zeros_like(sums_ref)

    sums_ref[0:1, :] = sums_ref[0:1, :] + gain_sum
    sums_ref[1:2, :] = sums_ref[1:2, :] + bias_sum


def norm_two_back(mine, theirs, middle, cot, gain_vec, out_full):
    length, width = middle.shape
    row = row_spec(width)
    return pl.pallas_call(
        norm_two_kernel,
        grid=(length // 256,),
        out_shape=(
            jax.ShapeDtypeStruct((length, width), F32),
            jax.ShapeDtypeStruct((length, width), BF),
            jax.ShapeDtypeStruct((length, width), BF),
            jax.ShapeDtypeStruct((2, width), F32),
        ),
        in_specs=[row] * 4 + [fixed(1, width), fixed(width, width)],
        out_specs=(row, row, row, fixed(2, width)),
        compiler_params=params(),
        cost_estimate=pl.CostEstimate(
            flops=2 * length * width * width, bytes_accessed=24 * length * width, transcendentals=0
        ),
        name="norm_two_back",
    )(mine, theirs, middle, cot, gain_vec, out_full)


def norm_one_kernel(
    gquery_ref, gmixed_ref, query_ref, mix_ref, rows_ref, gmiddle_ref, gain_ref, grad_ref, sums_ref
):
    grad = dot_last(gquery_ref[...], query_ref[...]) + dot_last(gmixed_ref[...], mix_ref[...])
    back, gain_sum, bias_sum = norm_backward(grad, rows_ref[...].astype(F32), gain_ref[...])
    grad_ref[...] = gmiddle_ref[...] + back
    add_sums(sums_ref, gain_sum, bias_sum)


def norm_one_back(gquery, gmixed, query_full, mix_full, rows, gmiddle, gain_vec):
    length, width = rows.shape
    row = row_spec(width)
    return pl.pallas_call(
        norm_one_kernel,
        grid=(length // 256,),
        out_shape=(
            jax.ShapeDtypeStruct((length, width), F32),
            jax.ShapeDtypeStruct((2, width), F32),
        ),
        in_specs=[row, row, fixed(width, width), fixed(width, width), row, row, fixed(1, width)],
        out_specs=(row, fixed(2, width)),
        compiler_params=params(),
        cost_estimate=pl.CostEstimate(
            flops=4 * length * width * width, bytes_accessed=20 * length * width, transcendentals=0
        ),
        name="norm_one_back",
    )(gquery, gmixed, query_full, mix_full, rows, gmiddle, gain_vec)


def weight_grads_kernel(count, side_ref, *refs):
    lefts, rights = refs[:count], refs[count : 2 * count]
    mine_ref, theirs_ref = refs[2 * count :]
    cols = mine_ref.shape[1] // count
    side = side_ref[0]
    for ref, at in ((theirs_ref, 1 - side), (mine_ref, side)):
        for k in range(count):
            part = rights[k][:, pl.ds(pl.multiple_of(at * cols, cols), cols)]
            ref[:, k * cols : (k + 1) * cols] = dot_first(lefts[k][...], part).astype(BF)


def weight_grads(side, lefts, rights):
    count = len(lefts)
    length, width = lefts[0].shape
    vm = pl.BlockSpec(memory_space=pltpu.VMEM)
    return pl.pallas_call(
        functools.partial(weight_grads_kernel, count),
        out_shape=(jax.ShapeDtypeStruct((width, count * width // 2), BF),) * 2,
        in_specs=[pl.BlockSpec(memory_space=pltpu.SMEM)] + [vm] * (2 * count),
        out_specs=(vm, vm),
        compiler_params=pltpu.CompilerParams(vmem_limit_bytes=VMEM),
        cost_estimate=pl.CostEstimate(
            flops=2 * count * length * width * width,
            bytes_accessed=6 * count * length * width,
            transcendentals=0,
        ),
        name="weight_grads",
    )(jnp.reshape(side, (1,)), *lefts, *rights)


def per_device(
    count,
    layer_in,
    segment_ids,
    w_mix_in,
    w_query,
    w_key,
    w_value,
    w_attn_out,
    w_up,
    w_down,
    norm1_gain,
    norm1_bias,
    norm2_gain,
    norm2_bias,
    ssm_decay,
    ssm_inject,
    ssm_readout,
    out_grad,
):
    index = lax.axis_index("dp")
    side = lax.axis_index("tensor")
    half = layer_in.shape[2]
    width = layer_in.shape[3]
    length = 2 * half
    tiles = width // LANES
    states = ssm_decay.shape[0]

    def whole_sequence(halves):
        own = lax.dynamic_index_in_dim(halves, side, 0, keepdims=False)
        other = pair(lax.dynamic_index_in_dim(halves, 1 - side, 0, keepdims=False))
        return join_pair(own, other, side, 0)

    def both_halves(sequence):
        own = lax.dynamic_slice_in_dim(sequence, side * half, half, 0)
        other = pair(lax.dynamic_slice_in_dim(sequence, (1 - side) * half, half, 0))
        return jnp.where(side == 0, jnp.stack([own, other]), jnp.stack([other, own]))

    cols = w_query.shape[1]

    rows = whole_sequence(layer_in[:, 0])
    coefs = jnp.stack([ssm_decay, ssm_inject, ssm_readout])
    coefs = join_pair(coefs, pair(coefs), side, 2)
    decay, inject, readout = coefs.reshape(3, states, tiles, LANES)
    coef = inject * readout
    segments = lax.dynamic_index_in_dim(segment_ids[:, 0], side, 0, keepdims=False)
    starts = jnp.sum(
        (segments[None, :] < jnp.arange(16, dtype=jnp.int32)[:, None]).astype(jnp.int32), axis=1
    )
    seg_col, seg_row = segments[:, None], segments[None, :]

    def pieces(kind, left, right):
        return [kind(left, count, index, False), kind(right, count, index, True)]

    parts = 2
    units = w_up.shape[1] // parts
    turned_out, turned_down = w_attn_out.T, w_down.T
    shard_rows = w_mix_in.shape[0]
    norms = jnp.concatenate([norm1_gain, norm1_bias, norm2_gain, norm2_bias])
    norms = jnp.pad(norms[None], ((0, 7), (0, cols - norms.shape[0])))
    mix = [Gather(jnp.concatenate([w_mix_in, norms], axis=0), count, index, False)]
    attn = pieces(
        Gather,
        jnp.concatenate([w_query, w_key], axis=1),
        jnp.concatenate([w_value, turned_out], axis=1),
    )
    ffn = [
        pieces(
            Gather,
            w_up[:, i * units : (i + 1) * units],
            turned_down[:, i * units : (i + 1) * units],
        )
        for i in range(parts)
    ]
    step(mix + attn)
    step(mix)
    step(mix + attn[:1])
    step(mix + attn[1:])
    complete(mix)
    send(attn + ffn[0], marks(mix))
    mix_all = mix[0].result().reshape(count, shard_rows + 8, cols)
    mix_half = mix_all[:, :shard_rows].reshape(width, cols)
    norms_all = mix_all[:, shard_rows, : 4 * shard_rows].reshape(count, 4, shard_rows)
    norms_all = norms_all.astype(F32).transpose(1, 0, 2).reshape(4, width)
    gain_one, bias_one, gain_two, bias_two = (norms_all[i : i + 1] for i in range(4))
    mix_full = join_pair(mix_half, pair(mix_half), side, 1)
    rows, coef, mix_full = fence(attn + ffn[0], rows, coef, mix_full)
    send(attn + ffn[0])

    normed, drive, ssm_first, state_mid = ssm_forward(
        starts, rows, gain_one, bias_one, mix_full, decay, coef
    )
    state_mid = fence(attn + ffn[0], state_mid)
    complete(attn)
    send(ffn[0] + ffn[1], marks(attn))
    ssm_out = ssm_rest(starts, drive, decay, coef, state_mid, ssm_first)
    cot = whole_sequence(tie(out_grad, state_mid)[0][:, 0])
    halves = [m.result() for m in attn]
    others = [pair(h) for h in halves]
    query_full, key_full, value_full, out_full = (
        join_pair(h[:, i * cols : (i + 1) * cols], o[:, i * cols : (i + 1) * cols], side, 1)
        for h, o in zip(halves, others)
        for i in range(2)
    )
    ssm_out, cot, query_full, key_full, value_full, out_full = fence(
        ffn[0] + ffn[1], ssm_out, cot, query_full, key_full, value_full, out_full
    )
    send(ffn[0] + ffn[1])
    cot_other = pair(cot)
    query = dot_plain(normed, query_full).astype(BF)
    key = dot_plain(ssm_out, key_full).astype(BF)
    value = dot_plain(ssm_out, value_full).astype(BF)
    attended, lse = attention_forward(seg_col, seg_row, query, key, value)
    attended, cot_other = fence(ffn[0] + ffn[1], attended, cot_other)
    complete(ffn[0])
    send(ffn[1])
    middle, normed_two = middle_of(attended, out_full, rows, gain_two, bias_two)

    normed_other = pair(normed_two)
    normed_two, normed_other = fence(ffn[1], normed_two, normed_other)
    send(ffn[1])
    both = feed_forward(
        0, parts, normed_two, normed_other, cot, cot_other, *(m.result() for m in ffn[0]), ()
    )
    both = fence(ffn[1], both)
    complete(ffn[1])
    own, other, gown, gother, grad_up, grad_down = feed_forward(
        1, parts, normed_two, normed_other, cot, cot_other, *(m.result() for m in ffn[1]), both
    )
    sums_ffn = pieces(Scatter, grad_up, grad_down)
    send(sums_ffn)

    def pair_sum(mine, theirs):
        return mine.astype(F32) + pair(theirs).astype(F32)

    grad_middle, grad_branch, grad_attended, norm_two_sums = norm_two_back(
        gown, pair(gother), middle, cot, gain_two, out_full
    )
    grads_out = weight_grads(side, (grad_branch,), (attended,))
    grads_out, grad_attended = tie(grads_out, grad_attended)
    sum_out = pair_sum(*grads_out).astype(BF)
    grad_query, grad_key, grad_value = attention_backward(
        seg_col, seg_row, query, key, value, lse, grad_attended
    )
    sum_out, grad_query, grad_key, grad_value = fence(
        sums_ffn, sum_out, grad_query, grad_key, grad_value
    )
    send(sums_ffn)
    grads_qkv = weight_grads(side, (normed, ssm_out, ssm_out), (grad_query, grad_key, grad_value))
    grads_qkv, own, other = tie(grads_qkv, own, other)
    sum_qkv = pair_sum(*grads_qkv).astype(BF)
    layer_out = both_halves(middle + pair_sum(own, other))
    sum_qkv, sum_out, layer_out, grad_key, grad_value = fence(
        sums_ffn, sum_qkv, sum_out, layer_out, grad_key, grad_value
    )
    sums_attn = pieces(
        Scatter,
        sum_qkv[:, : 2 * cols],
        jnp.concatenate([sum_qkv[:, 2 * cols :], sum_out], axis=1),
    )
    join_chains(sums_ffn)
    send(sums_attn + sums_ffn)
    g_steps, gm_steps, sum_one, dsum_one = ssm_backward(
        starts, grad_key, grad_value, key_full, value_full, drive, decay, coef
    )
    g_steps, gm_steps = fence(sums_attn, g_steps, gm_steps)
    send(sums_attn)
    grad_mixed, sum_two, dsum_two = ssm_backward_rest(
        starts, g_steps, gm_steps, drive, decay, coef
    )
    grad_mixed = fence(sums_attn + sums_ffn, grad_mixed)
    join_chains(sums_attn)
    send(sums_attn + sums_ffn)
    grad_mix = pair_sum(*weight_grads(side, (normed,), (grad_mixed,))).astype(BF)
    grad_mixed, grad_mix = tie(grad_mixed, grad_mix)
    sums_mix = [Scatter(grad_mix, count, index, False)]
    send(sums_mix)
    grad_rows, norm_one_sums = norm_one_back(
        grad_query, grad_mixed, query_full, mix_full, rows, grad_middle, gain_one
    )
    grad_rows, norm_one_sums = fence(
        sums_mix + sums_attn + sums_ffn, grad_rows, norm_one_sums
    )
    in_grad = both_halves(grad_rows)

    state_sums = jnp.concatenate([sum_one, sum_two, dsum_one, dsum_two]).reshape(
        2 * states, width
    )
    sums = jnp.concatenate(
        [
            lax.dynamic_slice_in_dim(state_sums, (1 - side) * cols, cols, 1),
            norm_one_sums.reshape(-1, cols),
            norm_two_sums.reshape(-1, cols),
        ]
    )
    mine = lax.dynamic_slice_in_dim(state_sums, side * cols, cols, 1)
    small = [Total(jnp.concatenate([mine, sums[2 * states :]]) + pair(sums), count)]
    complete(sums_mix + small + sums_attn + sums_ffn)
    small = small[0].values
    total, dtotal = small[:states], small[states : 2 * states]
    norm_sums = lax.dynamic_slice_in_dim(
        small[2 * states :].reshape(4, width), index * shard_rows, shard_rows, 1
    )
    shard_attn = sums_attn[0].result()
    shard_ffn = sums_ffn[0].result()
    return (
        layer_out[:, None],
        in_grad[:, None],
        sums_mix[0].result(),
        shard_attn[:, :cols],
        shard_attn[:, cols : 2 * cols],
        shard_attn[:, 2 * cols : 3 * cols],
        shard_attn[:, 3 * cols :].T,
        shard_ffn[:, : parts * units],
        shard_ffn[:, parts * units :].T,
        norm_sums[0],
        norm_sums[1],
        norm_sums[2],
        norm_sums[3],
        ssm_inject * ssm_readout * dtotal,
        ssm_readout * total,
        ssm_inject * total,
    )


def solution(mesh):
    return jax.shard_map(
        functools.partial(per_device, mesh.shape["dp"]),
        mesh=mesh,
        in_specs=(
            P(None, "dp", "tensor", None),
            P(None, "dp", None),
            P("dp", "tensor"),
            P("dp", "tensor"),
            P("dp", "tensor"),
            P("dp", "tensor"),
            P("tensor", "dp"),
            P("dp", "tensor"),
            P("tensor", "dp"),
            P("dp"),
            P("dp"),
            P("dp"),
            P("dp"),
            P(None, "tensor"),
            P(None, "tensor"),
            P(None, "tensor"),
            P(None, "dp", "tensor", None),
        ),
        out_specs=(
            P(None, "dp", "tensor", None),
            P(None, "dp", "tensor", None),
            P("dp", "tensor"),
            P("dp", "tensor"),
            P("dp", "tensor"),
            P("dp", "tensor"),
            P("tensor", "dp"),
            P("dp", "tensor"),
            P("tensor", "dp"),
            P("dp"),
            P("dp"),
            P("dp"),
            P("dp"),
            P(None, "tensor"),
            P(None, "tensor"),
            P(None, "tensor"),
        ),
        check_vma=False,
    )
```

```python
import functools
import math

import jax
import jax.numpy as jnp
from jax import lax
from jax.experimental import pallas as pl
from jax.experimental.pallas import tpu as pltpu
from jax.sharding import PartitionSpec as P

HEAD_DIM = 128
BLOCK = 512
CTX = 128
NDOCS = 8
LANES = 128
QTILE = 256
HEADS_EACH = 2

norm_eps = 1e-05
masked_score = -1e30
VMEM = 56 * 1024 * 1024
BF = jnp.bfloat16
F32 = jnp.float32


def dot_plain(left_op, right_op):
    return jnp.dot(left_op, right_op, preferred_element_type=F32)


def dot_last(left_op, right_op):
    return lax.dot_general(left_op, right_op, (((1,), (1,)), ((), ())), preferred_element_type=F32)


def dot_first(left_op, right_op):
    return lax.dot_general(left_op, right_op, (((0,), (0,)), ((), ())), preferred_element_type=F32)


def params(count=1):
    return pltpu.CompilerParams(
        dimension_semantics=("arbitrary",) * count, vmem_limit_bytes=VMEM
    )


def bits_of(count):
    out = []
    bit = 1
    while bit < count:
        out.append(bit)
        bit *= 2
    return out


def groups_of(count, low_groups):
    high = bits_of(count)[2:]
    return [tuple(high[k : k + 2]) for k in range(0, len(high), 2)] + [
        tuple(b for b in g if b < count) for g in low_groups
    ]


X_FIRST = ((1,), (2,))
Y_FIRST = ((2,), (1,))
DIRECT = ((1, 2),)


def swap(values, count, mask):
    return lax.ppermute(values, "dp", [(i, i ^ mask) for i in range(count)])


def tie(*trees):
    return lax.optimization_barrier(trees)


def in_order(upper, own, got, axis):
    return jnp.where(
        upper, jnp.stack([got, own], axis=axis), jnp.stack([own, got], axis=axis)
    )


class Gather:
    def __init__(self, shard, count, index, low):
        self.values, self.count, self.index = shard, count, index
        self.shape = (count * shard.shape[0],) + shard.shape[1:]
        self.left = groups_of(count, low)
        self.present = []

    def send(self):
        self.got = [swap(self.values, self.count, m) for m in masks_of(self.left[0])]

    def merge(self):
        pieces = [self.values] + list(self.got)
        for bit in self.left.pop(0):
            place = sum(1 for p in self.present if p > bit)
            self.present.append(bit)
            upper = (self.index // bit) % 2 == 1
            pieces = [
                in_order(upper, pieces[k], pieces[k + 1], place)
                for k in range(0, len(pieces), 2)
            ]
        self.values = pieces[0]

    def split(self, lows):
        cols = self.values.shape[-1] // 2
        out = []
        for k, low in enumerate(lows):
            part = Gather.__new__(Gather)
            part.count, part.index, part.present = self.count, self.index, list(self.present)
            part.values = self.values[..., k * cols : (k + 1) * cols]
            part.shape = self.shape[:-1] + (cols,)
            part.left = self.left[: -len(lows)] + list(low)
            out.append(part)
        return out

    def result(self):
        return self.values.reshape(self.shape)


def masks_of(group):
    return [group[0]] if len(group) == 1 else [group[0], group[1], group[0] | group[1]]


class Scatter:
    def __init__(self, full, count, index, low):
        bits = bits_of(count)
        self.values = full.reshape((2,) * len(bits) + (full.shape[0] // count,) + full.shape[1:])
        self.count, self.index = count, index
        self.present = sorted(bits, reverse=True)
        self.left = groups_of(count, low)[::-1]

    def block(self, group, mask):
        values, present = self.values, list(self.present)
        for bit in group:
            place = present.index(bit)
            digit = ((self.index ^ mask) // bit) % 2
            values = lax.dynamic_index_in_dim(values, digit, place, keepdims=False)
            present.remove(bit)
        return values

    def send(self):
        group = self.left[0]
        self.got = [swap(self.block(group, m), self.count, m) for m in masks_of(group)]

    def merge(self):
        group = self.left.pop(0)
        total = self.block(group, 0).astype(F32)
        for got in self.got:
            total = total + got.astype(F32)
        for bit in group:
            self.present.remove(bit)
        self.values = total.astype(BF) if self.present else total

    def result(self):
        return self.values


class Total:
    def __init__(self, values, count):
        self.values, self.count = values, count
        self.left = groups_of(count, DIRECT)[::-1]

    def send(self):
        self.got = [swap(self.values, self.count, m) for m in masks_of(self.left[0])]

    def merge(self):
        self.left.pop(0)
        total = self.values + self.got[0]
        if len(self.got) > 1:
            total = total + (self.got[1] + self.got[2])
        self.values = total


def send(chains, *gates):
    chains = [c for c in chains if c.left]
    held = tie([c.values for c in chains], gates)[0]
    for c, v in zip(chains, held):
        c.values = v
    for c in chains:
        c.send()


def fence(chains, *values):
    chains = [c for c in chains if c.left]
    held, values = tie([(c.values, c.got) for c in chains], values)
    for c, (v, g) in zip(chains, held):
        c.values, c.got = v, g
        c.merge()
    held, values = tie(marks(chains), values)
    for c, v in zip(chains, held):
        c.values = v
    return values if len(values) != 1 else values[0]


def step(chains, *gates):
    send(chains, *gates)
    fence(chains)


def complete(chains):
    while any(c.left for c in chains):
        step(chains)


def join_chains(chains):
    chains[0].values = jnp.concatenate([c.values for c in chains], axis=-1)
    del chains[1:]


def marks(chains):
    return [c.values for c in chains]


def pair(values):
    return lax.ppermute(values, "tensor", [(0, 1), (1, 0)])


def norm_of(values, gain_vec, bias_vec):
    centred = values - jnp.mean(values, axis=-1, keepdims=True)
    inverse = lax.rsqrt(jnp.mean(centred * centred, axis=-1, keepdims=True) + norm_eps)
    return centred * inverse * gain_vec + bias_vec


def to_steps(steps_ref, row_first, values, col_first):
    rows, cols = values.shape
    tiles = steps_ref.shape[1]
    for j in range(cols // LANES):
        steps_ref[pl.ds(row_first, rows), col_first // LANES + j, :] = values[
            :, j * LANES : (j + 1) * LANES
        ]


def run_docs(starts_ref, low, high, one_step, make_start, finish, backward, unroll=8):
    for doc in range(NDOCS):
        d = NDOCS - 1 - doc if backward else doc
        first = jnp.minimum(jnp.maximum(starts_ref[d], low), high)
        last = jnp.minimum(jnp.maximum(starts_ref[d + 1], low), high)
        length = last - first
        groups = length // unroll
        carry = make_start(d)

        def group_body(g, carry):
            base = last - 1 - g * unroll if backward else first + g * unroll
            for i in range(unroll):
                carry = one_step(base - i if backward else base + i, carry)
            return carry

        carry = lax.fori_loop(0, groups, group_body, carry)
        done = groups * unroll

        def one_body(i, carry):
            return one_step(last - 1 - done - i if backward else first + done + i, carry)

        carry = lax.fori_loop(0, length - done, one_body, carry)
        finish(d, length, carry)


def add_up(parts):
    while len(parts) > 1:
        parts = [parts[k] + parts[k + 1] for k in range(0, len(parts), 2)]
    return parts[0]


def scan_states(starts_ref, low, high, drive_ref, decay_ref, coef_ref, y_ref, start_ref, end_ref):
    states = decay_ref.shape[0]
    zero = jnp.zeros(decay_ref.shape[1:], F32)

    def one_step(t, state):
        u = drive_ref[t]
        new = [decay_ref[n] * state[n] + u for n in range(states)]
        y_ref[t - low] = add_up([coef_ref[n] * new[n] for n in range(states)])
        return tuple(new)

    def make_start(d):
        if start_ref is None:
            return (zero,) * states
        going = starts_ref[d] < low
        return tuple(jnp.where(going, start_ref[n], zero) for n in range(states))

    def finish(d, length, carry):
        if end_ref is not None:

            @pl.when(length > 0)
            def _():
                for n in range(states):
                    end_ref[n] = carry[n]

    run_docs(starts_ref, low, high, one_step, make_start, finish, False)


def from_steps(steps_ref, out_ref):
    length, tiles, _ = steps_ref.shape
    chunk = 256

    def write(i, _):
        r = pl.multiple_of(i * chunk, chunk)
        for j in range(tiles):
            out_ref[pl.ds(r, chunk), j * LANES : (j + 1) * LANES] = steps_ref[
                pl.ds(r, chunk), j, :
            ].astype(BF)
        return 0

    lax.fori_loop(0, length // chunk, write, 0)


def both_parts(own, other, joined, at, sems):
    copies = [
        pltpu.make_async_copy(own, joined.at[at(0)], sems.at[0]),
        pltpu.make_async_copy(other, joined.at[at(1)], sems.at[1]),
    ]
    for copy in copies:
        copy.start()
    return copies


def cols_at(side, cols):
    return lambda k: (
        slice(None),
        pl.ds(pl.multiple_of((side if k == 0 else 1 - side) * cols, cols), cols),
    )


def rows_at(side, rows, *lead):
    return lambda k: lead + (
        pl.ds(pl.multiple_of((side if k == 0 else 1 - side) * rows, rows), rows),
    )


def wait_all(copies):
    for copy in copies:
        copy.wait()


def ssm_forward_kernel(
    starts_ref, side_ref, mine_ref, got_ref, mix_own_ref, mix_other_ref, gain_ref, bias_ref, decay_ref, coef_ref,
    rows_ref, normed_ref, drive_ref, out_ref, end_ref, y_ref, mix_ref, sems,
):
    length, width = rows_ref.shape
    side = side_ref[0]
    copies = both_parts(
        mine_ref.at[side], got_ref.at[side], rows_ref, rows_at(side, length // 2), sems.at[0]
    ) + both_parts(
        mix_own_ref, mix_other_ref, mix_ref, cols_at(side, width // 2), sems.at[1]
    )
    wait_all(copies)
    chunk = 256

    def project(i, _):
        r = pl.multiple_of(i * chunk, chunk)
        normed = norm_of(
            rows_ref[pl.ds(r, chunk), :].astype(F32), gain_ref[...], bias_ref[...]
        ).astype(BF)
        normed_ref[pl.ds(r, chunk), :] = normed
        for c in range(0, width, 256):
            to_steps(drive_ref, r, dot_plain(normed, mix_ref[:, c : c + 256]), c)
        return 0

    lax.fori_loop(0, length // chunk, project, 0)
    scan_states(
        starts_ref, 0, length // 2, drive_ref, decay_ref, coef_ref, y_ref, None, end_ref
    )
    from_steps(y_ref, out_ref)


def ssm_rest_kernel(
    starts_ref, side_ref, mine_ref, got_ref, drive_ref, decay_ref, coef_ref, start_ref, first_ref,
    out_ref, cot_ref, y_ref, sems,
):
    length = drive_ref.shape[0]
    half = length // 2
    side = side_ref[0]
    copies = both_parts(
        mine_ref.at[side], got_ref.at[side], cot_ref, rows_at(side, half, 0), sems.at[0]
    ) + both_parts(
        mine_ref.at[1 - side], got_ref.at[1 - side], cot_ref, rows_at(side, half, 1), sems.at[1]
    )
    scan_states(
        starts_ref, half, length, drive_ref, decay_ref, coef_ref, y_ref, start_ref, None
    )
    out_ref[:half, :] = first_ref[...]
    from_steps(y_ref, out_ref.at[half:])
    wait_all(copies)


SMALL = pl.BlockSpec(memory_space=pltpu.SMEM)
WHOLE = pl.BlockSpec(memory_space=pltpu.VMEM)
ANYWHERE = pl.BlockSpec(memory_space=pl.ANY)
COPIES = pltpu.SemaphoreType.DMA((2, 2))


def ssm_forward(starts, side, mine, got, mix_own, mix_other, gain_vec, bias_vec, decay, coef):
    length, width = 2 * mine.shape[1], mine.shape[2]
    tiles = width // LANES
    return pl.pallas_call(
        ssm_forward_kernel,
        out_shape=(
            jax.ShapeDtypeStruct((length, width), BF),
            jax.ShapeDtypeStruct((length, width), BF),
            jax.ShapeDtypeStruct((length, tiles, LANES), F32),
            jax.ShapeDtypeStruct((length // 2, width), BF),
            jax.ShapeDtypeStruct(decay.shape, F32),
        ),
        in_specs=[SMALL] * 2 + [ANYWHERE] * 4 + [WHOLE] * 4,
        out_specs=(WHOLE,) * 5,
        scratch_shapes=[
            pltpu.VMEM((length // 2, tiles, LANES), F32),
            pltpu.VMEM((width, width), BF),
            COPIES,
        ],
        compiler_params=pltpu.CompilerParams(vmem_limit_bytes=VMEM),
        cost_estimate=pl.CostEstimate(
            flops=12 * length * width * width,
            bytes_accessed=16 * length * width,
            transcendentals=0,
        ),
        name="ssm_forward",
    )(starts, side, mine, got, mix_own, mix_other, gain_vec, bias_vec, decay, coef)


def ssm_rest(starts, side, mine, got, drive, decay, coef, start, first):
    length, tiles, _ = drive.shape
    width = tiles * LANES
    return pl.pallas_call(
        ssm_rest_kernel,
        out_shape=(
            jax.ShapeDtypeStruct((length, width), BF),
            jax.ShapeDtypeStruct((2, length, width), BF),
        ),
        in_specs=[SMALL] * 2 + [ANYWHERE] * 2 + [WHOLE] * 5,
        out_specs=(WHOLE, WHOLE),
        scratch_shapes=[pltpu.VMEM((length // 2, tiles, LANES), F32), COPIES],
        compiler_params=pltpu.CompilerParams(vmem_limit_bytes=VMEM),
        cost_estimate=pl.CostEstimate(
            flops=10 * length * width * width,
            bytes_accessed=16 * length * width,
            transcendentals=0,
        ),
        name="ssm_rest",
    )(starts, side, mine, got, drive, decay, coef, start, first)


def project_kernel(
    side_ref, normed_ref, ssm_ref, left_own_ref, left_other_ref, right_own_ref, right_other_ref,
    query_ref, key_ref, value_ref, weights_ref, sems,
):
    width = normed_ref.shape[1]
    cols = width // 2
    at = cols_at(side_ref[0], cols)
    sources = (
        (left_own_ref, left_other_ref, 0),
        (left_own_ref, left_other_ref, cols),
        (right_own_ref, right_other_ref, 0),
    )
    copies = [
        both_parts(
            own.at[:, c : c + cols], other.at[:, c : c + cols], weights_ref.at[k], at, sems.at[k]
        )
        for k, (own, other, c) in enumerate(sources)
    ]
    for k, (rows_ref, out_ref) in enumerate(
        ((normed_ref, query_ref), (ssm_ref, key_ref), (ssm_ref, value_ref))
    ):
        wait_all(copies[k])
        for c in range(0, width, cols):
            out_ref[:, c : c + cols] = dot_plain(
                rows_ref[...], weights_ref[k, :, c : c + cols]
            ).astype(BF)


def project(side, normed, ssm_out, left, right):
    length, width = normed.shape
    return pl.pallas_call(
        project_kernel,
        out_shape=(jax.ShapeDtypeStruct((length, width), BF),) * 3,
        in_specs=[SMALL] + [WHOLE] * 2 + [ANYWHERE] * 4,
        out_specs=(WHOLE,) * 3,
        scratch_shapes=[pltpu.VMEM((3, width, width), BF), pltpu.SemaphoreType.DMA((3, 2))],
        compiler_params=pltpu.CompilerParams(vmem_limit_bytes=VMEM),
        cost_estimate=pl.CostEstimate(
            flops=6 * length * width * width, bytes_accessed=16 * length * width, transcendentals=0
        ),
        name="project",
    )(side, normed, ssm_out, *left, *right)


def adjoint_states(starts_ref, low, drive_ref, g_ref, decay_ref, coef_ref, gm_ref, sum_ref, dsum_ref, given_ref):
    length = g_ref.shape[0]
    part = sum_ref.shape[0]
    zero = jnp.zeros(decay_ref.shape[1:], F32)

    def one_step(t, carry):
        mu, rho, total, dtotal = carry
        u = drive_ref[t]
        g = g_ref[t]
        new_mu, new_rho, new_total, new_dtotal, parts = [], [], [], [], []
        for n in range(part):
            a = decay_ref[low + n]
            r = a * rho[n] + mu[n]
            m = a * mu[n] + g
            new_mu.append(m)
            new_rho.append(r)
            new_total.append(total[n] + u * m)
            new_dtotal.append(dtotal[n] + u * r)
            parts.append(coef_ref[low + n] * m)
        gm = add_up(parts)
        gm_ref[t] = gm if given_ref is None else gm + given_ref[t]
        return tuple(new_mu), tuple(new_rho), tuple(new_total), tuple(new_dtotal)

    for n in range(part):
        sum_ref[n] = zero
        dsum_ref[n] = zero

    def make_start(d):
        zeros = (zero,) * part
        return zeros, zeros, zeros, zeros

    def finish(d, count, carry):
        for n in range(part):
            sum_ref[n] = sum_ref[n] + carry[2][n]
            dsum_ref[n] = dsum_ref[n] + carry[3][n]

    run_docs(starts_ref, 0, length, one_step, make_start, finish, True)


def ssm_backward_kernel(
    starts_ref, side_ref, gkey_ref, gvalue_ref, left_own_ref, left_other_ref, right_own_ref, right_other_ref,
    drive_ref, decay_ref, coef_ref, g_ref, gm_ref, sum_ref, dsum_ref, wkey_ref, wvalue_ref, sems,
):
    length, width = gkey_ref.shape
    cols = width // 2
    at = cols_at(side_ref[0], cols)
    copies = both_parts(
        left_own_ref.at[:, cols:], left_other_ref.at[:, cols:], wkey_ref, at, sems.at[0]
    ) + both_parts(
        right_own_ref.at[:, :cols], right_other_ref.at[:, :cols], wvalue_ref, at, sems.at[1]
    )
    wait_all(copies)
    chunk = 256

    def project(i, _):
        r = pl.multiple_of(i * chunk, chunk)
        gkey = gkey_ref[pl.ds(r, chunk), :]
        gvalue = gvalue_ref[pl.ds(r, chunk), :]
        for c in range(0, width, 256):
            to_steps(
                g_ref,
                r,
                dot_last(gkey, wkey_ref[c : c + 256, :])
                + dot_last(gvalue, wvalue_ref[c : c + 256, :]),
                c,
            )
        return 0

    lax.fori_loop(0, length // chunk, project, 0)
    adjoint_states(
        starts_ref, 0, drive_ref, g_ref, decay_ref, coef_ref, gm_ref, sum_ref, dsum_ref, None
    )


def ssm_backward_rest_kernel(
    starts_ref, g_ref, given_ref, drive_ref, decay_ref, coef_ref,
    gmixed_ref, sum_ref, dsum_ref, gm_ref,
):
    adjoint_states(
        starts_ref, decay_ref.shape[0] // 2, drive_ref, g_ref, decay_ref, coef_ref, gm_ref,
        sum_ref, dsum_ref, given_ref,
    )
    from_steps(gm_ref, gmixed_ref)


def ssm_backward(starts, side, gkey, gvalue, left, right, drive, decay, coef):
    length, width = gkey.shape
    tiles = width // LANES
    vm = pl.BlockSpec(memory_space=pltpu.VMEM)
    half = (decay.shape[0] // 2,) + decay.shape[1:]
    return pl.pallas_call(
        ssm_backward_kernel,
        out_shape=(
            jax.ShapeDtypeStruct((length, tiles, LANES), F32),
            jax.ShapeDtypeStruct((length, tiles, LANES), F32),
            jax.ShapeDtypeStruct(half, F32),
            jax.ShapeDtypeStruct(half, F32),
        ),
        in_specs=[SMALL] * 2 + [vm] * 2 + [ANYWHERE] * 4 + [vm] * 3,
        out_specs=(vm,) * 4,
        scratch_shapes=[pltpu.VMEM((width, width), BF)] * 2 + [COPIES],
        compiler_params=pltpu.CompilerParams(vmem_limit_bytes=VMEM),
        cost_estimate=pl.CostEstimate(
            flops=20 * length * width * width,
            bytes_accessed=20 * length * width,
            transcendentals=0,
        ),
        name="ssm_backward",
    )(starts, side, gkey, gvalue, *left, *right, drive, decay, coef)


def ssm_backward_rest(starts, g, given, drive, decay, coef):
    length, tiles, _ = drive.shape
    width = tiles * LANES
    vm = pl.BlockSpec(memory_space=pltpu.VMEM)
    half = (decay.shape[0] // 2,) + decay.shape[1:]
    return pl.pallas_call(
        ssm_backward_rest_kernel,
        out_shape=(
            jax.ShapeDtypeStruct((length, width), BF),
            jax.ShapeDtypeStruct(half, F32),
            jax.ShapeDtypeStruct(half, F32),
        ),
        in_specs=[pl.BlockSpec(memory_space=pltpu.SMEM)] + [vm] * 5,
        out_specs=(vm,) * 3,
        scratch_shapes=[pltpu.VMEM((length, tiles, LANES), F32)],
        compiler_params=pltpu.CompilerParams(vmem_limit_bytes=VMEM),
        cost_estimate=pl.CostEstimate(
            flops=20 * length * width * width,
            bytes_accessed=20 * length * width,
            transcendentals=0,
        ),
        name="ssm_backward_rest",
    )(starts, g, given, drive, decay, coef)


def attention_tiles(length):
    tiles = []
    for first in range(0, length, QTILE):
        block_first = first // BLOCK * BLOCK
        key_first = max(0, block_first - CTX)
        tiles.append((first, key_first, first + QTILE - key_first))
    return tiles


def fill_bias(seg_col_ref, seg_row_ref, bias_ref, tiles):
    at = 0
    for first, key_first, count in tiles:
        same = seg_col_ref[first : first + QTILE, :] == seg_row_ref[:, key_first : key_first + count]
        query_pos = lax.broadcasted_iota(jnp.int32, (QTILE, count), 0) + first
        key_pos = lax.broadcasted_iota(jnp.int32, (QTILE, count), 1) + key_first
        bias_ref[:, at : at + count] = jnp.where(
            same & (key_pos <= query_pos), 0.0, masked_score
        ).astype(F32)
        at += count


EXP_SCALE = HEAD_DIM ** (-0.5) * math.log2(math.e)


def attention_jobs(length):
    jobs = []
    for h in range(HEADS_EACH):
        at = 0
        for first, key_first, count in attention_tiles(length):
            jobs.append(
                (
                    h,
                    slice(h * HEAD_DIM, (h + 1) * HEAD_DIM),
                    slice(first, first + QTILE),
                    slice(key_first, key_first + count),
                    slice(at, at + count),
                )
            )
            at += count
    return jobs


def attention_forward_kernel(
    seg_col_ref, seg_row_ref, query_ref, key_ref, value_ref, out_ref, lse_ref, bias_ref, value_one_ref
):
    length = query_ref.shape[0]

    @pl.when(pl.program_id(0) == 0)
    def _():
        fill_bias(seg_col_ref, seg_row_ref, bias_ref, attention_tiles(length))
        for h in range(HEADS_EACH):
            value_one_ref[h, :, HEAD_DIM:] = jnp.ones((length, HEAD_DIM), BF)

    for h in range(HEADS_EACH):
        value_one_ref[h, :, :HEAD_DIM] = value_ref[:, h * HEAD_DIM : (h + 1) * HEAD_DIM]
    jobs = attention_jobs(length)

    def scores_of(job):
        _, lanes, rows, keys, _ = job
        return dot_last(query_ref[rows, lanes], key_ref[keys, lanes])

    ahead = scores_of(jobs[0])
    for k, (h, lanes, rows, keys, mask) in enumerate(jobs):
        scores = ahead
        if k + 1 < len(jobs):
            ahead = scores_of(jobs[k + 1])
        scores = scores * EXP_SCALE + bias_ref[:, mask]
        top = jnp.max(scores, axis=-1, keepdims=True)
        raised = jnp.exp2(scores - top).astype(BF)
        both = dot_plain(raised, value_one_ref[h, keys, :])
        total = both[:, HEAD_DIM:]
        out_ref[rows, lanes] = (both[:, :HEAD_DIM] / total).astype(BF)
        lse_ref[h, rows, :] = top + jnp.log2(total[:, :1])


def attention_forward(seg_col, seg_row, query, key, value):
    length, width = query.shape
    heads = width // HEAD_DIM
    tiles = attention_tiles(length)
    cols = sum(t[2] for t in tiles)
    head = pl.BlockSpec((length, HEADS_EACH * HEAD_DIM), lambda h: (0, h))
    whole = lambda shape: pl.BlockSpec(shape, lambda h: (0, 0))
    return pl.pallas_call(
        attention_forward_kernel,
        grid=(heads // HEADS_EACH,),
        out_shape=(
            jax.ShapeDtypeStruct((length, width), BF),
            jax.ShapeDtypeStruct((heads, length, 1), F32),
        ),
        in_specs=[whole((length, 1)), whole((1, length)), head, head, head],
        out_specs=(head, pl.BlockSpec((HEADS_EACH, length, 1), lambda h: (h, 0, 0))),
        scratch_shapes=[
            pltpu.VMEM((QTILE, cols), F32),
            pltpu.VMEM((HEADS_EACH, length, 2 * HEAD_DIM), BF),
        ],
        compiler_params=params(),
        cost_estimate=pl.CostEstimate(
            flops=4 * QTILE * cols * width,
            bytes_accessed=8 * length * width,
            transcendentals=QTILE * cols * heads,
        ),
        name="attention_forward",
    )(seg_col, seg_row, query, key, value)


def attention_backward_kernel(
    seg_col_ref, seg_row_ref, query_ref, key_ref, value_ref, lse_ref, gout_ref,
    gquery_ref, gkey_ref, gvalue_ref, bias_ref, gk_ref, gv_ref,
):
    length = query_ref.shape[0]
    scale = HEAD_DIM ** (-0.5)

    @pl.when(pl.program_id(0) == 0)
    def _():
        fill_bias(seg_col_ref, seg_row_ref, bias_ref, attention_tiles(length))

    gk_ref[...] = jnp.zeros_like(gk_ref)
    gv_ref[...] = jnp.zeros_like(gv_ref)
    jobs = attention_jobs(length)

    def scores_of(job):
        _, lanes, rows, keys, _ = job
        return (
            dot_last(query_ref[rows, lanes], key_ref[keys, lanes]),
            dot_last(gout_ref[rows, lanes], value_ref[keys, lanes]),
        )

    ahead = scores_of(jobs[0])
    for k, (h, lanes, rows, keys, mask) in enumerate(jobs):
        scores, gprobs = ahead
        if k + 1 < len(jobs):
            ahead = scores_of(jobs[k + 1])
        gout = gout_ref[rows, lanes]
        probs = jnp.exp2(scores * EXP_SCALE + bias_ref[:, mask] - lse_ref[h, rows, :])
        gv_ref[keys, lanes] = gv_ref[keys, lanes] + dot_first(probs.astype(BF), gout)
        inner = jnp.sum(probs * gprobs, axis=-1, keepdims=True)
        gscores = (probs * (gprobs - inner)).astype(BF)
        gquery_ref[rows, lanes] = (dot_plain(gscores, key_ref[keys, lanes]) * scale).astype(BF)
        gk_ref[keys, lanes] = gk_ref[keys, lanes] + dot_first(gscores, query_ref[rows, lanes])
    gkey_ref[...] = (gk_ref[...] * scale).astype(BF)
    gvalue_ref[...] = gv_ref[...].astype(BF)


def attention_backward(seg_col, seg_row, query, key, value, lse, gout):
    length, width = query.shape
    heads = width // HEAD_DIM
    tiles = attention_tiles(length)
    cols = sum(t[2] for t in tiles)
    head = pl.BlockSpec((length, HEADS_EACH * HEAD_DIM), lambda h: (0, h))
    whole = lambda shape: pl.BlockSpec(shape, lambda h: (0, 0))
    return pl.pallas_call(
        attention_backward_kernel,
        grid=(heads // HEADS_EACH,),
        out_shape=(jax.ShapeDtypeStruct((length, width), BF),) * 3,
        in_specs=[whole((length, 1)), whole((1, length)), head, head, head]
        + [pl.BlockSpec((HEADS_EACH, length, 1), lambda h: (h, 0, 0)), head],
        out_specs=(head,) * 3,
        scratch_shapes=[
            pltpu.VMEM((QTILE, cols), F32),
            pltpu.VMEM((length, HEADS_EACH * HEAD_DIM), F32),
            pltpu.VMEM((length, HEADS_EACH * HEAD_DIM), F32),
        ],
        compiler_params=params(),
        cost_estimate=pl.CostEstimate(
            flops=10 * QTILE * cols * width,
            bytes_accessed=14 * length * width,
            transcendentals=QTILE * cols * heads,
        ),
        name="attention_backward",
    )(seg_col, seg_row, query, key, value, lse, gout)


def norm_backward(grad, values, gain_vec):
    centred = values - jnp.mean(values, axis=-1, keepdims=True)
    inverse = lax.rsqrt(jnp.mean(centred * centred, axis=-1, keepdims=True) + norm_eps)
    xhat = centred * inverse
    dxhat = grad * gain_vec
    back = (
        dxhat
        - jnp.mean(dxhat, axis=-1, keepdims=True)
        - xhat * jnp.mean(dxhat * xhat, axis=-1, keepdims=True)
    ) * inverse
    return back, jnp.sum(grad * xhat, axis=0, keepdims=True), jnp.sum(grad, axis=0, keepdims=True)


def gelu_parts(values):
    below = 0.5 + 0.5 * lax.erf(values * (2.0**-0.5))
    bell = jnp.exp2((-0.5 * math.log2(math.e)) * (values * values))
    return values * below, below + values * (bell * ((2.0 * math.pi) ** -0.5))


FTILE = 512


def feed_forward_kernel(part, *refs):
    ins, refs = refs[: 5 + 4 * (part > 0)], refs[5 + 4 * (part > 0) :]
    own_ref, other_ref, cot_ref, up_in_ref, down_in_ref = ins[:5]
    outs, grads, refs = refs[:4], refs[4:6], refs[6:]
    normed_ref, cots_ref, up_ref, down_ref, hidden_ref, gpre_ref, sums_ref, total_ref = refs[:8]
    row_sems, weight_sems, out_sems, grad_sems = refs[8:12]
    length, width = own_ref.shape
    units = up_ref.shape[1]
    tile = FTILE
    per = length // tile
    count = 2 * per

    def tile_of(i):
        return pl.ds(pl.multiple_of(i * tile, tile), tile)

    weights = [
        pltpu.make_async_copy(up_in_ref, up_ref, weight_sems.at[0]),
        pltpu.make_async_copy(down_in_ref, down_ref, weight_sems.at[1]),
    ]
    for copy in weights:
        copy.start()
    for i in range(count):
        rows = tile_of(i % per)
        source = (own_ref, other_ref)[i // per]
        pltpu.make_async_copy(source.at[rows], normed_ref.at[tile_of(i)], row_sems.at[0, i]).start()
        pltpu.make_async_copy(
            cot_ref.at[i // per, rows], cots_ref.at[tile_of(i)], row_sems.at[1, i]
        ).start()
    if part:
        earlier = [
            pltpu.make_async_copy(ins[5 + k], total_ref.at[k], out_sems.at[k, count])
            for k in range(4)
        ]
        for copy in earlier:
            copy.start()
    wait_all(weights)

    def one(i, _):
        rows = tile_of(i)
        for k, ref in enumerate((normed_ref, cots_ref)):
            pltpu.make_async_copy(ref.at[rows], ref.at[rows], row_sems.at[k, i]).wait()
        for n in range(0, units, tile):
            pre = dot_plain(normed_ref[rows, :], up_ref[:, n : n + tile])
            ghidden = dot_plain(cots_ref[rows, :], down_ref[:, n : n + tile])
            hidden, slope = gelu_parts(pre)
            hidden_ref[rows, n : n + tile] = hidden.astype(BF)
            gpre_ref[rows, n : n + tile] = (ghidden * slope).astype(BF)
        return 0

    lax.fori_loop(0, count, one, 0)

    grad_copies = []
    for k, (first_ref, held_ref) in enumerate(((normed_ref, gpre_ref), (cots_ref, hidden_ref))):

        def three(i, _, k=k, first_ref=first_ref, held_ref=held_ref):
            cols = tile_of(i)
            sums_ref[k, cols, :] = dot_first(first_ref[:, cols], held_ref[...]).astype(BF)
            return 0

        lax.fori_loop(0, width // tile, three, 0)
        copy = pltpu.make_async_copy(
            sums_ref.at[k], grads[k], grad_sems.at[k]
        )
        copy.start()
        grad_copies.append(copy)

    if part:
        wait_all(earlier)
    out_copies = []
    for i in range(count):
        s, rows = i // per, slice(i % per * tile, (i % per + 1) * tile)
        held = slice(i * tile, (i + 1) * tile)
        for k, (held_ref, weight_ref) in enumerate(((hidden_ref, down_ref), (gpre_ref, up_ref))):
            total = dot_last(held_ref[held, :], weight_ref[...])
            if part:
                total = total + total_ref[2 * k + s, rows, :].astype(F32)
            total_ref[2 * k + s, rows, :] = total.astype(BF)
            copy = pltpu.make_async_copy(
                total_ref.at[2 * k + s, rows], outs[2 * k + s].at[rows], out_sems.at[k, i]
            )
            copy.start()
            out_copies.append(copy)
    wait_all(grad_copies + out_copies)


def feed_forward(part, own, other, cot, up, down, earlier):
    length, width = own.shape
    units = up.shape[1]
    count = 2 * length // FTILE
    dma = pltpu.SemaphoreType.DMA
    return pl.pallas_call(
        functools.partial(feed_forward_kernel, part),
        out_shape=(jax.ShapeDtypeStruct((length, width), BF),) * 4
        + (jax.ShapeDtypeStruct((width, units), BF),) * 2,
        in_specs=[ANYWHERE] * (9 if part else 5),
        out_specs=(ANYWHERE,) * 6,
        scratch_shapes=[pltpu.VMEM((2 * length, width), BF)] * 2
        + [pltpu.VMEM((width, units), BF)] * 2
        + [pltpu.VMEM((2 * length, units), BF)] * 2
        + [pltpu.VMEM((2, width, units), BF), pltpu.VMEM((4, length, width), BF)]
        + [dma((2, count)), dma((2,)), dma((4, count + 1)), dma((2,))],
        compiler_params=pltpu.CompilerParams(vmem_limit_bytes=VMEM),
        cost_estimate=pl.CostEstimate(
            flops=28 * length * width * units,
            bytes_accessed=48 * length * width,
            transcendentals=4 * length * units,
        ),
        name="feed_forward",
    )(own, other, cot, up, down, *earlier)


def at_first(joins, sems, side):
    @pl.when(pl.program_id(0) == 0)
    def _():
        copies = []
        for k, (own, other, joined) in enumerate(joins):
            copies += both_parts(own, other, joined, cols_at(side, joined.shape[1] // 2), sems.at[k])
        wait_all(copies)


ROWS = 256


def row_spec(width, lead=None):
    if lead is None:
        return pl.BlockSpec((ROWS, width), lambda i: (i, 0))
    return pl.BlockSpec((None, ROWS, width), lambda i: (lead, i, 0))


def fixed(*shape):
    return pl.BlockSpec(shape, lambda i: (0,) * len(shape))


def middle_kernel(
    side_ref, attended_ref, own_ref, other_ref, rows_ref, gain_ref, bias_ref, middle_ref, normed_ref, out_ref, sems
):
    cols = out_ref.shape[1] // 2
    at_first([(own_ref.at[:, cols:], other_ref.at[:, cols:], out_ref)], sems, side_ref[0])
    middle = rows_ref[...].astype(F32) + dot_last(attended_ref[...], out_ref[...])
    middle_ref[...] = middle
    normed_ref[...] = norm_of(middle, gain_ref[...], bias_ref[...]).astype(BF)


def middle_of(side, attended, right, rows, gain_vec, bias_vec):
    length, width = rows.shape
    row = row_spec(width)
    return pl.pallas_call(
        middle_kernel,
        grid=(length // ROWS,),
        out_shape=(
            jax.ShapeDtypeStruct((length, width), F32),
            jax.ShapeDtypeStruct((length, width), BF),
        ),
        in_specs=[SMALL, row, ANYWHERE, ANYWHERE, row, fixed(1, width), fixed(1, width)],
        out_specs=(row, row),
        scratch_shapes=[pltpu.VMEM((width, width), BF), COPIES],
        compiler_params=params(),
        cost_estimate=pl.CostEstimate(
            flops=2 * length * width * width, bytes_accessed=12 * length * width, transcendentals=0
        ),
        name="middle",
    )(side, attended, *right, rows, gain_vec, bias_vec)


def norm_two_kernel(
    side_ref, mine_ref, theirs_ref, middle_ref, cot_ref, gain_ref, own_ref, other_ref,
    gmiddle_ref, gbranch_ref, gattended_ref, sums_ref, out_ref, sems,
):
    cols = out_ref.shape[1] // 2
    at_first([(own_ref.at[:, cols:], other_ref.at[:, cols:], out_ref)], sems, side_ref[0])
    grad = mine_ref[...].astype(F32) + theirs_ref[...].astype(F32)
    back, gain_sum, bias_sum = norm_backward(grad, middle_ref[...], gain_ref[...])
    gmiddle = cot_ref[...].astype(F32) + back
    gmiddle_ref[...] = gmiddle
    gbranch = gmiddle.astype(BF)
    gbranch_ref[...] = gbranch
    gattended_ref[...] = dot_plain(gbranch, out_ref[...]).astype(BF)
    add_sums(sums_ref, gain_sum, bias_sum)


def add_sums(sums_ref, gain_sum, bias_sum):
    @pl.when(pl.program_id(0) == 0)
    def _():
        sums_ref[...] = jnp.zeros_like(sums_ref)

    sums_ref[0:1, :] = sums_ref[0:1, :] + gain_sum
    sums_ref[1:2, :] = sums_ref[1:2, :] + bias_sum


def norm_two_back(side, mine, theirs, middle, cot, gain_vec, right):
    length, width = middle.shape
    row = row_spec(width)
    return pl.pallas_call(
        norm_two_kernel,
        grid=(length // ROWS,),
        out_shape=(
            jax.ShapeDtypeStruct((length, width), F32),
            jax.ShapeDtypeStruct((length, width), BF),
            jax.ShapeDtypeStruct((length, width), BF),
            jax.ShapeDtypeStruct((2, width), F32),
        ),
        in_specs=[SMALL, row, row, row, row_spec(width, 0), fixed(1, width), ANYWHERE, ANYWHERE],
        out_specs=(row, row, row, fixed(2, width)),
        scratch_shapes=[pltpu.VMEM((width, width), BF), COPIES],
        compiler_params=params(),
        cost_estimate=pl.CostEstimate(
            flops=2 * length * width * width, bytes_accessed=24 * length * width, transcendentals=0
        ),
        name="norm_two_back",
    )(side, mine, theirs, middle, cot, gain_vec, *right)


def norm_one_kernel(
    side_ref, gquery_ref, gmixed_ref, rows_ref, gmiddle_ref, gain_ref,
    left_own_ref, left_other_ref, mix_own_ref, mix_other_ref, grad_ref, sums_ref, query_ref, mix_ref, sems,
):
    cols = query_ref.shape[1] // 2
    at_first(
        [
            (left_own_ref.at[:, :cols], left_other_ref.at[:, :cols], query_ref),
            (mix_own_ref, mix_other_ref, mix_ref),
        ],
        sems,
        side_ref[0],
    )
    grad = dot_last(gquery_ref[...], query_ref[...]) + dot_last(gmixed_ref[...], mix_ref[...])
    back, gain_sum, bias_sum = norm_backward(grad, rows_ref[...].astype(F32), gain_ref[...])
    grad_ref[...] = gmiddle_ref[...] + back
    add_sums(sums_ref, gain_sum, bias_sum)


def norm_one_back(side, gquery, gmixed, rows, gmiddle, gain_vec, left, mix, for_partner):
    length, width = rows.shape
    half = length // 2
    steps = half // ROWS

    def place(side):
        return 1 - side[0] if for_partner else side[0]

    row = pl.BlockSpec((ROWS, width), lambda i, side: (place(side) * steps + i, 0))
    whole = lambda *shape: pl.BlockSpec(shape, lambda i, side: (0,) * len(shape))
    if for_partner:
        out = jax.ShapeDtypeStruct((half, width), F32)
        out_spec = pl.BlockSpec((ROWS, width), lambda i, side: (i, 0))
    else:
        out = jax.ShapeDtypeStruct((2, half, width), F32)
        out_spec = pl.BlockSpec((None, ROWS, width), lambda i, side: (side[0], i, 0))
    return pl.pallas_call(
        norm_one_kernel,
        grid_spec=pltpu.PrefetchScalarGridSpec(
            num_scalar_prefetch=1,
            grid=(steps,),
            in_specs=[row] * 4 + [whole(1, width)] + [ANYWHERE] * 4,
            out_specs=(out_spec, whole(2, width)),
            scratch_shapes=[pltpu.VMEM((width, width), BF)] * 2 + [COPIES],
        ),
        out_shape=(out, jax.ShapeDtypeStruct((2, width), F32)),
        compiler_params=params(),
        cost_estimate=pl.CostEstimate(
            flops=4 * half * width * width, bytes_accessed=20 * half * width, transcendentals=0
        ),
        name="norm_one_back",
    )(side, gquery, gmixed, rows, gmiddle, gain_vec, *left, *mix)


def put_kernel(side_ref, got_ref, given_ref, out_ref):
    out_ref[...] = got_ref[...]


def put(side, got, given):
    half, width = got.shape
    return pl.pallas_call(
        put_kernel,
        grid_spec=pltpu.PrefetchScalarGridSpec(
            num_scalar_prefetch=1,
            grid=(half // ROWS,),
            in_specs=[pl.BlockSpec((ROWS, width), lambda i, side: (i, 0)), ANYWHERE],
            out_specs=pl.BlockSpec((None, ROWS, width), lambda i, side: (1 - side[0], i, 0)),
        ),
        out_shape=jax.ShapeDtypeStruct(given.shape, given.dtype),
        input_output_aliases={2: 0},
        compiler_params=params(),
        name="put",
    )(side, got, given)


def layer_out_kernel(side_ref, middle_ref, own_ref, other_ref, sum_ref, theirs_ref, out_ref):
    side = side_ref[0]
    out_ref[side] = (
        middle_ref[...] + own_ref[...].astype(F32) + theirs_ref[...].astype(F32)
    )
    out_ref[1 - side] = sum_ref[...] + other_ref[...].astype(F32)


def layer_out_of(side, middle, own, other, partner_sum, partner_other):
    length, width = middle.shape
    half = length // 2
    steps = half // ROWS
    mine = pl.BlockSpec((ROWS, width), lambda i, side: (side[0] * steps + i, 0))
    row = pl.BlockSpec((ROWS, width), lambda i, side: (i, 0))
    return pl.pallas_call(
        layer_out_kernel,
        grid_spec=pltpu.PrefetchScalarGridSpec(
            num_scalar_prefetch=1,
            grid=(steps,),
            in_specs=[mine] * 3 + [row] * 2,
            out_specs=pl.BlockSpec((2, ROWS, width), lambda i, side: (0, i, 0)),
        ),
        out_shape=jax.ShapeDtypeStruct((2, half, width), F32),
        compiler_params=params(),
        cost_estimate=pl.CostEstimate(
            flops=4 * half * width, bytes_accessed=24 * half * width, transcendentals=0
        ),
        name="layer_out",
    )(side, middle, own, other, partner_sum, partner_other)


def weight_grads_kernel(count, side_ref, *refs):
    lefts, rights = refs[: len(refs) - 2 - count], refs[len(refs) - 2 - count : -2]
    theirs_ref, mine_ref = refs[-2:]
    cols = rights[0].shape[1] // 2
    side = side_ref[0]
    for k in range(count):
        for ref, at in ((theirs_ref, 1 - side), (mine_ref, side)):
            part = rights[k][:, pl.ds(pl.multiple_of(at * cols, cols), cols)]
            ref[:, k * cols : (k + 1) * cols] = dot_first(
                lefts[k % len(lefts)][...], part
            ).astype(BF)


def weight_grads(side, lefts, rights):
    count = len(rights)
    length, width = lefts[0].shape
    cols = width // 2
    vm = pl.BlockSpec(memory_space=pltpu.VMEM)
    return pl.pallas_call(
        functools.partial(weight_grads_kernel, count),
        out_shape=(jax.ShapeDtypeStruct((width, count * cols), BF),) * 2,
        in_specs=[SMALL] + [vm] * (len(lefts) + count),
        out_specs=(vm,) * 2,
        compiler_params=pltpu.CompilerParams(vmem_limit_bytes=VMEM),
        cost_estimate=pl.CostEstimate(
            flops=2 * count * length * width * width,
            bytes_accessed=6 * count * length * width,
            transcendentals=0,
        ),
        name="weight_grads",
    )(side, *lefts, *rights)


def per_device(
    count,
    layer_in,
    segment_ids,
    w_mix_in,
    w_query,
    w_key,
    w_value,
    w_attn_out,
    w_up,
    w_down,
    norm1_gain,
    norm1_bias,
    norm2_gain,
    norm2_bias,
    ssm_decay,
    ssm_inject,
    ssm_readout,
    out_grad,
):
    index = lax.axis_index("dp")
    side = lax.axis_index("tensor")
    at_side = jnp.reshape(side, (1,))
    half = layer_in.shape[2]
    width = layer_in.shape[3]
    tiles = width // LANES
    states = ssm_decay.shape[0]
    cols = w_query.shape[1]
    parts = 2
    units = w_up.shape[1] // parts
    shard_rows = w_mix_in.shape[0]

    norms = jnp.concatenate([norm1_gain, norm1_bias, norm2_gain, norm2_bias])
    norms = jnp.pad(norms[None], ((0, 7), (0, cols - norms.shape[0])))
    mix = [Gather(jnp.concatenate([w_mix_in, norms], axis=0), count, index, DIRECT)]
    send(mix)
    mine_in, got_in = layer_in[:, 0], pair(layer_in[:, 0])
    coefs = jnp.stack([ssm_decay, ssm_inject, ssm_readout])
    coefs_got = pair(coefs)
    fence(mix)
    attn = [
        Gather(
            jnp.concatenate([w_query, w_key, w_value, w_attn_out.T], axis=1), count, index, X_FIRST
        )
    ]
    turned_down = w_down.T
    ffn = [
        [
            Gather(
                jnp.concatenate(
                    [
                        w_up[:, i * units : (i + 1) * units],
                        turned_down[:, i * units : (i + 1) * units],
                    ],
                    axis=1,
                ),
                count,
                index,
                X_FIRST,
            )
        ]
        for i in range(parts)
    ]
    both_ways = (X_FIRST, Y_FIRST)
    while len(mix[0].left) > 1:
        step(mix)
    send(mix + attn)
    fence(mix + attn)
    mix_all = mix[0].result().reshape(count, shard_rows + 8, cols)
    mix_half = mix_all[:, :shard_rows].reshape(width, cols)
    mix_both = (mix_half, pair(mix_half))
    norms_all = mix_all[:, shard_rows, : 4 * shard_rows].reshape(count, 4, shard_rows)
    norms_all = norms_all.astype(F32).transpose(1, 0, 2).reshape(4, width)
    gain_one, bias_one, gain_two, bias_two = (norms_all[i : i + 1] for i in range(4))
    coefs = jnp.where(
        side == 0,
        jnp.concatenate([coefs, coefs_got], axis=2),
        jnp.concatenate([coefs_got, coefs], axis=2),
    )
    decay, inject, readout = coefs.reshape(3, states, tiles, LANES)
    coef = inject * readout
    segments = lax.dynamic_index_in_dim(segment_ids[:, 0], side, 0, keepdims=False)
    starts = jnp.sum(
        (segments[None, :] < jnp.arange(16, dtype=jnp.int32)[:, None]).astype(jnp.int32), axis=1
    )
    seg_col, seg_row = segments[:, None], segments[None, :]
    while len(attn[0].left) > 2:
        step(attn)
    attn = attn[0].split(both_ways)
    send(attn)

    rows, normed, drive, ssm_first, state_mid = ssm_forward(
        starts, at_side, mine_in, got_in, *mix_both, gain_one, bias_one, decay, coef
    )
    state_mid = fence(attn, state_mid)
    send(attn + ffn[0])
    mine_cot, got_cot = out_grad[:, 0], pair(tie(out_grad, state_mid)[0][:, 0])
    ssm_out, cot = ssm_rest(
        starts, at_side, mine_cot, got_cot, drive, decay, coef, state_mid, ssm_first
    )
    ssm_out = fence(attn + ffn[0], ssm_out)
    left, right = ((h, pair(h)) for h in (m.result() for m in attn))
    while len(ffn[0][0].left) > 2:
        step(ffn[0])
    ffn[0] = ffn[0][0].split(both_ways)
    send(ffn[0] + ffn[1])
    query, key, value = project(at_side, normed, ssm_out, left, right)
    query = fence(ffn[0], query)
    send(ffn[0])
    attended, lse = attention_forward(seg_col, seg_row, query, key, value)
    attended = fence(ffn[0] + ffn[1], attended)
    while len(ffn[1][0].left) > 2:
        step(ffn[1])
    ffn[1] = ffn[1][0].split(both_ways)
    send(ffn[1])
    middle, normed_two = middle_of(at_side, attended, right, rows, gain_two, bias_two)

    middle, normed_two = fence(ffn[1], middle, normed_two)
    send(ffn[1])

    def scatters(left, right):
        return [Scatter(left, count, index, X_FIRST), Scatter(right, count, index, Y_FIRST)]

    normed_other = pair(normed_two)
    *both, grad_up, grad_down = feed_forward(
        0, normed_two, normed_other, cot, *(m.result() for m in ffn[0]), ()
    )
    both, grad_up, grad_down = fence(ffn[1], both, grad_up, grad_down)
    sums_one = scatters(grad_up, grad_down)
    send(sums_one)
    own, other, gown, gother, grad_up, grad_down = feed_forward(
        1, normed_two, normed_other, cot, *(m.result() for m in ffn[1]), both
    )
    own, other, gown, gother, grad_up, grad_down = fence(
        sums_one, own, other, gown, gother, grad_up, grad_down
    )
    send(sums_one)
    sums_two = scatters(grad_up, grad_down)

    grad_middle, grad_branch, grad_attended, norm_two_sums = norm_two_back(
        at_side, gown, pair(gother), middle, cot, gain_two, right
    )
    grad_attended = fence(sums_one, grad_attended)
    send(sums_two)
    grad_query, grad_key, grad_value = attention_backward(
        seg_col, seg_row, query, key, value, lse, grad_attended
    )
    grad_query, grad_key, grad_value = fence(sums_two, grad_query, grad_key, grad_value)
    send(sums_two)

    def pair_sum(theirs, mine):
        return (mine.astype(F32) + pair(theirs).astype(F32)).astype(BF)

    grads_left = weight_grads(at_side, (normed, grad_branch), (grad_query, attended))
    grads_left, ssm_out = tie(grads_left, ssm_out)
    grads_right = weight_grads(at_side, (ssm_out,), (grad_key, grad_value))
    sums_left = pair_sum(*grads_left)
    grads_right = fence(sums_two, grads_right)
    sums_attn = scatters(sums_left, pair_sum(*grads_right))
    sums_ffn = sums_one + sums_two
    join_chains(sums_ffn)
    send(sums_attn + sums_ffn)
    g_steps, gm_steps, sum_one, dsum_one = ssm_backward(
        starts, at_side, grad_key, grad_value, left, right, drive, decay, coef
    )
    g_steps, gm_steps = fence(sums_attn, g_steps, gm_steps)
    send(sums_attn)
    grad_mixed, sum_two, dsum_two = ssm_backward_rest(
        starts, g_steps, gm_steps, drive, decay, coef
    )
    grad_mixed = fence(sums_attn + sums_ffn, grad_mixed)
    join_chains(sums_attn)
    send(sums_attn)
    grads_mix = weight_grads(at_side, (normed,), (grad_mixed,))
    grads_mix, grad_mixed = tie(grads_mix, grad_mixed)
    sums_mix = [Scatter(pair_sum(*grads_mix), count, index, DIRECT)]
    for_partner, norm_one_first = norm_one_back(
        at_side, grad_query, grad_mixed, rows, grad_middle, gain_one, left, mix_both, True
    )
    for_partner, grad_mixed, sums_mix[0].values = fence(
        sums_attn, for_partner, grad_mixed, sums_mix[0].values
    )
    send(sums_mix)
    got_grad = pair(for_partner)
    in_grad, norm_one_second = norm_one_back(
        at_side, grad_query, grad_mixed, rows, grad_middle, gain_one, left, mix_both, False
    )
    in_grad, norm_one_second, middle, own, other = fence(
        sums_mix, in_grad, norm_one_second, middle, own, other
    )

    state_sums = jnp.concatenate([sum_one, sum_two, dsum_one, dsum_two]).reshape(
        2 * states, width
    )
    sums = jnp.concatenate(
        [
            lax.dynamic_slice_in_dim(state_sums, (1 - side) * cols, cols, 1),
            (norm_one_first + norm_one_second).reshape(-1, cols),
            norm_two_sums.reshape(-1, cols),
        ]
    )
    mine = lax.dynamic_slice_in_dim(state_sums, side * cols, cols, 1)
    small = [Total(jnp.concatenate([mine, sums[2 * states :]]) + pair(sums), count)]
    send(sums_mix + small)
    in_half = (1 - side) * half
    partner_sum = pair(
        lax.dynamic_slice_in_dim(middle, in_half, half, 0)
        + lax.dynamic_slice_in_dim(own, in_half, half, 0).astype(F32)
    )
    partner_other = pair(lax.dynamic_slice_in_dim(other, in_half, half, 0))
    in_grad = put(at_side, got_grad, in_grad)
    in_grad, middle = fence(sums_mix + small, in_grad, middle)
    send(small)
    layer_out = layer_out_of(at_side, middle, own, other, partner_sum, partner_other)
    layer_out = fence(small, layer_out)
    complete(sums_mix + small + sums_attn + sums_ffn)
    small = small[0].values
    total, dtotal = small[:states], small[states : 2 * states]
    norm_sums = lax.dynamic_slice_in_dim(
        small[2 * states :].reshape(4, width), index * shard_rows, shard_rows, 1
    )
    shard_attn = sums_attn[0].result()
    ups, downs = (
        [sums_ffn[0].result()[:, k * units : (k + 1) * units] for k in at] for at in ((0, 2), (1, 3))
    )
    return (
        layer_out[:, None],
        in_grad[:, None],
        sums_mix[0].result(),
        shard_attn[:, :cols],
        shard_attn[:, 2 * cols : 3 * cols],
        shard_attn[:, 3 * cols :],
        shard_attn[:, cols : 2 * cols].T,
        jnp.concatenate(ups, axis=1),
        jnp.concatenate(downs, axis=1).T,
        norm_sums[0],
        norm_sums[1],
        norm_sums[2],
        norm_sums[3],
        ssm_inject * ssm_readout * dtotal,
        ssm_readout * total,
        ssm_inject * total,
    )


def solution(mesh):
    return jax.shard_map(
        functools.partial(per_device, mesh.shape["dp"]),
        mesh=mesh,
        in_specs=(
            P(None, "dp", "tensor", None),
            P(None, "dp", None),
            P("dp", "tensor"),
            P("dp", "tensor"),
            P("dp", "tensor"),
            P("dp", "tensor"),
            P("tensor", "dp"),
            P("dp", "tensor"),
            P("tensor", "dp"),
            P("dp"),
            P("dp"),
            P("dp"),
            P("dp"),
            P(None, "tensor"),
            P(None, "tensor"),
            P(None, "tensor"),
            P(None, "dp", "tensor", None),
        ),
        out_specs=(
            P(None, "dp", "tensor", None),
            P(None, "dp", "tensor", None),
            P("dp", "tensor"),
            P("dp", "tensor"),
            P("dp", "tensor"),
            P("dp", "tensor"),
            P("tensor", "dp"),
            P("dp", "tensor"),
            P("tensor", "dp"),
            P("dp"),
            P("dp"),
            P("dp"),
            P("dp"),
            P(None, "tensor"),
            P(None, "tensor"),
            P(None, "tensor"),
        ),
        check_vma=False,
    )
```

```python
import functools
import math

import jax
import jax.numpy as jnp
from jax import lax
from jax.experimental import pallas as pl
from jax.experimental.pallas import tpu as pltpu
from jax.sharding import PartitionSpec as P

HEAD_DIM = 128
BLOCK = 512
CTX = 128
NDOCS = 8
LANES = 128
QTILE = 256
HEADS_EACH = 2
CUT = 4

norm_eps = 1e-05
masked_score = -1e30
VMEM = 56 * 1024 * 1024
BF = jnp.bfloat16
F32 = jnp.float32


def dot_plain(left_op, right_op):
    return jnp.dot(left_op, right_op, preferred_element_type=F32)


def dot_last(left_op, right_op):
    return lax.dot_general(left_op, right_op, (((1,), (1,)), ((), ())), preferred_element_type=F32)


def dot_first(left_op, right_op):
    return lax.dot_general(left_op, right_op, (((0,), (0,)), ((), ())), preferred_element_type=F32)


def params(count=1):
    return pltpu.CompilerParams(
        dimension_semantics=("arbitrary",) * count, vmem_limit_bytes=VMEM
    )


def bits_of(count):
    out = []
    bit = 1
    while bit < count:
        out.append(bit)
        bit *= 2
    return out


def groups_of(count, low_groups):
    high = bits_of(count)[2:]
    return [tuple(high[k : k + 2]) for k in range(0, len(high), 2)] + [
        tuple(b for b in g if b < count) for g in low_groups
    ]


X_FIRST = ((1,), (2,))
Y_FIRST = ((2,), (1,))
DIRECT = ((1, 2),)


def swap(values, count, mask):
    return lax.ppermute(values, "dp", [(i, i ^ mask) for i in range(count)])


def tie(*trees):
    return lax.optimization_barrier(trees)


def in_order(upper, own, got, axis):
    return jnp.where(
        upper, jnp.stack([got, own], axis=axis), jnp.stack([own, got], axis=axis)
    )


class Gather:
    def __init__(self, shard, count, index, low):
        self.values, self.count, self.index = shard, count, index
        self.shape = (count * shard.shape[0],) + shard.shape[1:]
        self.left = groups_of(count, low)
        self.present = []
        self.loose = False
        self.last = None

    def send(self):
        self.got = [swap(self.values, self.count, m) for m in masks_of(self.left[0])]

    def merge(self):
        pieces = [self.values] + list(self.got)
        if self.loose and len(self.left) == 1:
            self.last = self.left.pop()[0]
            self.values = pieces
            return
        for bit in self.left.pop(0):
            place = sum(1 for p in self.present if p > bit)
            self.present.append(bit)
            upper = (self.index // bit) % 2 == 1
            pieces = [
                in_order(upper, pieces[k], pieces[k + 1], place)
                for k in range(0, len(pieces), 2)
            ]
        self.values = pieces[0]

    def blocks(self, low):
        after = low[-1][0]
        rows = after * self.shape[0] // self.count
        return self.shape[0] // (2 * rows), rows

    def split(self, lows, loose=False):
        cols = self.values.shape[-1] // 2
        out = []
        for k, low in enumerate(lows):
            part = Gather.__new__(Gather)
            part.count, part.index, part.present = self.count, self.index, list(self.present)
            part.values = self.values[..., k * cols : (k + 1) * cols]
            part.shape = self.shape[:-1] + (cols,)
            part.left = self.left[: -len(lows)] + list(low)
            part.last = None
            part.loose = loose and self.blocks(low)[1] % 16 == 0
            out.append(part)
        return out

    def result(self):
        return self.values.reshape(self.shape)

    def parts(self):
        if self.last is None:
            return [self.result()], (1, self.shape[0]), jnp.int32(0)
        half = (self.shape[0] // 2,) + self.shape[1:]
        return (
            [v.reshape(half) for v in self.values],
            self.blocks(((self.last,),)),
            (self.index // self.last) % 2,
        )


def masks_of(group):
    return [group[0]] if len(group) == 1 else [group[0], group[1], group[0] | group[1]]


class Scatter:
    def __init__(self, full, count, index, low):
        bits = bits_of(count)
        self.values = full.reshape((2,) * len(bits) + (full.shape[0] // count,) + full.shape[1:])
        self.count, self.index = count, index
        self.present = sorted(bits, reverse=True)
        self.left = groups_of(count, low)[::-1]

    def block(self, group, mask):
        values, present = self.values, list(self.present)
        for bit in group:
            place = present.index(bit)
            digit = ((self.index ^ mask) // bit) % 2
            values = lax.dynamic_index_in_dim(values, digit, place, keepdims=False)
            present.remove(bit)
        return values

    def send(self):
        group = self.left[0]
        self.got = [swap(self.block(group, m), self.count, m) for m in masks_of(group)]

    def merge(self):
        group = self.left.pop(0)
        total = self.block(group, 0).astype(F32)
        for got in self.got:
            total = total + got.astype(F32)
        for bit in group:
            self.present.remove(bit)
        self.values = total.astype(BF) if self.present else total

    def result(self):
        return self.values


class Total:
    def __init__(self, values, count):
        self.values, self.count = values, count
        self.left = groups_of(count, DIRECT)[::-1]

    def send(self):
        self.got = [swap(self.values, self.count, m) for m in masks_of(self.left[0])]

    def merge(self):
        self.left.pop(0)
        total = self.values + self.got[0]
        if len(self.got) > 1:
            total = total + (self.got[1] + self.got[2])
        self.values = total


def send(chains, *gates):
    chains = [c for c in chains if c.left]
    held = tie([c.values for c in chains], gates)[0]
    for c, v in zip(chains, held):
        c.values = v
    for c in chains:
        c.send()


def fence(chains, *values):
    chains = [c for c in chains if c.left]
    held, values = tie([(c.values, c.got) for c in chains], values)
    for c, (v, g) in zip(chains, held):
        c.values, c.got = v, g
        c.merge()
    held, values = tie(marks(chains), values)
    for c, v in zip(chains, held):
        c.values = v
    return values if len(values) != 1 else values[0]


def step(chains, *gates):
    send(chains, *gates)
    fence(chains)


def complete(chains):
    while any(c.left for c in chains):
        step(chains)


def join_chains(chains):
    chains[0].values = jnp.concatenate([c.values for c in chains], axis=-1)
    del chains[1:]


def marks(chains):
    return [c.values for c in chains]


def pair(values):
    return lax.ppermute(values, "tensor", [(0, 1), (1, 0)])


def norm_of(values, gain_vec, bias_vec):
    centred = values - jnp.mean(values, axis=-1, keepdims=True)
    inverse = lax.rsqrt(jnp.mean(centred * centred, axis=-1, keepdims=True) + norm_eps)
    return centred * inverse * gain_vec + bias_vec


def to_steps(steps_ref, row_first, values, col_first):
    rows, cols = values.shape
    tiles = steps_ref.shape[1]
    for j in range(cols // LANES):
        steps_ref[pl.ds(row_first, rows), col_first // LANES + j, :] = values[
            :, j * LANES : (j + 1) * LANES
        ]


def run_docs(starts_ref, low, high, one_step, make_start, finish, backward, unroll=8):
    for doc in range(NDOCS):
        d = NDOCS - 1 - doc if backward else doc
        first = jnp.minimum(jnp.maximum(starts_ref[d], low), high)
        last = jnp.minimum(jnp.maximum(starts_ref[d + 1], low), high)
        length = last - first
        groups = length // unroll
        carry = make_start(d)

        def group_body(g, carry):
            base = last - 1 - g * unroll if backward else first + g * unroll
            for i in range(unroll):
                carry = one_step(base - i if backward else base + i, carry)
            return carry

        carry = lax.fori_loop(0, groups, group_body, carry)
        done = groups * unroll

        def one_body(i, carry):
            return one_step(last - 1 - done - i if backward else first + done + i, carry)

        carry = lax.fori_loop(0, length - done, one_body, carry)
        finish(d, length, carry)


def add_up(parts):
    while len(parts) > 1:
        parts = [parts[k] + parts[k + 1] for k in range(0, len(parts), 2)]
    return parts[0]


def scan_states(starts_ref, low, high, drive_ref, decay_ref, coef_ref, y_ref, start_ref, end_ref):
    states = decay_ref.shape[0]
    zero = jnp.zeros(decay_ref.shape[1:], F32)

    def one_step(t, state):
        u = drive_ref[t]
        new = [decay_ref[n] * state[n] + u for n in range(states)]
        y_ref[t - low] = add_up([coef_ref[n] * new[n] for n in range(states)])
        return tuple(new)

    def make_start(d):
        if start_ref is None:
            return (zero,) * states
        going = starts_ref[d] < low
        return tuple(jnp.where(going, start_ref[n], zero) for n in range(states))

    def finish(d, length, carry):
        if end_ref is not None:

            @pl.when(length > 0)
            def _():
                for n in range(states):
                    end_ref[n] = carry[n]

    run_docs(starts_ref, low, high, one_step, make_start, finish, False)


def from_steps(steps_ref, out_ref):
    length, tiles, _ = steps_ref.shape
    chunk = 256

    def write(i, _):
        r = pl.multiple_of(i * chunk, chunk)
        for j in range(tiles):
            out_ref[pl.ds(r, chunk), j * LANES : (j + 1) * LANES] = steps_ref[
                pl.ds(r, chunk), j, :
            ].astype(BF)
        return 0

    lax.fori_loop(0, length // chunk, write, 0)


def both_parts(own, other, joined, at, sems):
    copies = [
        pltpu.make_async_copy(own, joined.at[at(0)], sems.at[0]),
        pltpu.make_async_copy(other, joined.at[at(1)], sems.at[1]),
    ]
    for copy in copies:
        copy.start()
    return copies


def cols_at(side, cols):
    return lambda k: (
        slice(None),
        pl.ds(pl.multiple_of((side if k == 0 else 1 - side) * cols, cols), cols),
    )


def rows_at(side, rows, *lead):
    return lambda k: lead + (
        pl.ds(pl.multiple_of((side if k == 0 else 1 - side) * rows, rows), rows),
    )


def wait_all(copies):
    for copy in copies:
        copy.wait()


def ssm_forward_kernel(
    starts_ref, side_ref, mine_ref, got_ref, mix_own_ref, mix_other_ref, gain_ref, bias_ref, decay_ref, coef_ref,
    rows_ref, normed_ref, drive_ref, out_ref, end_ref, y_ref, mix_ref, sems,
):
    length, width = rows_ref.shape
    side = side_ref[0]
    copies = both_parts(
        mine_ref.at[side], got_ref.at[side], rows_ref, rows_at(side, length // 2), sems.at[0]
    ) + both_parts(
        mix_own_ref, mix_other_ref, mix_ref, cols_at(side, width // 2), sems.at[1]
    )
    wait_all(copies)
    chunk = 256

    def project(i, _):
        r = pl.multiple_of(i * chunk, chunk)
        normed = norm_of(
            rows_ref[pl.ds(r, chunk), :].astype(F32), gain_ref[...], bias_ref[...]
        ).astype(BF)
        normed_ref[pl.ds(r, chunk), :] = normed
        for c in range(0, width, 256):
            to_steps(drive_ref, r, dot_plain(normed, mix_ref[:, c : c + 256]), c)
        return 0

    lax.fori_loop(0, length // chunk, project, 0)
    scan_states(
        starts_ref, 0, length // CUT, drive_ref, decay_ref, coef_ref, y_ref, None, end_ref
    )
    from_steps(y_ref, out_ref)


def ssm_rest_kernel(
    starts_ref, side_ref, mine_ref, got_ref, drive_ref, decay_ref, coef_ref, start_ref, first_ref,
    out_ref, cot_ref, y_ref, sems,
):
    length = drive_ref.shape[0]
    half = length // 2
    cut = length // CUT
    side = side_ref[0]
    copies = both_parts(
        mine_ref.at[side], got_ref.at[side], cot_ref, rows_at(side, half, 0), sems.at[0]
    ) + both_parts(
        mine_ref.at[1 - side], got_ref.at[1 - side], cot_ref, rows_at(side, half, 1), sems.at[1]
    )
    scan_states(
        starts_ref, cut, length, drive_ref, decay_ref, coef_ref, y_ref, start_ref, None
    )
    out_ref[:cut, :] = first_ref[...]
    from_steps(y_ref, out_ref.at[cut:])
    wait_all(copies)


SMALL = pl.BlockSpec(memory_space=pltpu.SMEM)
WHOLE = pl.BlockSpec(memory_space=pltpu.VMEM)
ANYWHERE = pl.BlockSpec(memory_space=pl.ANY)
COPIES = pltpu.SemaphoreType.DMA((2, 2))


def ssm_forward(starts, side, mine, got, mix_own, mix_other, gain_vec, bias_vec, decay, coef):
    length, width = 2 * mine.shape[1], mine.shape[2]
    tiles = width // LANES
    return pl.pallas_call(
        ssm_forward_kernel,
        out_shape=(
            jax.ShapeDtypeStruct((length, width), BF),
            jax.ShapeDtypeStruct((length, width), BF),
            jax.ShapeDtypeStruct((length, tiles, LANES), F32),
            jax.ShapeDtypeStruct((length // CUT, width), BF),
            jax.ShapeDtypeStruct(decay.shape, F32),
        ),
        in_specs=[SMALL] * 2 + [ANYWHERE] * 4 + [WHOLE] * 4,
        out_specs=(WHOLE,) * 5,
        scratch_shapes=[
            pltpu.VMEM((length // CUT, tiles, LANES), F32),
            pltpu.VMEM((width, width), BF),
            COPIES,
        ],
        compiler_params=pltpu.CompilerParams(vmem_limit_bytes=VMEM),
        cost_estimate=pl.CostEstimate(
            flops=12 * length * width * width,
            bytes_accessed=16 * length * width,
            transcendentals=0,
        ),
        name="ssm_forward",
    )(starts, side, mine, got, mix_own, mix_other, gain_vec, bias_vec, decay, coef)


def ssm_rest(starts, side, mine, got, drive, decay, coef, start, first):
    length, tiles, _ = drive.shape
    width = tiles * LANES
    return pl.pallas_call(
        ssm_rest_kernel,
        out_shape=(
            jax.ShapeDtypeStruct((length, width), BF),
            jax.ShapeDtypeStruct((2, length, width), BF),
        ),
        in_specs=[SMALL] * 2 + [ANYWHERE] * 2 + [WHOLE] * 5,
        out_specs=(WHOLE, WHOLE),
        scratch_shapes=[pltpu.VMEM((length - length // CUT, tiles, LANES), F32), COPIES],
        compiler_params=pltpu.CompilerParams(vmem_limit_bytes=VMEM),
        cost_estimate=pl.CostEstimate(
            flops=10 * length * width * width,
            bytes_accessed=16 * length * width,
            transcendentals=0,
        ),
        name="ssm_rest",
    )(starts, side, mine, got, drive, decay, coef, start, first)


def project_kernel(
    side_ref, normed_ref, ssm_ref, left_own_ref, left_other_ref, right_own_ref, right_other_ref,
    query_ref, key_ref, value_ref, weights_ref, sems,
):
    width = normed_ref.shape[1]
    cols = width // 2
    at = cols_at(side_ref[0], cols)
    sources = (
        (left_own_ref, left_other_ref, 0),
        (left_own_ref, left_other_ref, cols),
        (right_own_ref, right_other_ref, 0),
    )
    copies = [
        both_parts(
            own.at[:, c : c + cols], other.at[:, c : c + cols], weights_ref.at[k], at, sems.at[k]
        )
        for k, (own, other, c) in enumerate(sources)
    ]
    for k, (rows_ref, out_ref) in enumerate(
        ((normed_ref, query_ref), (ssm_ref, key_ref), (ssm_ref, value_ref))
    ):
        wait_all(copies[k])
        for c in range(0, width, cols):
            out_ref[:, c : c + cols] = dot_plain(
                rows_ref[...], weights_ref[k, :, c : c + cols]
            ).astype(BF)


def project(side, normed, ssm_out, left, right):
    length, width = normed.shape
    return pl.pallas_call(
        project_kernel,
        out_shape=(jax.ShapeDtypeStruct((length, width), BF),) * 3,
        in_specs=[SMALL] + [WHOLE] * 2 + [ANYWHERE] * 4,
        out_specs=(WHOLE,) * 3,
        scratch_shapes=[pltpu.VMEM((3, width, width), BF), pltpu.SemaphoreType.DMA((3, 2))],
        compiler_params=pltpu.CompilerParams(vmem_limit_bytes=VMEM),
        cost_estimate=pl.CostEstimate(
            flops=6 * length * width * width, bytes_accessed=16 * length * width, transcendentals=0
        ),
        name="project",
    )(side, normed, ssm_out, *left, *right)


def adjoint_states(starts_ref, low, drive_ref, g_ref, decay_ref, coef_ref, gm_ref, sum_ref, dsum_ref, given_ref):
    length = g_ref.shape[0]
    part = sum_ref.shape[0]
    zero = jnp.zeros(decay_ref.shape[1:], F32)

    def one_step(t, carry):
        mu, rho, total, dtotal = carry
        u = drive_ref[t]
        g = g_ref[t]
        new_mu, new_rho, new_total, new_dtotal, parts = [], [], [], [], []
        for n in range(part):
            a = decay_ref[low + n]
            r = a * rho[n] + mu[n]
            m = a * mu[n] + g
            new_mu.append(m)
            new_rho.append(r)
            new_total.append(total[n] + u * m)
            new_dtotal.append(dtotal[n] + u * r)
            parts.append(coef_ref[low + n] * m)
        gm = add_up(parts)
        gm_ref[t] = gm if given_ref is None else gm + given_ref[t]
        return tuple(new_mu), tuple(new_rho), tuple(new_total), tuple(new_dtotal)

    for n in range(part):
        sum_ref[n] = zero
        dsum_ref[n] = zero

    def make_start(d):
        zeros = (zero,) * part
        return zeros, zeros, zeros, zeros

    def finish(d, count, carry):
        for n in range(part):
            sum_ref[n] = sum_ref[n] + carry[2][n]
            dsum_ref[n] = dsum_ref[n] + carry[3][n]

    run_docs(starts_ref, 0, length, one_step, make_start, finish, True)


def ssm_backward_kernel(
    starts_ref, side_ref, gkey_ref, gvalue_ref, left_own_ref, left_other_ref, right_own_ref, right_other_ref,
    drive_ref, decay_ref, coef_ref, g_ref, gm_ref, sum_ref, dsum_ref, wkey_ref, wvalue_ref, sems,
):
    length, width = gkey_ref.shape
    cols = width // 2
    at = cols_at(side_ref[0], cols)
    copies = both_parts(
        left_own_ref.at[:, cols:], left_other_ref.at[:, cols:], wkey_ref, at, sems.at[0]
    ) + both_parts(
        right_own_ref.at[:, :cols], right_other_ref.at[:, :cols], wvalue_ref, at, sems.at[1]
    )
    wait_all(copies)
    chunk = 256

    def project(i, _):
        r = pl.multiple_of(i * chunk, chunk)
        gkey = gkey_ref[pl.ds(r, chunk), :]
        gvalue = gvalue_ref[pl.ds(r, chunk), :]
        for c in range(0, width, 256):
            to_steps(
                g_ref,
                r,
                dot_last(gkey, wkey_ref[c : c + 256, :])
                + dot_last(gvalue, wvalue_ref[c : c + 256, :]),
                c,
            )
        return 0

    lax.fori_loop(0, length // chunk, project, 0)
    adjoint_states(
        starts_ref, 0, drive_ref, g_ref, decay_ref, coef_ref, gm_ref, sum_ref, dsum_ref, None
    )


def ssm_backward_rest_kernel(
    starts_ref, g_ref, given_ref, drive_ref, decay_ref, coef_ref,
    gmixed_ref, sum_ref, dsum_ref, gm_ref,
):
    adjoint_states(
        starts_ref, decay_ref.shape[0] // 2, drive_ref, g_ref, decay_ref, coef_ref, gm_ref,
        sum_ref, dsum_ref, given_ref,
    )
    from_steps(gm_ref, gmixed_ref)


def ssm_backward(starts, side, gkey, gvalue, left, right, drive, decay, coef):
    length, width = gkey.shape
    tiles = width // LANES
    vm = pl.BlockSpec(memory_space=pltpu.VMEM)
    half = (decay.shape[0] // 2,) + decay.shape[1:]
    return pl.pallas_call(
        ssm_backward_kernel,
        out_shape=(
            jax.ShapeDtypeStruct((length, tiles, LANES), F32),
            jax.ShapeDtypeStruct((length, tiles, LANES), F32),
            jax.ShapeDtypeStruct(half, F32),
            jax.ShapeDtypeStruct(half, F32),
        ),
        in_specs=[SMALL] * 2 + [vm] * 2 + [ANYWHERE] * 4 + [vm] * 3,
        out_specs=(vm,) * 4,
        scratch_shapes=[pltpu.VMEM((width, width), BF)] * 2 + [COPIES],
        compiler_params=pltpu.CompilerParams(vmem_limit_bytes=VMEM),
        cost_estimate=pl.CostEstimate(
            flops=20 * length * width * width,
            bytes_accessed=20 * length * width,
            transcendentals=0,
        ),
        name="ssm_backward",
    )(starts, side, gkey, gvalue, *left, *right, drive, decay, coef)


def ssm_backward_rest(starts, g, given, drive, decay, coef):
    length, tiles, _ = drive.shape
    width = tiles * LANES
    vm = pl.BlockSpec(memory_space=pltpu.VMEM)
    half = (decay.shape[0] // 2,) + decay.shape[1:]
    return pl.pallas_call(
        ssm_backward_rest_kernel,
        out_shape=(
            jax.ShapeDtypeStruct((length, width), BF),
            jax.ShapeDtypeStruct(half, F32),
            jax.ShapeDtypeStruct(half, F32),
        ),
        in_specs=[pl.BlockSpec(memory_space=pltpu.SMEM)] + [vm] * 5,
        out_specs=(vm,) * 3,
        scratch_shapes=[pltpu.VMEM((length, tiles, LANES), F32)],
        compiler_params=pltpu.CompilerParams(vmem_limit_bytes=VMEM),
        cost_estimate=pl.CostEstimate(
            flops=20 * length * width * width,
            bytes_accessed=20 * length * width,
            transcendentals=0,
        ),
        name="ssm_backward_rest",
    )(starts, g, given, drive, decay, coef)


def attention_tiles(length):
    tiles = []
    for first in range(0, length, QTILE):
        block_first = first // BLOCK * BLOCK
        key_first = max(0, block_first - CTX)
        tiles.append((first, key_first, first + QTILE - key_first))
    return tiles


def fill_bias(seg_col_ref, seg_row_ref, bias_ref, tiles):
    at = 0
    for first, key_first, count in tiles:
        same = seg_col_ref[first : first + QTILE, :] == seg_row_ref[:, key_first : key_first + count]
        query_pos = lax.broadcasted_iota(jnp.int32, (QTILE, count), 0) + first
        key_pos = lax.broadcasted_iota(jnp.int32, (QTILE, count), 1) + key_first
        bias_ref[:, at : at + count] = jnp.where(
            same & (key_pos <= query_pos), 0.0, masked_score
        ).astype(F32)
        at += count


EXP_SCALE = HEAD_DIM ** (-0.5) * math.log2(math.e)


def attention_jobs(length):
    jobs = []
    for h in range(HEADS_EACH):
        at = 0
        for first, key_first, count in attention_tiles(length):
            jobs.append(
                (
                    h,
                    slice(h * HEAD_DIM, (h + 1) * HEAD_DIM),
                    slice(first, first + QTILE),
                    slice(key_first, key_first + count),
                    slice(at, at + count),
                )
            )
            at += count
    return jobs


def attention_forward_kernel(
    seg_col_ref, seg_row_ref, query_ref, key_ref, value_ref, out_ref, lse_ref, bias_ref, value_one_ref
):
    length = query_ref.shape[0]

    @pl.when(pl.program_id(0) == 0)
    def _():
        fill_bias(seg_col_ref, seg_row_ref, bias_ref, attention_tiles(length))
        for h in range(HEADS_EACH):
            value_one_ref[h, :, HEAD_DIM:] = jnp.ones((length, HEAD_DIM), BF)

    for h in range(HEADS_EACH):
        value_one_ref[h, :, :HEAD_DIM] = value_ref[:, h * HEAD_DIM : (h + 1) * HEAD_DIM]
    jobs = attention_jobs(length)

    def scores_of(job):
        _, lanes, rows, keys, _ = job
        return dot_last(query_ref[rows, lanes], key_ref[keys, lanes])

    ahead = scores_of(jobs[0])
    for k, (h, lanes, rows, keys, mask) in enumerate(jobs):
        scores = ahead
        if k + 1 < len(jobs):
            ahead = scores_of(jobs[k + 1])
        scores = scores * EXP_SCALE + bias_ref[:, mask]
        top = jnp.max(scores, axis=-1, keepdims=True)
        raised = jnp.exp2(scores - top).astype(BF)
        both = dot_plain(raised, value_one_ref[h, keys, :])
        total = both[:, HEAD_DIM:]
        out_ref[rows, lanes] = (both[:, :HEAD_DIM] / total).astype(BF)
        lse_ref[h, rows, :] = top + jnp.log2(total[:, :1])


def attention_forward(seg_col, seg_row, query, key, value):
    length, width = query.shape
    heads = width // HEAD_DIM
    tiles = attention_tiles(length)
    cols = sum(t[2] for t in tiles)
    head = pl.BlockSpec((length, HEADS_EACH * HEAD_DIM), lambda h: (0, h))
    whole = lambda shape: pl.BlockSpec(shape, lambda h: (0, 0))
    return pl.pallas_call(
        attention_forward_kernel,
        grid=(heads // HEADS_EACH,),
        out_shape=(
            jax.ShapeDtypeStruct((length, width), BF),
            jax.ShapeDtypeStruct((heads, length, 1), F32),
        ),
        in_specs=[whole((length, 1)), whole((1, length)), head, head, head],
        out_specs=(head, pl.BlockSpec((HEADS_EACH, length, 1), lambda h: (h, 0, 0))),
        scratch_shapes=[
            pltpu.VMEM((QTILE, cols), F32),
            pltpu.VMEM((HEADS_EACH, length, 2 * HEAD_DIM), BF),
        ],
        compiler_params=params(),
        cost_estimate=pl.CostEstimate(
            flops=4 * QTILE * cols * width,
            bytes_accessed=8 * length * width,
            transcendentals=QTILE * cols * heads,
        ),
        name="attention_forward",
    )(seg_col, seg_row, query, key, value)


def attention_backward_kernel(
    seg_col_ref, seg_row_ref, query_ref, key_ref, value_ref, lse_ref, gout_ref,
    gquery_ref, gkey_ref, gvalue_ref, bias_ref, gk_ref, gv_ref,
):
    length = query_ref.shape[0]
    scale = HEAD_DIM ** (-0.5)

    @pl.when(pl.program_id(0) == 0)
    def _():
        fill_bias(seg_col_ref, seg_row_ref, bias_ref, attention_tiles(length))

    gk_ref[...] = jnp.zeros_like(gk_ref)
    gv_ref[...] = jnp.zeros_like(gv_ref)
    jobs = attention_jobs(length)

    def scores_of(job):
        _, lanes, rows, keys, _ = job
        return (
            dot_last(query_ref[rows, lanes], key_ref[keys, lanes]),
            dot_last(gout_ref[rows, lanes], value_ref[keys, lanes]),
        )

    ahead = scores_of(jobs[0])
    for k, (h, lanes, rows, keys, mask) in enumerate(jobs):
        scores, gprobs = ahead
        if k + 1 < len(jobs):
            ahead = scores_of(jobs[k + 1])
        gout = gout_ref[rows, lanes]
        probs = jnp.exp2(scores * EXP_SCALE + bias_ref[:, mask] - lse_ref[h, rows, :])
        gv_ref[keys, lanes] = gv_ref[keys, lanes] + dot_first(probs.astype(BF), gout)
        inner = jnp.sum(probs * gprobs, axis=-1, keepdims=True)
        gscores = (probs * (gprobs - inner)).astype(BF)
        gquery_ref[rows, lanes] = (dot_plain(gscores, key_ref[keys, lanes]) * scale).astype(BF)
        gk_ref[keys, lanes] = gk_ref[keys, lanes] + dot_first(gscores, query_ref[rows, lanes])
    gkey_ref[...] = (gk_ref[...] * scale).astype(BF)
    gvalue_ref[...] = gv_ref[...].astype(BF)


def attention_backward(seg_col, seg_row, query, key, value, lse, gout):
    length, width = query.shape
    heads = width // HEAD_DIM
    tiles = attention_tiles(length)
    cols = sum(t[2] for t in tiles)
    head = pl.BlockSpec((length, HEADS_EACH * HEAD_DIM), lambda h: (0, h))
    whole = lambda shape: pl.BlockSpec(shape, lambda h: (0, 0))
    return pl.pallas_call(
        attention_backward_kernel,
        grid=(heads // HEADS_EACH,),
        out_shape=(jax.ShapeDtypeStruct((length, width), BF),) * 3,
        in_specs=[whole((length, 1)), whole((1, length)), head, head, head]
        + [pl.BlockSpec((HEADS_EACH, length, 1), lambda h: (h, 0, 0)), head],
        out_specs=(head,) * 3,
        scratch_shapes=[
            pltpu.VMEM((QTILE, cols), F32),
            pltpu.VMEM((length, HEADS_EACH * HEAD_DIM), F32),
            pltpu.VMEM((length, HEADS_EACH * HEAD_DIM), F32),
        ],
        compiler_params=params(),
        cost_estimate=pl.CostEstimate(
            flops=10 * QTILE * cols * width,
            bytes_accessed=14 * length * width,
            transcendentals=QTILE * cols * heads,
        ),
        name="attention_backward",
    )(seg_col, seg_row, query, key, value, lse, gout)


def norm_backward(grad, values, gain_vec):
    centred = values - jnp.mean(values, axis=-1, keepdims=True)
    inverse = lax.rsqrt(jnp.mean(centred * centred, axis=-1, keepdims=True) + norm_eps)
    xhat = centred * inverse
    dxhat = grad * gain_vec
    back = (
        dxhat
        - jnp.mean(dxhat, axis=-1, keepdims=True)
        - xhat * jnp.mean(dxhat * xhat, axis=-1, keepdims=True)
    ) * inverse
    return back, jnp.sum(grad * xhat, axis=0, keepdims=True), jnp.sum(grad, axis=0, keepdims=True)


def gelu_parts(values):
    below = 0.5 + 0.5 * lax.erf(values * (2.0**-0.5))
    bell = jnp.exp2((-0.5 * math.log2(math.e)) * (values * values))
    return values * below, below + values * (bell * ((2.0 * math.pi) ** -0.5))


FTILE = 512


def feed_forward_kernel(part, blocks, place_ref, own_ref, other_ref, cot_ref, *refs):
    pieces, refs = refs[: sum(b[0] for b in blocks)], refs[sum(b[0] for b in blocks) :]
    ins, refs = refs[: 4 * part], refs[4 * part :]
    outs, grads, refs = refs[:4], refs[4:6], refs[6:]
    normed_ref, cots_ref, up_ref, down_ref, hidden_ref, gpre_ref, sums_ref, total_ref = refs[:8]
    row_sems, weight_sems, out_sems, grad_sems = refs[8:12]
    length, width = own_ref.shape
    units = up_ref.shape[1]
    tile = FTILE
    per = length // tile
    count = 2 * per

    def tile_of(i):
        return pl.ds(pl.multiple_of(i * tile, tile), tile)

    weights = []
    for k, (ref, (number, (many, rows))) in enumerate(zip((up_ref, down_ref), blocks)):
        for p in range(number):
            source = pieces[k * blocks[0][0] + p]
            place = place_ref[k] if p == 0 else 1 - place_ref[k]
            for h in range(many):
                at = (2 * h + place) * rows if number == 2 else 0
                pltpu.make_async_copy(
                    source.at[pl.ds(h * rows, rows)],
                    ref.at[pl.ds(pl.multiple_of(at, 16), rows)],
                    weight_sems.at[k],
                ).start()
        weights.append(pltpu.make_async_copy(ref, ref, weight_sems.at[k]))
    for i in range(count):
        rows = tile_of(i % per)
        source = (own_ref, other_ref)[i // per]
        pltpu.make_async_copy(source.at[rows], normed_ref.at[tile_of(i)], row_sems.at[0, i]).start()
        pltpu.make_async_copy(
            cot_ref.at[i // per, rows], cots_ref.at[tile_of(i)], row_sems.at[1, i]
        ).start()
    if part:
        earlier = [
            pltpu.make_async_copy(ins[k], total_ref.at[k], out_sems.at[k, count])
            for k in range(4)
        ]
        for copy in earlier:
            copy.start()
    wait_all(weights)

    def one(i, _):
        rows = tile_of(i)
        for k, ref in enumerate((normed_ref, cots_ref)):
            pltpu.make_async_copy(ref.at[rows], ref.at[rows], row_sems.at[k, i]).wait()
        for n in range(0, units, tile):
            pre = dot_plain(normed_ref[rows, :], up_ref[:, n : n + tile])
            ghidden = dot_plain(cots_ref[rows, :], down_ref[:, n : n + tile])
            hidden, slope = gelu_parts(pre)
            hidden_ref[rows, n : n + tile] = hidden.astype(BF)
            gpre_ref[rows, n : n + tile] = (ghidden * slope).astype(BF)
        return 0

    lax.fori_loop(0, count, one, 0)

    grad_copies = []
    for k, (first_ref, held_ref) in enumerate(((normed_ref, gpre_ref), (cots_ref, hidden_ref))):

        def three(i, _, k=k, first_ref=first_ref, held_ref=held_ref):
            cols = tile_of(i)
            sums_ref[k, cols, :] = dot_first(first_ref[:, cols], held_ref[...]).astype(BF)
            return 0

        lax.fori_loop(0, width // tile, three, 0)
        copy = pltpu.make_async_copy(
            sums_ref.at[k], grads[k], grad_sems.at[k]
        )
        copy.start()
        grad_copies.append(copy)

    if part:
        wait_all(earlier)
    out_copies = []
    for i in range(count):
        s, rows = i // per, slice(i % per * tile, (i % per + 1) * tile)
        held = slice(i * tile, (i + 1) * tile)
        for k, (held_ref, weight_ref) in enumerate(((hidden_ref, down_ref), (gpre_ref, up_ref))):
            total = dot_last(held_ref[held, :], weight_ref[...])
            if part:
                total = total + total_ref[2 * k + s, rows, :].astype(F32)
            total_ref[2 * k + s, rows, :] = total.astype(BF)
            copy = pltpu.make_async_copy(
                total_ref.at[2 * k + s, rows], outs[2 * k + s].at[rows], out_sems.at[k, i]
            )
            copy.start()
            out_copies.append(copy)
    wait_all(grad_copies + out_copies)


def feed_forward(part, own, other, cot, up, down, earlier):
    length, width = own.shape
    pieces, blocks, places = zip(*(chain.parts() for chain in (up, down)))
    blocks = tuple((len(p), b) for p, b in zip(pieces, blocks))
    pieces = [p for each in pieces for p in each]
    units = pieces[0].shape[1]
    count = 2 * length // FTILE
    dma = pltpu.SemaphoreType.DMA
    return pl.pallas_call(
        functools.partial(feed_forward_kernel, part, blocks),
        out_shape=(jax.ShapeDtypeStruct((length, width), BF),) * 4
        + (jax.ShapeDtypeStruct((width, units), BF),) * 2,
        in_specs=[SMALL] + [ANYWHERE] * (3 + len(pieces) + 4 * part),
        out_specs=(ANYWHERE,) * 6,
        scratch_shapes=[pltpu.VMEM((2 * length, width), BF)] * 2
        + [pltpu.VMEM((width, units), BF)] * 2
        + [pltpu.VMEM((2 * length, units), BF)] * 2
        + [pltpu.VMEM((2, width, units), BF), pltpu.VMEM((4, length, width), BF)]
        + [dma((2, count)), dma((2,)), dma((4, count + 1)), dma((2,))],
        compiler_params=pltpu.CompilerParams(vmem_limit_bytes=VMEM),
        cost_estimate=pl.CostEstimate(
            flops=28 * length * width * units,
            bytes_accessed=48 * length * width,
            transcendentals=4 * length * units,
        ),
        name="feed_forward",
    )(jnp.stack(places), own, other, cot, *pieces, *earlier)


def at_first(joins, sems, side):
    @pl.when(pl.program_id(0) == 0)
    def _():
        copies = []
        for k, (own, other, joined) in enumerate(joins):
            copies += both_parts(own, other, joined, cols_at(side, joined.shape[1] // 2), sems.at[k])
        wait_all(copies)


ROWS = 256


def row_spec(width, lead=None):
    if lead is None:
        return pl.BlockSpec((ROWS, width), lambda i: (i, 0))
    return pl.BlockSpec((None, ROWS, width), lambda i: (lead, i, 0))


def fixed(*shape):
    return pl.BlockSpec(shape, lambda i: (0,) * len(shape))


def middle_kernel(
    side_ref, attended_ref, own_ref, other_ref, rows_ref, gain_ref, bias_ref, middle_ref, normed_ref, out_ref, sems
):
    cols = out_ref.shape[1] // 2
    at_first([(own_ref.at[:, cols:], other_ref.at[:, cols:], out_ref)], sems, side_ref[0])
    middle = rows_ref[...].astype(F32) + dot_last(attended_ref[...], out_ref[...])
    middle_ref[...] = middle
    normed_ref[...] = norm_of(middle, gain_ref[...], bias_ref[...]).astype(BF)


def middle_of(side, attended, right, rows, gain_vec, bias_vec):
    length, width = rows.shape
    row = row_spec(width)
    return pl.pallas_call(
        middle_kernel,
        grid=(length // ROWS,),
        out_shape=(
            jax.ShapeDtypeStruct((length, width), F32),
            jax.ShapeDtypeStruct((length, width), BF),
        ),
        in_specs=[SMALL, row, ANYWHERE, ANYWHERE, row, fixed(1, width), fixed(1, width)],
        out_specs=(row, row),
        scratch_shapes=[pltpu.VMEM((width, width), BF), COPIES],
        compiler_params=params(),
        cost_estimate=pl.CostEstimate(
            flops=2 * length * width * width, bytes_accessed=12 * length * width, transcendentals=0
        ),
        name="middle",
    )(side, attended, *right, rows, gain_vec, bias_vec)


def norm_two_kernel(
    side_ref, mine_ref, theirs_ref, middle_ref, cot_ref, gain_ref, own_ref, other_ref,
    gmiddle_ref, gbranch_ref, gattended_ref, sums_ref, out_ref, sems,
):
    cols = out_ref.shape[1] // 2
    at_first([(own_ref.at[:, cols:], other_ref.at[:, cols:], out_ref)], sems, side_ref[0])
    grad = mine_ref[...].astype(F32) + theirs_ref[...].astype(F32)
    back, gain_sum, bias_sum = norm_backward(grad, middle_ref[...], gain_ref[...])
    gmiddle = cot_ref[...].astype(F32) + back
    gmiddle_ref[...] = gmiddle
    gbranch = gmiddle.astype(BF)
    gbranch_ref[...] = gbranch
    gattended_ref[...] = dot_plain(gbranch, out_ref[...]).astype(BF)
    add_sums(sums_ref, gain_sum, bias_sum)


def add_sums(sums_ref, gain_sum, bias_sum):
    @pl.when(pl.program_id(0) == 0)
    def _():
        sums_ref[...] = jnp.zeros_like(sums_ref)

    sums_ref[0:1, :] = sums_ref[0:1, :] + gain_sum
    sums_ref[1:2, :] = sums_ref[1:2, :] + bias_sum


def norm_two_back(side, mine, theirs, middle, cot, gain_vec, right):
    length, width = middle.shape
    row = row_spec(width)
    return pl.pallas_call(
        norm_two_kernel,
        grid=(length // ROWS,),
        out_shape=(
            jax.ShapeDtypeStruct((length, width), F32),
            jax.ShapeDtypeStruct((length, width), BF),
            jax.ShapeDtypeStruct((length, width), BF),
            jax.ShapeDtypeStruct((2, width), F32),
        ),
        in_specs=[SMALL, row, row, row, row_spec(width, 0), fixed(1, width), ANYWHERE, ANYWHERE],
        out_specs=(row, row, row, fixed(2, width)),
        scratch_shapes=[pltpu.VMEM((width, width), BF), COPIES],
        compiler_params=params(),
        cost_estimate=pl.CostEstimate(
            flops=2 * length * width * width, bytes_accessed=24 * length * width, transcendentals=0
        ),
        name="norm_two_back",
    )(side, mine, theirs, middle, cot, gain_vec, *right)


def norm_one_kernel(
    side_ref, gquery_ref, gmixed_ref, rows_ref, gmiddle_ref, gain_ref,
    left_own_ref, left_other_ref, mix_own_ref, mix_other_ref, grad_ref, sums_ref, query_ref, mix_ref, sems,
):
    cols = query_ref.shape[1] // 2
    at_first(
        [
            (left_own_ref.at[:, :cols], left_other_ref.at[:, :cols], query_ref),
            (mix_own_ref, mix_other_ref, mix_ref),
        ],
        sems,
        side_ref[0],
    )
    grad = dot_last(gquery_ref[...], query_ref[...]) + dot_last(gmixed_ref[...], mix_ref[...])
    back, gain_sum, bias_sum = norm_backward(grad, rows_ref[...].astype(F32), gain_ref[...])
    grad_ref[...] = gmiddle_ref[...] + back
    add_sums(sums_ref, gain_sum, bias_sum)


def norm_one_back(side, gquery, gmixed, rows, gmiddle, gain_vec, left, mix, for_partner):
    length, width = rows.shape
    half = length // 2
    steps = half // ROWS

    def place(side):
        return 1 - side[0] if for_partner else side[0]

    row = pl.BlockSpec((ROWS, width), lambda i, side: (place(side) * steps + i, 0))
    whole = lambda *shape: pl.BlockSpec(shape, lambda i, side: (0,) * len(shape))
    if for_partner:
        out = jax.ShapeDtypeStruct((half, width), F32)
        out_spec = pl.BlockSpec((ROWS, width), lambda i, side: (i, 0))
    else:
        out = jax.ShapeDtypeStruct((2, half, width), F32)
        out_spec = pl.BlockSpec((None, ROWS, width), lambda i, side: (side[0], i, 0))
    return pl.pallas_call(
        norm_one_kernel,
        grid_spec=pltpu.PrefetchScalarGridSpec(
            num_scalar_prefetch=1,
            grid=(steps,),
            in_specs=[row] * 4 + [whole(1, width)] + [ANYWHERE] * 4,
            out_specs=(out_spec, whole(2, width)),
            scratch_shapes=[pltpu.VMEM((width, width), BF)] * 2 + [COPIES],
        ),
        out_shape=(out, jax.ShapeDtypeStruct((2, width), F32)),
        compiler_params=params(),
        cost_estimate=pl.CostEstimate(
            flops=4 * half * width * width, bytes_accessed=20 * half * width, transcendentals=0
        ),
        name="norm_one_back",
    )(side, gquery, gmixed, rows, gmiddle, gain_vec, *left, *mix)


def put_kernel(side_ref, got_ref, given_ref, out_ref):
    out_ref[...] = got_ref[...]


def put(side, got, given):
    half, width = got.shape
    return pl.pallas_call(
        put_kernel,
        grid_spec=pltpu.PrefetchScalarGridSpec(
            num_scalar_prefetch=1,
            grid=(half // ROWS,),
            in_specs=[pl.BlockSpec((ROWS, width), lambda i, side: (i, 0)), ANYWHERE],
            out_specs=pl.BlockSpec((None, ROWS, width), lambda i, side: (1 - side[0], i, 0)),
        ),
        out_shape=jax.ShapeDtypeStruct(given.shape, given.dtype),
        input_output_aliases={2: 0},
        compiler_params=params(),
        name="put",
    )(side, got, given)


def layer_out_kernel(side_ref, middle_ref, own_ref, other_ref, sum_ref, theirs_ref, out_ref):
    side = side_ref[0]
    out_ref[side] = (
        middle_ref[...] + own_ref[...].astype(F32) + theirs_ref[...].astype(F32)
    )
    out_ref[1 - side] = sum_ref[...] + other_ref[...].astype(F32)


def layer_out_of(side, middle, own, other, partner_sum, partner_other):
    length, width = middle.shape
    half = length // 2
    steps = half // ROWS
    mine = pl.BlockSpec((ROWS, width), lambda i, side: (side[0] * steps + i, 0))
    row = pl.BlockSpec((ROWS, width), lambda i, side: (i, 0))
    return pl.pallas_call(
        layer_out_kernel,
        grid_spec=pltpu.PrefetchScalarGridSpec(
            num_scalar_prefetch=1,
            grid=(steps,),
            in_specs=[mine] * 3 + [row] * 2,
            out_specs=pl.BlockSpec((2, ROWS, width), lambda i, side: (0, i, 0)),
        ),
        out_shape=jax.ShapeDtypeStruct((2, half, width), F32),
        compiler_params=params(),
        cost_estimate=pl.CostEstimate(
            flops=4 * half * width, bytes_accessed=24 * half * width, transcendentals=0
        ),
        name="layer_out",
    )(side, middle, own, other, partner_sum, partner_other)


def weight_grads_kernel(count, side_ref, *refs):
    ins, outs, refs = refs[:-6], refs[-6:-4], refs[-4:]
    held_ref, sums_ref, in_sems, out_sems = refs
    lefts = len(ins) - count
    width = held_ref.shape[2]
    cols = width // 2
    side = side_ref[0]
    order = []
    for k in range(count):
        order += [k % lefts, lefts + k]
    order = list(dict.fromkeys(order))
    loads = {
        j: pltpu.make_async_copy(ins[j], held_ref.at[j], in_sems.at[j]) for j in order
    }
    for j in order:
        loads[j].start()
    stores = []
    for k in range(count):
        for j in (k % lefts, lefts + k):
            if j in loads:
                loads.pop(j).wait()
        for which, at in enumerate((1 - side, side)):
            part = held_ref[lefts + k, :, pl.ds(pl.multiple_of(at * cols, cols), cols)]
            sums_ref[which, k] = dot_first(held_ref[k % lefts], part).astype(BF)
            copy = pltpu.make_async_copy(
                sums_ref.at[which, k],
                outs[which].at[:, k * cols : (k + 1) * cols],
                out_sems.at[which, k],
            )
            copy.start()
            stores.append(copy)
    wait_all(stores)


def weight_grads(side, lefts, rights):
    count = len(rights)
    length, width = lefts[0].shape
    cols = width // 2
    many = len(lefts) + count
    return pl.pallas_call(
        functools.partial(weight_grads_kernel, count),
        out_shape=(jax.ShapeDtypeStruct((width, count * cols), BF),) * 2,
        in_specs=[SMALL] + [ANYWHERE] * many,
        out_specs=(ANYWHERE,) * 2,
        scratch_shapes=[
            pltpu.VMEM((many, length, width), BF),
            pltpu.VMEM((2, count, width, cols), BF),
            pltpu.SemaphoreType.DMA((many,)),
            pltpu.SemaphoreType.DMA((2, count)),
        ],
        compiler_params=pltpu.CompilerParams(vmem_limit_bytes=VMEM),
        cost_estimate=pl.CostEstimate(
            flops=2 * count * length * width * width,
            bytes_accessed=6 * count * length * width,
            transcendentals=0,
        ),
        name="weight_grads",
    )(side, *lefts, *rights)


def per_device(
    count,
    layer_in,
    segment_ids,
    w_mix_in,
    w_query,
    w_key,
    w_value,
    w_attn_out,
    w_up,
    w_down,
    norm1_gain,
    norm1_bias,
    norm2_gain,
    norm2_bias,
    ssm_decay,
    ssm_inject,
    ssm_readout,
    out_grad,
):
    index = lax.axis_index("dp")
    side = lax.axis_index("tensor")
    at_side = jnp.reshape(side, (1,))
    half = layer_in.shape[2]
    width = layer_in.shape[3]
    tiles = width // LANES
    states = ssm_decay.shape[0]
    cols = w_query.shape[1]
    parts = 2
    units = w_up.shape[1] // parts
    shard_rows = w_mix_in.shape[0]

    norms = jnp.concatenate([norm1_gain, norm1_bias, norm2_gain, norm2_bias])
    norms = jnp.pad(norms[None], ((0, 7), (0, cols - norms.shape[0])))
    mix = [Gather(jnp.concatenate([w_mix_in, norms], axis=0), count, index, DIRECT)]
    send(mix)
    mine_in, got_in = layer_in[:, 0], pair(layer_in[:, 0])
    coefs = jnp.stack([ssm_decay, ssm_inject, ssm_readout])
    coefs_got = pair(coefs)
    fence(mix)
    attn = [
        Gather(
            jnp.concatenate([w_query, w_key, w_value, w_attn_out.T], axis=1), count, index, X_FIRST
        )
    ]
    turned_down = w_down.T
    ffn = [
        [
            Gather(
                jnp.concatenate(
                    [
                        w_up[:, i * units : (i + 1) * units],
                        turned_down[:, i * units : (i + 1) * units],
                    ],
                    axis=1,
                ),
                count,
                index,
                X_FIRST,
            )
        ]
        for i in range(parts)
    ]
    both_ways = (X_FIRST, Y_FIRST)
    while len(mix[0].left) > 1:
        step(mix)
    send(mix + attn)
    fence(mix + attn)
    mix_all = mix[0].result().reshape(count, shard_rows + 8, cols)
    mix_half = mix_all[:, :shard_rows].reshape(width, cols)
    mix_both = (mix_half, pair(mix_half))
    norms_all = mix_all[:, shard_rows, : 4 * shard_rows].reshape(count, 4, shard_rows)
    norms_all = norms_all.astype(F32).transpose(1, 0, 2).reshape(4, width)
    gain_one, bias_one, gain_two, bias_two = (norms_all[i : i + 1] for i in range(4))
    coefs = jnp.where(
        side == 0,
        jnp.concatenate([coefs, coefs_got], axis=2),
        jnp.concatenate([coefs_got, coefs], axis=2),
    )
    decay, inject, readout = coefs.reshape(3, states, tiles, LANES)
    coef = inject * readout
    segments = lax.dynamic_index_in_dim(segment_ids[:, 0], side, 0, keepdims=False)
    starts = jnp.sum(
        (segments[None, :] < jnp.arange(16, dtype=jnp.int32)[:, None]).astype(jnp.int32), axis=1
    )
    seg_col, seg_row = segments[:, None], segments[None, :]
    while len(attn[0].left) > 2:
        step(attn)
    attn = attn[0].split(both_ways)
    send(attn)

    rows, normed, drive, ssm_first, state_mid = ssm_forward(
        starts, at_side, mine_in, got_in, *mix_both, gain_one, bias_one, decay, coef
    )
    state_mid = fence(attn, state_mid)
    send(attn + ffn[0])
    mine_cot, got_cot = out_grad[:, 0], pair(tie(out_grad, state_mid)[0][:, 0])
    ssm_out, cot = ssm_rest(
        starts, at_side, mine_cot, got_cot, drive, decay, coef, state_mid, ssm_first
    )
    ssm_out = fence(attn + ffn[0], ssm_out)
    left, right = ((h, pair(h)) for h in (m.result() for m in attn))
    while len(ffn[0][0].left) > 2:
        step(ffn[0])
    ffn[0] = ffn[0][0].split(both_ways, True)
    send(ffn[0] + ffn[1])
    query, key, value = project(at_side, normed, ssm_out, left, right)
    query = fence(ffn[0], query)
    send(ffn[0])
    attended, lse = attention_forward(seg_col, seg_row, query, key, value)
    attended = fence(ffn[0] + ffn[1], attended)
    while len(ffn[1][0].left) > 2:
        step(ffn[1])
    ffn[1] = ffn[1][0].split(both_ways, True)
    send(ffn[1])
    middle, normed_two = middle_of(at_side, attended, right, rows, gain_two, bias_two)

    middle, normed_two = fence(ffn[1], middle, normed_two)
    send(ffn[1])

    def scatters(left, right):
        return [Scatter(left, count, index, X_FIRST), Scatter(right, count, index, Y_FIRST)]

    normed_other = pair(normed_two)
    *both, grad_up, grad_down = feed_forward(
        0, normed_two, normed_other, cot, *ffn[0], ()
    )
    both, grad_up, grad_down = fence(ffn[1], both, grad_up, grad_down)
    sums_one = scatters(grad_up, grad_down)
    send(sums_one)
    own, other, gown, gother, grad_up, grad_down = feed_forward(
        1, normed_two, normed_other, cot, *ffn[1], both
    )
    own, other, gown, gother, grad_up, grad_down = fence(
        sums_one, own, other, gown, gother, grad_up, grad_down
    )
    send(sums_one)
    sums_two = scatters(grad_up, grad_down)

    grad_middle, grad_branch, grad_attended, norm_two_sums = norm_two_back(
        at_side, gown, pair(gother), middle, cot, gain_two, right
    )
    grad_attended = fence(sums_one, grad_attended)
    join_chains(sums_one)
    send(sums_one + sums_two)
    grad_query, grad_key, grad_value = attention_backward(
        seg_col, seg_row, query, key, value, lse, grad_attended
    )
    grad_query, grad_key, grad_value = fence(
        sums_one + sums_two, grad_query, grad_key, grad_value
    )
    send(sums_two)

    def pair_sum(theirs, mine):
        return (mine.astype(F32) + pair(theirs).astype(F32)).astype(BF)

    grads_left = weight_grads(at_side, (normed, grad_branch), (grad_query, attended))
    grads_left, ssm_out = tie(grads_left, ssm_out)
    grads_right = weight_grads(at_side, (ssm_out,), (grad_key, grad_value))
    sums_left = pair_sum(*grads_left)
    grads_right = fence(sums_two, grads_right)
    sums_attn = scatters(sums_left, pair_sum(*grads_right))
    join_chains(sums_two)
    send(sums_attn + sums_two)
    g_steps, gm_steps, sum_one, dsum_one = ssm_backward(
        starts, at_side, grad_key, grad_value, left, right, drive, decay, coef
    )
    g_steps, gm_steps = fence(sums_attn + sums_two, g_steps, gm_steps)
    send(sums_attn)
    grad_mixed, sum_two, dsum_two = ssm_backward_rest(
        starts, g_steps, gm_steps, drive, decay, coef
    )
    grad_mixed = fence(sums_attn, grad_mixed)
    join_chains(sums_attn)
    send(sums_attn)
    grads_mix = weight_grads(at_side, (normed,), (grad_mixed,))
    grads_mix, grad_mixed = tie(grads_mix, grad_mixed)
    sums_mix = [Scatter(pair_sum(*grads_mix), count, index, DIRECT)]
    sums_mix[0].values, grad_mixed = tie(sums_mix[0].values, grad_mixed)
    send(sums_mix)
    for_partner, norm_one_first = norm_one_back(
        at_side, grad_query, grad_mixed, rows, grad_middle, gain_one, left, mix_both, True
    )
    for_partner, norm_one_first, grad_mixed = fence(
        sums_mix + sums_attn, for_partner, norm_one_first, grad_mixed
    )
    send(sums_mix)
    got_grad = pair(for_partner)
    in_grad, norm_one_second = norm_one_back(
        at_side, grad_query, grad_mixed, rows, grad_middle, gain_one, left, mix_both, False
    )
    in_grad, norm_one_second, middle, own, other = fence(
        sums_mix, in_grad, norm_one_second, middle, own, other
    )

    state_sums = jnp.concatenate([sum_one, sum_two, dsum_one, dsum_two]).reshape(
        2 * states, width
    )
    sums = jnp.concatenate(
        [
            lax.dynamic_slice_in_dim(state_sums, (1 - side) * cols, cols, 1),
            (norm_one_first + norm_one_second).reshape(-1, cols),
            norm_two_sums.reshape(-1, cols),
        ]
    )
    mine = lax.dynamic_slice_in_dim(state_sums, side * cols, cols, 1)
    small = [Total(jnp.concatenate([mine, sums[2 * states :]]) + pair(sums), count)]
    send(small)
    in_half = (1 - side) * half
    partner_sum = pair(
        lax.dynamic_slice_in_dim(middle, in_half, half, 0)
        + lax.dynamic_slice_in_dim(own, in_half, half, 0).astype(F32)
    )
    partner_other = pair(lax.dynamic_slice_in_dim(other, in_half, half, 0))
    in_grad = put(at_side, got_grad, in_grad)
    in_grad, middle = fence(small, in_grad, middle)
    send(small)
    layer_out = layer_out_of(at_side, middle, own, other, partner_sum, partner_other)
    layer_out = fence(small, layer_out)
    complete(sums_mix + small + sums_attn + sums_one + sums_two)
    small = small[0].values
    total, dtotal = small[:states], small[states : 2 * states]
    norm_sums = lax.dynamic_slice_in_dim(
        small[2 * states :].reshape(4, width), index * shard_rows, shard_rows, 1
    )
    shard_attn = sums_attn[0].result()
    shards = [sums_one[0].result(), sums_two[0].result()]
    return (
        layer_out[:, None],
        in_grad[:, None],
        sums_mix[0].result(),
        shard_attn[:, :cols],
        shard_attn[:, 2 * cols : 3 * cols],
        shard_attn[:, 3 * cols :],
        shard_attn[:, cols : 2 * cols].T,
        jnp.concatenate([v[:, :units] for v in shards], axis=1),
        jnp.concatenate([v[:, units:] for v in shards], axis=1).T,
        norm_sums[0],
        norm_sums[1],
        norm_sums[2],
        norm_sums[3],
        ssm_inject * ssm_readout * dtotal,
        ssm_readout * total,
        ssm_inject * total,
    )


def solution(mesh):
    return jax.shard_map(
        functools.partial(per_device, mesh.shape["dp"]),
        mesh=mesh,
        in_specs=(
            P(None, "dp", "tensor", None),
            P(None, "dp", None),
            P("dp", "tensor"),
            P("dp", "tensor"),
            P("dp", "tensor"),
            P("dp", "tensor"),
            P("tensor", "dp"),
            P("dp", "tensor"),
            P("tensor", "dp"),
            P("dp"),
            P("dp"),
            P("dp"),
            P("dp"),
            P(None, "tensor"),
            P(None, "tensor"),
            P(None, "tensor"),
            P(None, "dp", "tensor", None),
        ),
        out_specs=(
            P(None, "dp", "tensor", None),
            P(None, "dp", "tensor", None),
            P("dp", "tensor"),
            P("dp", "tensor"),
            P("dp", "tensor"),
            P("dp", "tensor"),
            P("tensor", "dp"),
            P("dp", "tensor"),
            P("tensor", "dp"),
            P("dp"),
            P("dp"),
            P("dp"),
            P("dp"),
            P(None, "tensor"),
            P(None, "tensor"),
            P(None, "tensor"),
        ),
        check_vma=False,
    )
```

```python
import functools
import math

import jax
import jax.numpy as jnp
from jax import lax
from jax.experimental import pallas as pl
from jax.experimental.pallas import tpu as pltpu
from jax.sharding import PartitionSpec as P

HEAD_DIM = 128
BLOCK = 512
CTX = 128
NDOCS = 8
LANES = 128
QTILE = 256
HEADS_EACH = 2
CUT = 4

norm_eps = 1e-05
masked_score = -1e30
VMEM = 56 * 1024 * 1024
BF = jnp.bfloat16
F32 = jnp.float32


def dot_plain(left_op, right_op):
    return jnp.dot(left_op, right_op, preferred_element_type=F32)


def dot_last(left_op, right_op):
    return lax.dot_general(left_op, right_op, (((1,), (1,)), ((), ())), preferred_element_type=F32)


def dot_first(left_op, right_op):
    return lax.dot_general(left_op, right_op, (((0,), (0,)), ((), ())), preferred_element_type=F32)


def params(count=1):
    return pltpu.CompilerParams(
        dimension_semantics=("arbitrary",) * count, vmem_limit_bytes=VMEM
    )


def bits_of(count):
    out = []
    bit = 1
    while bit < count:
        out.append(bit)
        bit *= 2
    return out


def groups_of(count, low_groups):
    high = bits_of(count)[2:]
    return [tuple(high[k : k + 2]) for k in range(0, len(high), 2)] + [
        tuple(b for b in g if b < count) for g in low_groups
    ]


X_FIRST = ((1,), (2,))
Y_FIRST = ((2,), (1,))
DIRECT = ((1, 2),)


def swap(values, count, mask):
    return lax.ppermute(values, "dp", [(i, i ^ mask) for i in range(count)])


def tie(*trees):
    return lax.optimization_barrier(trees)


def in_order(upper, own, got, axis):
    return jnp.where(
        upper, jnp.stack([got, own], axis=axis), jnp.stack([own, got], axis=axis)
    )


class Gather:
    def __init__(self, shard, count, index, low):
        self.values, self.count, self.index = shard, count, index
        self.shape = (count * shard.shape[0],) + shard.shape[1:]
        self.left = groups_of(count, low)
        self.present = []
        self.loose = False
        self.last = None

    def send(self):
        self.got = [swap(self.values, self.count, m) for m in masks_of(self.left[0])]

    def merge(self):
        pieces = [self.values] + list(self.got)
        if self.loose and len(self.left) == 1:
            self.last = self.left.pop()[0]
            self.values = pieces
            return
        for bit in self.left.pop(0):
            place = 0 if self.loose else sum(1 for p in self.present if p > bit)
            self.present.insert(place, bit)
            upper = (self.index // bit) % 2 == 1
            pieces = [
                in_order(upper, pieces[k], pieces[k + 1], place)
                for k in range(0, len(pieces), 2)
            ]
        self.values = pieces[0]

    def split(self, lows, loose=False):
        cols = self.values.shape[-1] // 2
        out = []
        for k, low in enumerate(lows):
            part = Gather.__new__(Gather)
            part.count, part.index, part.present = self.count, self.index, list(self.present)
            part.values = self.values[..., k * cols : (k + 1) * cols]
            part.shape = self.shape[:-1] + (cols,)
            part.left = self.left[: -len(lows)] + list(low)
            part.last = None
            part.loose = loose and self.shape[0] // self.count % 16 == 0
            out.append(part)
        return out

    def result(self):
        return self.values.reshape(self.shape)

    def parts(self):
        if self.last is None:
            return [self.result()], ((0,), 0), jnp.int32(0)
        half = (self.shape[0] // 2,) + self.shape[1:]
        blocks = [0]
        for bit in self.present[::-1]:
            blocks = blocks + [b + bit for b in blocks]
        return (
            [v.reshape(half) for v in self.values],
            (tuple(blocks), self.last),
            (self.index // self.last) % 2,
        )


def masks_of(group):
    return [group[0]] if len(group) == 1 else [group[0], group[1], group[0] | group[1]]


class Scatter:
    def __init__(self, full, count, index, low, singly=False):
        bits = bits_of(count)
        self.values = full.reshape((2,) * len(bits) + (full.shape[0] // count,) + full.shape[1:])
        self.count, self.index = count, index
        self.present = sorted(bits, reverse=True)
        self.left = groups_of(count, low)[::-1]
        if singly:
            self.left = [(b,) for group in self.left for b in group[::-1]]

    def block(self, group, mask):
        values, present = self.values, list(self.present)
        for bit in group:
            place = present.index(bit)
            digit = ((self.index ^ mask) // bit) % 2
            values = lax.dynamic_index_in_dim(values, digit, place, keepdims=False)
            present.remove(bit)
        return values

    def send(self):
        group = self.left[0]
        self.got = [swap(self.block(group, m), self.count, m) for m in masks_of(group)]

    def merge(self):
        group = self.left.pop(0)
        total = self.block(group, 0).astype(F32)
        for got in self.got:
            total = total + got.astype(F32)
        for bit in group:
            self.present.remove(bit)
        self.values = total.astype(BF) if self.present else total

    def result(self):
        return self.values


class Total:
    def __init__(self, values, count):
        self.values, self.count = values, count
        self.left = groups_of(count, DIRECT)[::-1]

    def send(self):
        self.got = [swap(self.values, self.count, m) for m in masks_of(self.left[0])]

    def merge(self):
        self.left.pop(0)
        total = self.values + self.got[0]
        if len(self.got) > 1:
            total = total + (self.got[1] + self.got[2])
        self.values = total


def send(chains, *gates):
    chains = [c for c in chains if c.left]
    held = tie([c.values for c in chains], gates)[0]
    for c, v in zip(chains, held):
        c.values = v
    for c in chains:
        c.send()


def fence(chains, *values):
    chains = [c for c in chains if c.left]
    held, values = tie([(c.values, c.got) for c in chains], values)
    for c, (v, g) in zip(chains, held):
        c.values, c.got = v, g
        c.merge()
    held, values = tie(marks(chains), values)
    for c, v in zip(chains, held):
        c.values = v
    return values if len(values) != 1 else values[0]


def step(chains, *gates):
    send(chains, *gates)
    fence(chains)


def complete(chains):
    while any(c.left for c in chains):
        step(chains)


def join_chains(chains):
    chains[0].values = jnp.concatenate([c.values for c in chains], axis=-1)
    del chains[1:]


def marks(chains):
    return [c.values for c in chains]


def pair(values):
    return lax.ppermute(values, "tensor", [(0, 1), (1, 0)])


def norm_of(values, gain_vec, bias_vec):
    centred = values - jnp.mean(values, axis=-1, keepdims=True)
    inverse = lax.rsqrt(jnp.mean(centred * centred, axis=-1, keepdims=True) + norm_eps)
    return centred * inverse * gain_vec + bias_vec


def to_steps(steps_ref, row_first, values, col_first):
    rows, cols = values.shape
    tiles = steps_ref.shape[1]
    for j in range(cols // LANES):
        steps_ref[pl.ds(row_first, rows), col_first // LANES + j, :] = values[
            :, j * LANES : (j + 1) * LANES
        ]


def run_docs(starts_ref, low, high, one_step, make_start, finish, backward, unroll=8):
    for doc in range(NDOCS):
        d = NDOCS - 1 - doc if backward else doc
        first = jnp.minimum(jnp.maximum(starts_ref[d], low), high)
        last = jnp.minimum(jnp.maximum(starts_ref[d + 1], low), high)
        length = last - first
        groups = length // unroll
        carry = make_start(d)

        def group_body(g, carry):
            base = last - 1 - g * unroll if backward else first + g * unroll
            for i in range(unroll):
                carry = one_step(base - i if backward else base + i, carry)
            return carry

        carry = lax.fori_loop(0, groups, group_body, carry)
        done = groups * unroll

        def one_body(i, carry):
            return one_step(last - 1 - done - i if backward else first + done + i, carry)

        carry = lax.fori_loop(0, length - done, one_body, carry)
        finish(d, length, carry)


def add_up(parts):
    while len(parts) > 1:
        parts = [parts[k] + parts[k + 1] for k in range(0, len(parts), 2)]
    return parts[0]


def scan_states(starts_ref, low, high, drive_ref, decay_ref, coef_ref, y_ref, start_ref, end_ref):
    states = decay_ref.shape[0]
    zero = jnp.zeros(decay_ref.shape[1:], F32)

    def one_step(t, state):
        u = drive_ref[t]
        new = [decay_ref[n] * state[n] + u for n in range(states)]
        y_ref[t - low] = add_up([coef_ref[n] * new[n] for n in range(states)])
        return tuple(new)

    def make_start(d):
        if start_ref is None:
            return (zero,) * states
        going = starts_ref[d] < low
        return tuple(jnp.where(going, start_ref[n], zero) for n in range(states))

    def finish(d, length, carry):
        if end_ref is not None:

            @pl.when(length > 0)
            def _():
                for n in range(states):
                    end_ref[n] = carry[n]

    run_docs(starts_ref, low, high, one_step, make_start, finish, False)


def from_steps(steps_ref, out_ref):
    length, tiles, _ = steps_ref.shape
    chunk = 256

    def write(i, _):
        r = pl.multiple_of(i * chunk, chunk)
        for j in range(tiles):
            out_ref[pl.ds(r, chunk), j * LANES : (j + 1) * LANES] = steps_ref[
                pl.ds(r, chunk), j, :
            ].astype(BF)
        return 0

    lax.fori_loop(0, length // chunk, write, 0)


def both_parts(own, other, joined, at, sems):
    copies = [
        pltpu.make_async_copy(own, joined.at[at(0)], sems.at[0]),
        pltpu.make_async_copy(other, joined.at[at(1)], sems.at[1]),
    ]
    for copy in copies:
        copy.start()
    return copies


def cols_at(side, cols):
    return lambda k: (
        slice(None),
        pl.ds(pl.multiple_of((side if k == 0 else 1 - side) * cols, cols), cols),
    )


def rows_at(side, rows, *lead):
    return lambda k: lead + (
        pl.ds(pl.multiple_of((side if k == 0 else 1 - side) * rows, rows), rows),
    )


def wait_all(copies):
    for copy in copies:
        copy.wait()


def ssm_forward_kernel(
    starts_ref, side_ref, mine_ref, got_ref, mix_own_ref, mix_other_ref, gain_ref, bias_ref, decay_ref, coef_ref,
    rows_ref, normed_ref, drive_ref, out_ref, end_ref, y_ref, mix_ref, sems,
):
    length, width = rows_ref.shape
    side = side_ref[0]
    copies = both_parts(
        mine_ref.at[side], got_ref.at[side], rows_ref, rows_at(side, length // 2), sems.at[0]
    ) + both_parts(
        mix_own_ref, mix_other_ref, mix_ref, cols_at(side, width // 2), sems.at[1]
    )
    wait_all(copies)
    chunk = 256

    def project(i, _):
        r = pl.multiple_of(i * chunk, chunk)
        normed = norm_of(
            rows_ref[pl.ds(r, chunk), :].astype(F32), gain_ref[...], bias_ref[...]
        ).astype(BF)
        normed_ref[pl.ds(r, chunk), :] = normed
        for c in range(0, width, 256):
            to_steps(drive_ref, r, dot_plain(normed, mix_ref[:, c : c + 256]), c)
        return 0

    lax.fori_loop(0, length // chunk, project, 0)
    scan_states(
        starts_ref, 0, length // CUT, drive_ref, decay_ref, coef_ref, y_ref, None, end_ref
    )
    from_steps(y_ref, out_ref)


def ssm_rest_kernel(
    starts_ref, side_ref, mine_ref, got_ref, drive_ref, decay_ref, coef_ref, start_ref, first_ref,
    out_ref, cot_ref, y_ref, sems,
):
    length = drive_ref.shape[0]
    half = length // 2
    cut = length // CUT
    side = side_ref[0]
    copies = both_parts(
        mine_ref.at[side], got_ref.at[side], cot_ref, rows_at(side, half, 0), sems.at[0]
    ) + both_parts(
        mine_ref.at[1 - side], got_ref.at[1 - side], cot_ref, rows_at(side, half, 1), sems.at[1]
    )
    scan_states(
        starts_ref, cut, length, drive_ref, decay_ref, coef_ref, y_ref, start_ref, None
    )
    out_ref[:cut, :] = first_ref[...]
    from_steps(y_ref, out_ref.at[cut:])
    wait_all(copies)


SMALL = pl.BlockSpec(memory_space=pltpu.SMEM)
WHOLE = pl.BlockSpec(memory_space=pltpu.VMEM)
ANYWHERE = pl.BlockSpec(memory_space=pl.ANY)
COPIES = pltpu.SemaphoreType.DMA((2, 2))


def ssm_forward(starts, side, mine, got, mix_own, mix_other, gain_vec, bias_vec, decay, coef):
    length, width = 2 * mine.shape[1], mine.shape[2]
    tiles = width // LANES
    return pl.pallas_call(
        ssm_forward_kernel,
        out_shape=(
            jax.ShapeDtypeStruct((length, width), BF),
            jax.ShapeDtypeStruct((length, width), BF),
            jax.ShapeDtypeStruct((length, tiles, LANES), F32),
            jax.ShapeDtypeStruct((length // CUT, width), BF),
            jax.ShapeDtypeStruct(decay.shape, F32),
        ),
        in_specs=[SMALL] * 2 + [ANYWHERE] * 4 + [WHOLE] * 4,
        out_specs=(WHOLE,) * 5,
        scratch_shapes=[
            pltpu.VMEM((length // CUT, tiles, LANES), F32),
            pltpu.VMEM((width, width), BF),
            COPIES,
        ],
        compiler_params=pltpu.CompilerParams(vmem_limit_bytes=VMEM),
        cost_estimate=pl.CostEstimate(
            flops=12 * length * width * width,
            bytes_accessed=16 * length * width,
            transcendentals=0,
        ),
        name="ssm_forward",
    )(starts, side, mine, got, mix_own, mix_other, gain_vec, bias_vec, decay, coef)


def ssm_rest(starts, side, mine, got, drive, decay, coef, start, first):
    length, tiles, _ = drive.shape
    width = tiles * LANES
    return pl.pallas_call(
        ssm_rest_kernel,
        out_shape=(
            jax.ShapeDtypeStruct((length, width), BF),
            jax.ShapeDtypeStruct((2, length, width), BF),
        ),
        in_specs=[SMALL] * 2 + [ANYWHERE] * 2 + [WHOLE] * 5,
        out_specs=(WHOLE, WHOLE),
        scratch_shapes=[pltpu.VMEM((length - length // CUT, tiles, LANES), F32), COPIES],
        compiler_params=pltpu.CompilerParams(vmem_limit_bytes=VMEM),
        cost_estimate=pl.CostEstimate(
            flops=10 * length * width * width,
            bytes_accessed=16 * length * width,
            transcendentals=0,
        ),
        name="ssm_rest",
    )(starts, side, mine, got, drive, decay, coef, start, first)


def project_kernel(
    side_ref, normed_ref, ssm_ref, left_own_ref, left_other_ref, right_own_ref, right_other_ref,
    query_ref, key_ref, value_ref, weights_ref, sems,
):
    width = normed_ref.shape[1]
    cols = width // 2
    at = cols_at(side_ref[0], cols)
    sources = (
        (left_own_ref, left_other_ref, 0),
        (left_own_ref, left_other_ref, cols),
        (right_own_ref, right_other_ref, 0),
    )
    copies = [
        both_parts(
            own.at[:, c : c + cols], other.at[:, c : c + cols], weights_ref.at[k], at, sems.at[k]
        )
        for k, (own, other, c) in enumerate(sources)
    ]
    for k, (rows_ref, out_ref) in enumerate(
        ((normed_ref, query_ref), (ssm_ref, key_ref), (ssm_ref, value_ref))
    ):
        wait_all(copies[k])
        for c in range(0, width, cols):
            out_ref[:, c : c + cols] = dot_plain(
                rows_ref[...], weights_ref[k, :, c : c + cols]
            ).astype(BF)


def project(side, normed, ssm_out, left, right):
    length, width = normed.shape
    return pl.pallas_call(
        project_kernel,
        out_shape=(jax.ShapeDtypeStruct((length, width), BF),) * 3,
        in_specs=[SMALL] + [WHOLE] * 2 + [ANYWHERE] * 4,
        out_specs=(WHOLE,) * 3,
        scratch_shapes=[pltpu.VMEM((3, width, width), BF), pltpu.SemaphoreType.DMA((3, 2))],
        compiler_params=pltpu.CompilerParams(vmem_limit_bytes=VMEM),
        cost_estimate=pl.CostEstimate(
            flops=6 * length * width * width, bytes_accessed=16 * length * width, transcendentals=0
        ),
        name="project",
    )(side, normed, ssm_out, *left, *right)


def adjoint_states(starts_ref, low, drive_ref, g_ref, decay_ref, coef_ref, gm_ref, sum_ref, dsum_ref, given_ref):
    length = g_ref.shape[0]
    part = sum_ref.shape[0]
    zero = jnp.zeros(decay_ref.shape[1:], F32)

    def one_step(t, carry):
        mu, rho, total, dtotal = carry
        u = drive_ref[t]
        g = g_ref[t]
        new_mu, new_rho, new_total, new_dtotal, parts = [], [], [], [], []
        for n in range(part):
            a = decay_ref[low + n]
            r = a * rho[n] + mu[n]
            m = a * mu[n] + g
            new_mu.append(m)
            new_rho.append(r)
            new_total.append(total[n] + u * m)
            new_dtotal.append(dtotal[n] + u * r)
            parts.append(coef_ref[low + n] * m)
        gm = add_up(parts)
        gm_ref[t] = gm if given_ref is None else gm + given_ref[t]
        return tuple(new_mu), tuple(new_rho), tuple(new_total), tuple(new_dtotal)

    for n in range(part):
        sum_ref[n] = zero
        dsum_ref[n] = zero

    def make_start(d):
        zeros = (zero,) * part
        return zeros, zeros, zeros, zeros

    def finish(d, count, carry):
        for n in range(part):
            sum_ref[n] = sum_ref[n] + carry[2][n]
            dsum_ref[n] = dsum_ref[n] + carry[3][n]

    run_docs(starts_ref, 0, length, one_step, make_start, finish, True)


def ssm_backward_kernel(
    starts_ref, side_ref, gkey_ref, gvalue_ref, left_own_ref, left_other_ref, right_own_ref, right_other_ref,
    drive_ref, decay_ref, coef_ref, gmixed_ref, sum_ref, dsum_ref, g_ref, gm_ref, wkey_ref, wvalue_ref, sems,
):
    length, width = gkey_ref.shape
    cols = width // 2
    at = cols_at(side_ref[0], cols)
    copies = both_parts(
        left_own_ref.at[:, cols:], left_other_ref.at[:, cols:], wkey_ref, at, sems.at[0]
    ) + both_parts(
        right_own_ref.at[:, :cols], right_other_ref.at[:, :cols], wvalue_ref, at, sems.at[1]
    )
    wait_all(copies)
    chunk = 256

    def project(i, _):
        r = pl.multiple_of(i * chunk, chunk)
        gkey = gkey_ref[pl.ds(r, chunk), :]
        gvalue = gvalue_ref[pl.ds(r, chunk), :]
        for c in range(0, width, 256):
            to_steps(
                g_ref,
                r,
                dot_last(gkey, wkey_ref[c : c + 256, :])
                + dot_last(gvalue, wvalue_ref[c : c + 256, :]),
                c,
            )
        return 0

    lax.fori_loop(0, length // chunk, project, 0)
    part = decay_ref.shape[0] // 2
    for k in range(2):
        mine = pl.ds(k * part, part)
        adjoint_states(
            starts_ref, k * part, drive_ref, g_ref, decay_ref, coef_ref, gm_ref,
            sum_ref.at[mine], dsum_ref.at[mine], gm_ref if k else None,
        )
    from_steps(gm_ref, gmixed_ref)


def ssm_backward(starts, side, gkey, gvalue, left, right, drive, decay, coef):
    length, width = gkey.shape
    tiles = width // LANES
    return pl.pallas_call(
        ssm_backward_kernel,
        out_shape=(
            jax.ShapeDtypeStruct((length, width), BF),
            jax.ShapeDtypeStruct(decay.shape, F32),
            jax.ShapeDtypeStruct(decay.shape, F32),
        ),
        in_specs=[SMALL] * 2 + [WHOLE] * 2 + [ANYWHERE] * 4 + [WHOLE] * 3,
        out_specs=(WHOLE,) * 3,
        scratch_shapes=[pltpu.VMEM((length, tiles, LANES), F32)] * 2
        + [pltpu.VMEM((width, width), BF)] * 2
        + [COPIES],
        compiler_params=pltpu.CompilerParams(vmem_limit_bytes=VMEM),
        cost_estimate=pl.CostEstimate(
            flops=40 * length * width * width,
            bytes_accessed=20 * length * width,
            transcendentals=0,
        ),
        name="ssm_backward",
    )(starts, side, gkey, gvalue, *left, *right, drive, decay, coef)


def attention_tiles(length):
    tiles = []
    for first in range(0, length, QTILE):
        block_first = first // BLOCK * BLOCK
        key_first = max(0, block_first - CTX)
        tiles.append((first, key_first, first + QTILE - key_first))
    return tiles


def fill_bias(seg_col_ref, seg_row_ref, bias_ref, tiles):
    at = 0
    for first, key_first, count in tiles:
        same = seg_col_ref[first : first + QTILE, :] == seg_row_ref[:, key_first : key_first + count]
        query_pos = lax.broadcasted_iota(jnp.int32, (QTILE, count), 0) + first
        key_pos = lax.broadcasted_iota(jnp.int32, (QTILE, count), 1) + key_first
        bias_ref[:, at : at + count] = jnp.where(
            same & (key_pos <= query_pos), 0.0, masked_score
        ).astype(F32)
        at += count


EXP_SCALE = HEAD_DIM ** (-0.5) * math.log2(math.e)


def attention_jobs(length):
    jobs = []
    for h in range(HEADS_EACH):
        at = 0
        for first, key_first, count in attention_tiles(length):
            jobs.append(
                (
                    h,
                    slice(h * HEAD_DIM, (h + 1) * HEAD_DIM),
                    slice(first, first + QTILE),
                    slice(key_first, key_first + count),
                    slice(at, at + count),
                )
            )
            at += count
    return jobs


def attention_forward_kernel(
    seg_col_ref, seg_row_ref, query_ref, key_ref, value_ref, out_ref, lse_ref, bias_ref, value_one_ref
):
    length = query_ref.shape[0]

    @pl.when(pl.program_id(0) == 0)
    def _():
        fill_bias(seg_col_ref, seg_row_ref, bias_ref, attention_tiles(length))
        for h in range(HEADS_EACH):
            value_one_ref[h, :, HEAD_DIM:] = jnp.ones((length, HEAD_DIM), BF)

    for h in range(HEADS_EACH):
        value_one_ref[h, :, :HEAD_DIM] = value_ref[:, h * HEAD_DIM : (h + 1) * HEAD_DIM]
    jobs = attention_jobs(length)

    def scores_of(job):
        _, lanes, rows, keys, _ = job
        return dot_last(query_ref[rows, lanes], key_ref[keys, lanes])

    ahead = scores_of(jobs[0])
    for k, (h, lanes, rows, keys, mask) in enumerate(jobs):
        scores = ahead
        if k + 1 < len(jobs):
            ahead = scores_of(jobs[k + 1])
        scores = scores * EXP_SCALE + bias_ref[:, mask]
        top = jnp.max(scores, axis=-1, keepdims=True)
        raised = jnp.exp2(scores - top).astype(BF)
        both = dot_plain(raised, value_one_ref[h, keys, :])
        total = both[:, HEAD_DIM:]
        out_ref[rows, lanes] = (both[:, :HEAD_DIM] / total).astype(BF)
        lse_ref[h, rows, :] = top + jnp.log2(total[:, :1])


def attention_forward(seg_col, seg_row, query, key, value):
    length, width = query.shape
    heads = width // HEAD_DIM
    tiles = attention_tiles(length)
    cols = sum(t[2] for t in tiles)
    head = pl.BlockSpec((length, HEADS_EACH * HEAD_DIM), lambda h: (0, h))
    whole = lambda shape: pl.BlockSpec(shape, lambda h: (0, 0))
    return pl.pallas_call(
        attention_forward_kernel,
        grid=(heads // HEADS_EACH,),
        out_shape=(
            jax.ShapeDtypeStruct((length, width), BF),
            jax.ShapeDtypeStruct((heads, length, 1), F32),
        ),
        in_specs=[whole((length, 1)), whole((1, length)), head, head, head],
        out_specs=(head, pl.BlockSpec((HEADS_EACH, length, 1), lambda h: (h, 0, 0))),
        scratch_shapes=[
            pltpu.VMEM((QTILE, cols), F32),
            pltpu.VMEM((HEADS_EACH, length, 2 * HEAD_DIM), BF),
        ],
        compiler_params=params(),
        cost_estimate=pl.CostEstimate(
            flops=4 * QTILE * cols * width,
            bytes_accessed=8 * length * width,
            transcendentals=QTILE * cols * heads,
        ),
        name="attention_forward",
    )(seg_col, seg_row, query, key, value)


def attention_backward_kernel(
    seg_col_ref, seg_row_ref, query_ref, key_ref, value_ref, lse_ref, gout_ref,
    gquery_ref, gkey_ref, gvalue_ref, bias_ref, gk_ref, gv_ref,
):
    length = query_ref.shape[0]
    scale = HEAD_DIM ** (-0.5)

    @pl.when(pl.program_id(0) == 0)
    def _():
        fill_bias(seg_col_ref, seg_row_ref, bias_ref, attention_tiles(length))

    gk_ref[...] = jnp.zeros_like(gk_ref)
    gv_ref[...] = jnp.zeros_like(gv_ref)
    jobs = attention_jobs(length)

    def scores_of(job):
        _, lanes, rows, keys, _ = job
        return (
            dot_last(query_ref[rows, lanes], key_ref[keys, lanes]),
            dot_last(gout_ref[rows, lanes], value_ref[keys, lanes]),
        )

    ahead = scores_of(jobs[0])
    for k, (h, lanes, rows, keys, mask) in enumerate(jobs):
        scores, gprobs = ahead
        if k + 1 < len(jobs):
            ahead = scores_of(jobs[k + 1])
        gout = gout_ref[rows, lanes]
        probs = jnp.exp2(scores * EXP_SCALE + bias_ref[:, mask] - lse_ref[h, rows, :])
        gv_ref[keys, lanes] = gv_ref[keys, lanes] + dot_first(probs.astype(BF), gout)
        inner = jnp.sum(probs * gprobs, axis=-1, keepdims=True)
        gscores = (probs * (gprobs - inner)).astype(BF)
        gquery_ref[rows, lanes] = (dot_plain(gscores, key_ref[keys, lanes]) * scale).astype(BF)
        gk_ref[keys, lanes] = gk_ref[keys, lanes] + dot_first(gscores, query_ref[rows, lanes])
    gkey_ref[...] = (gk_ref[...] * scale).astype(BF)
    gvalue_ref[...] = gv_ref[...].astype(BF)


def attention_backward(seg_col, seg_row, query, key, value, lse, gout):
    length, width = query.shape
    heads = width // HEAD_DIM
    tiles = attention_tiles(length)
    cols = sum(t[2] for t in tiles)
    head = pl.BlockSpec((length, HEADS_EACH * HEAD_DIM), lambda h: (0, h))
    whole = lambda shape: pl.BlockSpec(shape, lambda h: (0, 0))
    return pl.pallas_call(
        attention_backward_kernel,
        grid=(heads // HEADS_EACH,),
        out_shape=(jax.ShapeDtypeStruct((length, width), BF),) * 3,
        in_specs=[whole((length, 1)), whole((1, length)), head, head, head]
        + [pl.BlockSpec((HEADS_EACH, length, 1), lambda h: (h, 0, 0)), head],
        out_specs=(head,) * 3,
        scratch_shapes=[
            pltpu.VMEM((QTILE, cols), F32),
            pltpu.VMEM((length, HEADS_EACH * HEAD_DIM), F32),
            pltpu.VMEM((length, HEADS_EACH * HEAD_DIM), F32),
        ],
        compiler_params=params(),
        cost_estimate=pl.CostEstimate(
            flops=10 * QTILE * cols * width,
            bytes_accessed=14 * length * width,
            transcendentals=QTILE * cols * heads,
        ),
        name="attention_backward",
    )(seg_col, seg_row, query, key, value, lse, gout)


def norm_backward(grad, values, gain_vec):
    centred = values - jnp.mean(values, axis=-1, keepdims=True)
    inverse = lax.rsqrt(jnp.mean(centred * centred, axis=-1, keepdims=True) + norm_eps)
    xhat = centred * inverse
    dxhat = grad * gain_vec
    back = (
        dxhat
        - jnp.mean(dxhat, axis=-1, keepdims=True)
        - xhat * jnp.mean(dxhat * xhat, axis=-1, keepdims=True)
    ) * inverse
    return back, jnp.sum(grad * xhat, axis=0, keepdims=True), jnp.sum(grad, axis=0, keepdims=True)


def gelu_parts(values):
    below = 0.5 + 0.5 * lax.erf(values * (2.0**-0.5))
    bell = jnp.exp2((-0.5 * math.log2(math.e)) * (values * values))
    return values * below, below + values * (bell * ((2.0 * math.pi) ** -0.5))


FTILE = 512


def feed_forward_kernel(part, blocks, place_ref, own_ref, other_ref, cot_ref, *refs):
    pieces, refs = refs[: sum(b[0] for b in blocks)], refs[sum(b[0] for b in blocks) :]
    ins, refs = refs[: 4 * part], refs[4 * part :]
    outs, grads, refs = refs[:4], refs[4:6], refs[6:]
    normed_ref, cots_ref, up_ref, down_ref, hidden_ref, gpre_ref, sums_ref, total_ref = refs[:8]
    row_sems, weight_sems, out_sems, grad_sems = refs[8:12]
    length, width = own_ref.shape
    units = up_ref.shape[1]
    tile = FTILE
    per = length // tile
    count = 2 * per

    def tile_of(i):
        return pl.ds(pl.multiple_of(i * tile, tile), tile)

    weights = []
    for k, (ref, (number, (places, last))) in enumerate(zip((up_ref, down_ref), blocks)):
        rows = ref.shape[0] // (number * len(places))
        for p in range(number):
            source = pieces[k * blocks[0][0] + p]
            place = place_ref[k] if p == 0 else 1 - place_ref[k]
            for h, at in enumerate(places):
                pltpu.make_async_copy(
                    source.at[pl.ds(h * rows, rows)],
                    ref.at[pl.ds(pl.multiple_of((at + place * last) * rows, rows), rows)],
                    weight_sems.at[k],
                ).start()
        weights.append(pltpu.make_async_copy(ref, ref, weight_sems.at[k]))
    for i in range(count):
        rows = tile_of(i % per)
        source = (own_ref, other_ref)[i // per]
        pltpu.make_async_copy(source.at[rows], normed_ref.at[tile_of(i)], row_sems.at[0, i]).start()
        pltpu.make_async_copy(
            cot_ref.at[i // per, rows], cots_ref.at[tile_of(i)], row_sems.at[1, i]
        ).start()
    if part:
        earlier = [
            pltpu.make_async_copy(ins[k], total_ref.at[k], out_sems.at[k, count])
            for k in range(4)
        ]
        for copy in earlier:
            copy.start()
    wait_all(weights)

    def one(i, _):
        rows = tile_of(i)
        for k, ref in enumerate((normed_ref, cots_ref)):
            pltpu.make_async_copy(ref.at[rows], ref.at[rows], row_sems.at[k, i]).wait()
        for n in range(0, units, tile):
            pre = dot_plain(normed_ref[rows, :], up_ref[:, n : n + tile])
            ghidden = dot_plain(cots_ref[rows, :], down_ref[:, n : n + tile])
            hidden, slope = gelu_parts(pre)
            hidden_ref[rows, n : n + tile] = hidden.astype(BF)
            gpre_ref[rows, n : n + tile] = (ghidden * slope).astype(BF)
        return 0

    lax.fori_loop(0, count, one, 0)

    grad_copies = []
    for k, (first_ref, held_ref) in enumerate(((normed_ref, gpre_ref), (cots_ref, hidden_ref))):

        def three(i, _, k=k, first_ref=first_ref, held_ref=held_ref):
            cols = tile_of(i)
            sums_ref[k, cols, :] = dot_first(first_ref[:, cols], held_ref[...]).astype(BF)
            return 0

        lax.fori_loop(0, width // tile, three, 0)
        copy = pltpu.make_async_copy(
            sums_ref.at[k], grads[k], grad_sems.at[k]
        )
        copy.start()
        grad_copies.append(copy)

    if part:
        wait_all(earlier)
    out_copies = []
    for i in range(count):
        s, rows = i // per, slice(i % per * tile, (i % per + 1) * tile)
        held = slice(i * tile, (i + 1) * tile)
        for k, (held_ref, weight_ref) in enumerate(((hidden_ref, down_ref), (gpre_ref, up_ref))):
            total = dot_last(held_ref[held, :], weight_ref[...])
            if part:
                total = total + total_ref[2 * k + s, rows, :].astype(F32)
            total_ref[2 * k + s, rows, :] = total.astype(BF)
            copy = pltpu.make_async_copy(
                total_ref.at[2 * k + s, rows], outs[2 * k + s].at[rows], out_sems.at[k, i]
            )
            copy.start()
            out_copies.append(copy)
    wait_all(grad_copies + out_copies)


def feed_forward(part, own, other, cot, up, down, earlier):
    length, width = own.shape
    pieces, blocks, places = zip(*(chain.parts() for chain in (up, down)))
    blocks = tuple((len(p), b) for p, b in zip(pieces, blocks))
    pieces = [p for each in pieces for p in each]
    units = pieces[0].shape[1]
    count = 2 * length // FTILE
    dma = pltpu.SemaphoreType.DMA
    return pl.pallas_call(
        functools.partial(feed_forward_kernel, part, blocks),
        out_shape=(jax.ShapeDtypeStruct((length, width), BF),) * 4
        + (jax.ShapeDtypeStruct((width, units), BF),) * 2,
        in_specs=[SMALL] + [ANYWHERE] * (3 + len(pieces) + 4 * part),
        out_specs=(ANYWHERE,) * 6,
        scratch_shapes=[pltpu.VMEM((2 * length, width), BF)] * 2
        + [pltpu.VMEM((width, units), BF)] * 2
        + [pltpu.VMEM((2 * length, units), BF)] * 2
        + [pltpu.VMEM((2, width, units), BF), pltpu.VMEM((4, length, width), BF)]
        + [dma((2, count)), dma((2,)), dma((4, count + 1)), dma((2,))],
        compiler_params=pltpu.CompilerParams(vmem_limit_bytes=VMEM),
        cost_estimate=pl.CostEstimate(
            flops=28 * length * width * units,
            bytes_accessed=48 * length * width,
            transcendentals=4 * length * units,
        ),
        name="feed_forward",
    )(jnp.stack(places), own, other, cot, *pieces, *earlier)


def at_first(joins, sems, side):
    @pl.when(pl.program_id(0) == 0)
    def _():
        copies = []
        for k, (own, other, joined) in enumerate(joins):
            copies += both_parts(own, other, joined, cols_at(side, joined.shape[1] // 2), sems.at[k])
        wait_all(copies)


ROWS = 256


def row_spec(width, lead=None):
    if lead is None:
        return pl.BlockSpec((ROWS, width), lambda i: (i, 0))
    return pl.BlockSpec((None, ROWS, width), lambda i: (lead, i, 0))


def fixed(*shape):
    return pl.BlockSpec(shape, lambda i: (0,) * len(shape))


def middle_kernel(
    side_ref, attended_ref, own_ref, other_ref, rows_ref, gain_ref, bias_ref, middle_ref, normed_ref, out_ref, sems
):
    cols = out_ref.shape[1] // 2
    at_first([(own_ref.at[:, cols:], other_ref.at[:, cols:], out_ref)], sems, side_ref[0])
    middle = rows_ref[...].astype(F32) + dot_last(attended_ref[...], out_ref[...])
    middle_ref[...] = middle
    normed_ref[...] = norm_of(middle, gain_ref[...], bias_ref[...]).astype(BF)


def middle_of(side, attended, right, rows, gain_vec, bias_vec):
    length, width = rows.shape
    row = row_spec(width)
    return pl.pallas_call(
        middle_kernel,
        grid=(length // ROWS,),
        out_shape=(
            jax.ShapeDtypeStruct((length, width), F32),
            jax.ShapeDtypeStruct((length, width), BF),
        ),
        in_specs=[SMALL, row, ANYWHERE, ANYWHERE, row, fixed(1, width), fixed(1, width)],
        out_specs=(row, row),
        scratch_shapes=[pltpu.VMEM((width, width), BF), COPIES],
        compiler_params=params(),
        cost_estimate=pl.CostEstimate(
            flops=2 * length * width * width, bytes_accessed=12 * length * width, transcendentals=0
        ),
        name="middle",
    )(side, attended, *right, rows, gain_vec, bias_vec)


def norm_two_kernel(
    side_ref, mine_ref, theirs_ref, middle_ref, cot_ref, gain_ref, own_ref, other_ref,
    gmiddle_ref, gbranch_ref, gattended_ref, sums_ref, out_ref, sems,
):
    cols = out_ref.shape[1] // 2
    at_first([(own_ref.at[:, cols:], other_ref.at[:, cols:], out_ref)], sems, side_ref[0])
    grad = mine_ref[...].astype(F32) + theirs_ref[...].astype(F32)
    back, gain_sum, bias_sum = norm_backward(grad, middle_ref[...], gain_ref[...])
    gmiddle = cot_ref[...].astype(F32) + back
    gmiddle_ref[...] = gmiddle
    gbranch = gmiddle.astype(BF)
    gbranch_ref[...] = gbranch
    gattended_ref[...] = dot_plain(gbranch, out_ref[...]).astype(BF)
    add_sums(sums_ref, gain_sum, bias_sum)


def add_sums(sums_ref, gain_sum, bias_sum):
    @pl.when(pl.program_id(0) == 0)
    def _():
        sums_ref[...] = jnp.zeros_like(sums_ref)

    sums_ref[0:1, :] = sums_ref[0:1, :] + gain_sum
    sums_ref[1:2, :] = sums_ref[1:2, :] + bias_sum


def norm_two_back(side, mine, theirs, middle, cot, gain_vec, right):
    length, width = middle.shape
    row = row_spec(width)
    return pl.pallas_call(
        norm_two_kernel,
        grid=(length // ROWS,),
        out_shape=(
            jax.ShapeDtypeStruct((length, width), F32),
            jax.ShapeDtypeStruct((length, width), BF),
            jax.ShapeDtypeStruct((length, width), BF),
            jax.ShapeDtypeStruct((2, width), F32),
        ),
        in_specs=[SMALL, row, row, row, row_spec(width, 0), fixed(1, width), ANYWHERE, ANYWHERE],
        out_specs=(row, row, row, fixed(2, width)),
        scratch_shapes=[pltpu.VMEM((width, width), BF), COPIES],
        compiler_params=params(),
        cost_estimate=pl.CostEstimate(
            flops=2 * length * width * width, bytes_accessed=24 * length * width, transcendentals=0
        ),
        name="norm_two_back",
    )(side, mine, theirs, middle, cot, gain_vec, *right)


def norm_one_kernel(
    side_ref, gquery_ref, gmixed_ref, rows_ref, gmiddle_ref, gain_ref,
    left_own_ref, left_other_ref, mix_own_ref, mix_other_ref, grad_ref, sums_ref, query_ref, mix_ref, sems,
):
    cols = query_ref.shape[1] // 2
    at_first(
        [
            (left_own_ref.at[:, :cols], left_other_ref.at[:, :cols], query_ref),
            (mix_own_ref, mix_other_ref, mix_ref),
        ],
        sems,
        side_ref[0],
    )
    grad = dot_last(gquery_ref[...], query_ref[...]) + dot_last(gmixed_ref[...], mix_ref[...])
    back, gain_sum, bias_sum = norm_backward(grad, rows_ref[...].astype(F32), gain_ref[...])
    grad_ref[...] = gmiddle_ref[...] + back
    add_sums(sums_ref, gain_sum, bias_sum)


def norm_one_back(side, gquery, gmixed, rows, gmiddle, gain_vec, left, mix, for_partner):
    length, width = rows.shape
    half = length // 2
    steps = half // ROWS

    def place(side):
        return 1 - side[0] if for_partner else side[0]

    row = pl.BlockSpec((ROWS, width), lambda i, side: (place(side) * steps + i, 0))
    whole = lambda *shape: pl.BlockSpec(shape, lambda i, side: (0,) * len(shape))
    if for_partner:
        out = jax.ShapeDtypeStruct((half, width), F32)
        out_spec = pl.BlockSpec((ROWS, width), lambda i, side: (i, 0))
    else:
        out = jax.ShapeDtypeStruct((2, half, width), F32)
        out_spec = pl.BlockSpec((None, ROWS, width), lambda i, side: (side[0], i, 0))
    return pl.pallas_call(
        norm_one_kernel,
        grid_spec=pltpu.PrefetchScalarGridSpec(
            num_scalar_prefetch=1,
            grid=(steps,),
            in_specs=[row] * 4 + [whole(1, width)] + [ANYWHERE] * 4,
            out_specs=(out_spec, whole(2, width)),
            scratch_shapes=[pltpu.VMEM((width, width), BF)] * 2 + [COPIES],
        ),
        out_shape=(out, jax.ShapeDtypeStruct((2, width), F32)),
        compiler_params=params(),
        cost_estimate=pl.CostEstimate(
            flops=4 * half * width * width, bytes_accessed=20 * half * width, transcendentals=0
        ),
        name="norm_one_back",
    )(side, gquery, gmixed, rows, gmiddle, gain_vec, *left, *mix)


def put_kernel(side_ref, got_ref, given_ref, out_ref):
    out_ref[...] = got_ref[...]


def put(side, got, given):
    half, width = got.shape
    return pl.pallas_call(
        put_kernel,
        grid_spec=pltpu.PrefetchScalarGridSpec(
            num_scalar_prefetch=1,
            grid=(half // ROWS,),
            in_specs=[pl.BlockSpec((ROWS, width), lambda i, side: (i, 0)), ANYWHERE],
            out_specs=pl.BlockSpec((None, ROWS, width), lambda i, side: (1 - side[0], i, 0)),
        ),
        out_shape=jax.ShapeDtypeStruct(given.shape, given.dtype),
        input_output_aliases={2: 0},
        compiler_params=params(),
        name="put",
    )(side, got, given)


def layer_out_kernel(side_ref, middle_ref, own_ref, other_ref, sum_ref, theirs_ref, out_ref):
    side = side_ref[0]
    out_ref[side] = (
        middle_ref[...] + own_ref[...].astype(F32) + theirs_ref[...].astype(F32)
    )
    out_ref[1 - side] = sum_ref[...] + other_ref[...].astype(F32)


def layer_out_of(side, middle, own, other, partner_sum, partner_other):
    length, width = middle.shape
    half = length // 2
    steps = half // ROWS
    mine = pl.BlockSpec((ROWS, width), lambda i, side: (side[0] * steps + i, 0))
    row = pl.BlockSpec((ROWS, width), lambda i, side: (i, 0))
    return pl.pallas_call(
        layer_out_kernel,
        grid_spec=pltpu.PrefetchScalarGridSpec(
            num_scalar_prefetch=1,
            grid=(steps,),
            in_specs=[mine] * 3 + [row] * 2,
            out_specs=pl.BlockSpec((2, ROWS, width), lambda i, side: (0, i, 0)),
        ),
        out_shape=jax.ShapeDtypeStruct((2, half, width), F32),
        compiler_params=params(),
        cost_estimate=pl.CostEstimate(
            flops=4 * half * width, bytes_accessed=24 * half * width, transcendentals=0
        ),
        name="layer_out",
    )(side, middle, own, other, partner_sum, partner_other)


def weight_grads_kernel(count, side_ref, *refs):
    ins, outs, refs = refs[:-6], refs[-6:-4], refs[-4:]
    held_ref, sums_ref, in_sems, out_sems = refs
    lefts = len(ins) - count
    width = held_ref.shape[2]
    cols = width // 2
    side = side_ref[0]
    order = []
    for k in range(count):
        order += [k % lefts, lefts + k]
    order = list(dict.fromkeys(order))
    loads = {
        j: pltpu.make_async_copy(ins[j], held_ref.at[j], in_sems.at[j]) for j in order
    }
    for j in order:
        loads[j].start()
    stores = []
    for k in range(count):
        for j in (k % lefts, lefts + k):
            if j in loads:
                loads.pop(j).wait()
        for which, at in enumerate((1 - side, side)):
            part = held_ref[lefts + k, :, pl.ds(pl.multiple_of(at * cols, cols), cols)]
            sums_ref[which, k] = dot_first(held_ref[k % lefts], part).astype(BF)
            copy = pltpu.make_async_copy(
                sums_ref.at[which, k],
                outs[which].at[:, k * cols : (k + 1) * cols],
                out_sems.at[which, k],
            )
            copy.start()
            stores.append(copy)
    wait_all(stores)


def weight_grads(side, lefts, rights):
    count = len(rights)
    length, width = lefts[0].shape
    cols = width // 2
    many = len(lefts) + count
    return pl.pallas_call(
        functools.partial(weight_grads_kernel, count),
        out_shape=(jax.ShapeDtypeStruct((width, count * cols), BF),) * 2,
        in_specs=[SMALL] + [ANYWHERE] * many,
        out_specs=(ANYWHERE,) * 2,
        scratch_shapes=[
            pltpu.VMEM((many, length, width), BF),
            pltpu.VMEM((2, count, width, cols), BF),
            pltpu.SemaphoreType.DMA((many,)),
            pltpu.SemaphoreType.DMA((2, count)),
        ],
        compiler_params=pltpu.CompilerParams(vmem_limit_bytes=VMEM),
        cost_estimate=pl.CostEstimate(
            flops=2 * count * length * width * width,
            bytes_accessed=6 * count * length * width,
            transcendentals=0,
        ),
        name="weight_grads",
    )(side, *lefts, *rights)


def per_device(
    count,
    layer_in,
    segment_ids,
    w_mix_in,
    w_query,
    w_key,
    w_value,
    w_attn_out,
    w_up,
    w_down,
    norm1_gain,
    norm1_bias,
    norm2_gain,
    norm2_bias,
    ssm_decay,
    ssm_inject,
    ssm_readout,
    out_grad,
):
    index = lax.axis_index("dp")
    side = lax.axis_index("tensor")
    at_side = jnp.reshape(side, (1,))
    half = layer_in.shape[2]
    width = layer_in.shape[3]
    tiles = width // LANES
    states = ssm_decay.shape[0]
    cols = w_query.shape[1]
    parts = 2
    units = w_up.shape[1] // parts
    shard_rows = w_mix_in.shape[0]

    norms = jnp.concatenate([norm1_gain, norm1_bias, norm2_gain, norm2_bias])
    norms = jnp.pad(norms[None], ((0, 7), (0, cols - norms.shape[0])))
    mix = [Gather(jnp.concatenate([w_mix_in, norms], axis=0), count, index, DIRECT)]
    send(mix)
    mine_in, got_in = layer_in[:, 0], pair(layer_in[:, 0])
    coefs = jnp.stack([ssm_decay, ssm_inject, ssm_readout])
    coefs_got = pair(coefs)
    fence(mix)
    attn = [
        Gather(
            jnp.concatenate([w_query, w_key, w_value, w_attn_out.T], axis=1), count, index, X_FIRST
        )
    ]
    turned_down = w_down.T
    ffn = [
        [
            Gather(
                jnp.concatenate(
                    [
                        w_up[:, i * units : (i + 1) * units],
                        turned_down[:, i * units : (i + 1) * units],
                    ],
                    axis=1,
                ),
                count,
                index,
                X_FIRST,
            )
        ]
        for i in range(parts)
    ]
    both_ways = (X_FIRST, Y_FIRST)
    while len(mix[0].left) > 1:
        step(mix)
    send(mix + attn)
    fence(mix + attn)
    mix_all = mix[0].result().reshape(count, shard_rows + 8, cols)
    mix_half = mix_all[:, :shard_rows].reshape(width, cols)
    mix_both = (mix_half, pair(mix_half))
    norms_all = mix_all[:, shard_rows, : 4 * shard_rows].reshape(count, 4, shard_rows)
    norms_all = norms_all.astype(F32).transpose(1, 0, 2).reshape(4, width)
    gain_one, bias_one, gain_two, bias_two = (norms_all[i : i + 1] for i in range(4))
    coefs = jnp.where(
        side == 0,
        jnp.concatenate([coefs, coefs_got], axis=2),
        jnp.concatenate([coefs_got, coefs], axis=2),
    )
    decay, inject, readout = coefs.reshape(3, states, tiles, LANES)
    coef = inject * readout
    segments = lax.dynamic_index_in_dim(segment_ids[:, 0], side, 0, keepdims=False)
    starts = jnp.sum(
        (segments[None, :] < jnp.arange(16, dtype=jnp.int32)[:, None]).astype(jnp.int32), axis=1
    )
    seg_col, seg_row = segments[:, None], segments[None, :]
    while len(attn[0].left) > 2:
        step(attn)
    attn = attn[0].split(both_ways)
    send(attn)

    rows, normed, drive, ssm_first, state_mid = ssm_forward(
        starts, at_side, mine_in, got_in, *mix_both, gain_one, bias_one, decay, coef
    )
    state_mid = fence(attn, state_mid)
    send(attn + ffn[0])
    mine_cot, got_cot = out_grad[:, 0], pair(tie(out_grad, state_mid)[0][:, 0])
    ssm_out, cot = ssm_rest(
        starts, at_side, mine_cot, got_cot, drive, decay, coef, state_mid, ssm_first
    )
    ssm_out = fence(attn + ffn[0], ssm_out)
    left, right = ((h, pair(h)) for h in (m.result() for m in attn))
    while len(ffn[0][0].left) > 2:
        step(ffn[0])
    ffn[0] = ffn[0][0].split(both_ways, True)
    send(ffn[0] + ffn[1])
    query, key, value = project(at_side, normed, ssm_out, left, right)
    query = fence(ffn[0], query)
    send(ffn[0])
    attended, lse = attention_forward(seg_col, seg_row, query, key, value)
    attended = fence(ffn[0] + ffn[1], attended)
    while len(ffn[1][0].left) > 2:
        step(ffn[1])
    ffn[1] = ffn[1][0].split(both_ways, True)
    send(ffn[1])
    middle, normed_two = middle_of(at_side, attended, right, rows, gain_two, bias_two)

    middle, normed_two = fence(ffn[1], middle, normed_two)
    send(ffn[1])

    def scatters(left, right, singly=False):
        return [
            Scatter(left, count, index, X_FIRST, singly),
            Scatter(right, count, index, Y_FIRST, singly),
        ]

    normed_other = pair(normed_two)
    *both, grad_up, grad_down = feed_forward(
        0, normed_two, normed_other, cot, *ffn[0], ()
    )
    both, grad_up, grad_down = fence(ffn[1], both, grad_up, grad_down)
    sums_one = scatters(grad_up, grad_down)
    send(sums_one)
    own, other, gown, gother, grad_up, grad_down = feed_forward(
        1, normed_two, normed_other, cot, *ffn[1], both
    )
    own, other, gown, gother, grad_up, grad_down = fence(
        sums_one, own, other, gown, gother, grad_up, grad_down
    )
    send(sums_one)
    sums_two = scatters(grad_up, grad_down, True)

    grad_middle, grad_branch, grad_attended, norm_two_sums = norm_two_back(
        at_side, gown, pair(gother), middle, cot, gain_two, right
    )
    grad_attended = fence(sums_one, grad_attended)
    join_chains(sums_one)
    send(sums_one + sums_two)
    grad_query, grad_key, grad_value = attention_backward(
        seg_col, seg_row, query, key, value, lse, grad_attended
    )
    grad_query, grad_key, grad_value = fence(
        sums_one + sums_two, grad_query, grad_key, grad_value
    )
    send(sums_two)

    def pair_sum(theirs, mine):
        return (mine.astype(F32) + pair(theirs).astype(F32)).astype(BF)

    grads_left = weight_grads(at_side, (normed, grad_branch), (grad_query, attended))
    grads_left, ssm_out = tie(grads_left, ssm_out)
    grads_right = weight_grads(at_side, (ssm_out,), (grad_key, grad_value))
    sums_left = pair_sum(*grads_left)
    grads_right = fence(sums_two, grads_right)
    sums_attn = [
        Scatter(
            jnp.concatenate([sums_left, pair_sum(*grads_right)], axis=1), count, index, DIRECT
        )
    ]
    join_chains(sums_two)
    send(sums_attn + sums_two)
    grad_mixed, state_sum, state_dsum = ssm_backward(
        starts, at_side, grad_key, grad_value, left, right, drive, decay, coef
    )
    grad_mixed = fence(sums_attn + sums_two, grad_mixed)
    send(sums_attn)
    grads_mix = weight_grads(at_side, (normed,), (grad_mixed,))
    grads_mix, grad_mixed = tie(grads_mix, grad_mixed)
    sums_mix = [Scatter(pair_sum(*grads_mix), count, index, DIRECT)]
    sums_mix[0].values, grad_mixed = tie(sums_mix[0].values, grad_mixed)
    send(sums_mix)
    for_partner, norm_one_first = norm_one_back(
        at_side, grad_query, grad_mixed, rows, grad_middle, gain_one, left, mix_both, True
    )
    for_partner, norm_one_first, grad_mixed = fence(
        sums_mix + sums_attn, for_partner, norm_one_first, grad_mixed
    )
    send(sums_mix + sums_two)
    got_grad = pair(for_partner)
    in_grad, norm_one_second = norm_one_back(
        at_side, grad_query, grad_mixed, rows, grad_middle, gain_one, left, mix_both, False
    )
    in_grad, norm_one_second, middle, own, other = fence(
        sums_mix + sums_two, in_grad, norm_one_second, middle, own, other
    )

    state_sums = jnp.concatenate([state_sum, state_dsum]).reshape(
        2 * states, width
    )
    sums = jnp.concatenate(
        [
            lax.dynamic_slice_in_dim(state_sums, (1 - side) * cols, cols, 1),
            (norm_one_first + norm_one_second).reshape(-1, cols),
            norm_two_sums.reshape(-1, cols),
        ]
    )
    mine = lax.dynamic_slice_in_dim(state_sums, side * cols, cols, 1)
    small = [Total(jnp.concatenate([mine, sums[2 * states :]]) + pair(sums), count)]
    send(small)
    in_half = (1 - side) * half
    partner_sum = pair(
        lax.dynamic_slice_in_dim(middle, in_half, half, 0)
        + lax.dynamic_slice_in_dim(own, in_half, half, 0).astype(F32)
    )
    partner_other = pair(lax.dynamic_slice_in_dim(other, in_half, half, 0))
    in_grad = put(at_side, got_grad, in_grad)
    in_grad, middle = fence(small, in_grad, middle)
    send(small)
    layer_out = layer_out_of(at_side, middle, own, other, partner_sum, partner_other)
    layer_out = fence(small, layer_out)
    complete(sums_mix + small + sums_attn + sums_one + sums_two)
    small = small[0].values
    total, dtotal = small[:states], small[states : 2 * states]
    norm_sums = lax.dynamic_slice_in_dim(
        small[2 * states :].reshape(4, width), index * shard_rows, shard_rows, 1
    )
    shard_attn = sums_attn[0].result()
    shards = [sums_one[0].result(), sums_two[0].result()]
    return (
        layer_out[:, None],
        in_grad[:, None],
        sums_mix[0].result(),
        shard_attn[:, :cols],
        shard_attn[:, 2 * cols : 3 * cols],
        shard_attn[:, 3 * cols :],
        shard_attn[:, cols : 2 * cols].T,
        jnp.concatenate([v[:, :units] for v in shards], axis=1),
        jnp.concatenate([v[:, units:] for v in shards], axis=1).T,
        norm_sums[0],
        norm_sums[1],
        norm_sums[2],
        norm_sums[3],
        ssm_inject * ssm_readout * dtotal,
        ssm_readout * total,
        ssm_inject * total,
    )


def solution(mesh):
    return jax.shard_map(
        functools.partial(per_device, mesh.shape["dp"]),
        mesh=mesh,
        in_specs=(
            P(None, "dp", "tensor", None),
            P(None, "dp", None),
            P("dp", "tensor"),
            P("dp", "tensor"),
            P("dp", "tensor"),
            P("dp", "tensor"),
            P("tensor", "dp"),
            P("dp", "tensor"),
            P("tensor", "dp"),
            P("dp"),
            P("dp"),
            P("dp"),
            P("dp"),
            P(None, "tensor"),
            P(None, "tensor"),
            P(None, "tensor"),
            P(None, "dp", "tensor", None),
        ),
        out_specs=(
            P(None, "dp", "tensor", None),
            P(None, "dp", "tensor", None),
            P("dp", "tensor"),
            P("dp", "tensor"),
            P("dp", "tensor"),
            P("dp", "tensor"),
            P("tensor", "dp"),
            P("dp", "tensor"),
            P("tensor", "dp"),
            P("dp"),
            P("dp"),
            P("dp"),
            P("dp"),
            P(None, "tensor"),
            P(None, "tensor"),
            P(None, "tensor"),
        ),
        check_vma=False,
    )
```

```python
import functools
import math

import jax
import jax.numpy as jnp
from jax import lax
from jax.experimental import pallas as pl
from jax.experimental.pallas import tpu as pltpu
from jax.sharding import PartitionSpec as P

HEAD_DIM = 128
BLOCK = 512
CTX = 128
NDOCS = 8
LANES = 128
QTILE = 256
HEADS_EACH = 2
CUT = 4

norm_eps = 1e-05
masked_score = -1e30
VMEM = 56 * 1024 * 1024
BF = jnp.bfloat16
F32 = jnp.float32


def dot_plain(left_op, right_op):
    return jnp.dot(left_op, right_op, preferred_element_type=F32)


def dot_last(left_op, right_op):
    return lax.dot_general(left_op, right_op, (((1,), (1,)), ((), ())), preferred_element_type=F32)


def dot_first(left_op, right_op):
    return lax.dot_general(left_op, right_op, (((0,), (0,)), ((), ())), preferred_element_type=F32)


def params(count=1):
    return pltpu.CompilerParams(
        dimension_semantics=("arbitrary",) * count, vmem_limit_bytes=VMEM
    )


def bits_of(count):
    out = []
    bit = 1
    while bit < count:
        out.append(bit)
        bit *= 2
    return out


def groups_of(count, low_groups):
    high = bits_of(count)[2:]
    return [tuple(high[k : k + 2]) for k in range(0, len(high), 2)] + [
        tuple(b for b in g if b < count) for g in low_groups
    ]


X_FIRST = ((1,), (2,))
Y_FIRST = ((2,), (1,))
DIRECT = ((1, 2),)


def swap(values, count, mask):
    return lax.ppermute(values, "dp", [(i, i ^ mask) for i in range(count)])


def tie(*trees):
    return lax.optimization_barrier(trees)


def in_order(upper, own, got, axis):
    return jnp.where(
        upper, jnp.stack([got, own], axis=axis), jnp.stack([own, got], axis=axis)
    )


class Gather:
    def __init__(self, shard, count, index, low):
        self.values, self.count, self.index = shard, count, index
        self.shape = (count * shard.shape[0],) + shard.shape[1:]
        self.left = groups_of(count, low)
        self.present = []
        self.loose = False
        self.last = None

    def send(self):
        self.got = [swap(self.values, self.count, m) for m in masks_of(self.left[0])]

    def merge(self):
        pieces = [self.values] + list(self.got)
        if self.loose and len(self.left) == 1:
            self.last = self.left.pop()[0]
            self.values = pieces
            return
        for bit in self.left.pop(0):
            place = 0 if self.loose else sum(1 for p in self.present if p > bit)
            self.present.insert(place, bit)
            upper = (self.index // bit) % 2 == 1
            pieces = [
                in_order(upper, pieces[k], pieces[k + 1], place)
                for k in range(0, len(pieces), 2)
            ]
        self.values = pieces[0]

    def split(self, lows, loose=False):
        cols = self.values.shape[-1] // 2
        out = []
        for k, low in enumerate(lows):
            part = Gather.__new__(Gather)
            part.count, part.index, part.present = self.count, self.index, list(self.present)
            part.values = self.values[..., k * cols : (k + 1) * cols]
            part.shape = self.shape[:-1] + (cols,)
            part.left = self.left[: -len(lows)] + list(low)
            part.last = None
            part.loose = loose and self.shape[0] // self.count % 16 == 0
            out.append(part)
        return out

    def result(self):
        return self.values.reshape(self.shape)

    def parts(self):
        if self.last is None:
            return [self.result()], ((0,), 0), jnp.int32(0)
        half = (self.shape[0] // 2,) + self.shape[1:]
        blocks = [0]
        for bit in self.present[::-1]:
            blocks = blocks + [b + bit for b in blocks]
        return (
            [v.reshape(half) for v in self.values],
            (tuple(blocks), self.last),
            (self.index // self.last) % 2,
        )


def masks_of(group):
    return [group[0]] if len(group) == 1 else [group[0], group[1], group[0] | group[1]]


class Scatter:
    def __init__(self, full, count, index, low, singly=False):
        bits = bits_of(count)
        self.values = full.reshape((2,) * len(bits) + (full.shape[0] // count,) + full.shape[1:])
        self.count, self.index = count, index
        self.present = sorted(bits, reverse=True)
        self.left = groups_of(count, low)[::-1]
        if singly:
            self.left = [(b,) for group in self.left for b in group[::-1]]

    def block(self, group, mask):
        values, present = self.values, list(self.present)
        for bit in group:
            place = present.index(bit)
            digit = ((self.index ^ mask) // bit) % 2
            values = lax.dynamic_index_in_dim(values, digit, place, keepdims=False)
            present.remove(bit)
        return values

    def send(self):
        group = self.left[0]
        self.got = [swap(self.block(group, m), self.count, m) for m in masks_of(group)]

    def merge(self):
        group = self.left.pop(0)
        total = self.block(group, 0).astype(F32)
        for got in self.got:
            total = total + got.astype(F32)
        for bit in group:
            self.present.remove(bit)
        self.values = total.astype(BF) if self.present else total

    def result(self):
        return self.values


class Total:
    def __init__(self, values, count):
        self.values, self.count = values, count
        self.left = groups_of(count, DIRECT)[::-1]

    def send(self):
        self.got = [swap(self.values, self.count, m) for m in masks_of(self.left[0])]

    def merge(self):
        self.left.pop(0)
        total = self.values + self.got[0]
        if len(self.got) > 1:
            total = total + (self.got[1] + self.got[2])
        self.values = total


def send(chains, *gates):
    chains = [c for c in chains if c.left]
    held = tie([c.values for c in chains], gates)[0]
    for c, v in zip(chains, held):
        c.values = v
    for c in chains:
        c.send()


def fence(chains, *values):
    chains = [c for c in chains if c.left]
    held, values = tie([(c.values, c.got) for c in chains], values)
    for c, (v, g) in zip(chains, held):
        c.values, c.got = v, g
        c.merge()
    held, values = tie(marks(chains), values)
    for c, v in zip(chains, held):
        c.values = v
    return values if len(values) != 1 else values[0]


def step(chains, *gates):
    send(chains, *gates)
    fence(chains)


def complete(chains):
    while any(c.left for c in chains):
        step(chains)


def join_chains(chains):
    chains[0].values = jnp.concatenate([c.values for c in chains], axis=-1)
    del chains[1:]


def marks(chains):
    return [c.values for c in chains]


def pair(values):
    return lax.ppermute(values, "tensor", [(0, 1), (1, 0)])


def norm_of(values, gain_vec, bias_vec):
    centred = values - jnp.mean(values, axis=-1, keepdims=True)
    inverse = lax.rsqrt(jnp.mean(centred * centred, axis=-1, keepdims=True) + norm_eps)
    return centred * inverse * gain_vec + bias_vec


def to_steps(steps_ref, row_first, values, col_first):
    rows, cols = values.shape
    tiles = steps_ref.shape[1]
    for j in range(cols // LANES):
        steps_ref[pl.ds(row_first, rows), col_first // LANES + j, :] = values[
            :, j * LANES : (j + 1) * LANES
        ]


def run_docs(starts_ref, low, high, one_step, make_start, finish, backward, unroll=8):
    for doc in range(NDOCS):
        d = NDOCS - 1 - doc if backward else doc
        first = jnp.minimum(jnp.maximum(starts_ref[d], low), high)
        last = jnp.minimum(jnp.maximum(starts_ref[d + 1], low), high)
        length = last - first
        groups = length // unroll
        carry = make_start(d)

        def group_body(g, carry):
            base = last - 1 - g * unroll if backward else first + g * unroll
            for i in range(unroll):
                carry = one_step(base - i if backward else base + i, carry)
            return carry

        carry = lax.fori_loop(0, groups, group_body, carry)
        done = groups * unroll

        def one_body(i, carry):
            return one_step(last - 1 - done - i if backward else first + done + i, carry)

        carry = lax.fori_loop(0, length - done, one_body, carry)
        finish(d, length, carry)


def add_up(parts):
    while len(parts) > 1:
        parts = [parts[k] + parts[k + 1] for k in range(0, len(parts), 2)]
    return parts[0]


def scan_states(starts_ref, low, high, drive_ref, decay_ref, coef_ref, y_ref, start_ref, end_ref):
    states = decay_ref.shape[0]
    zero = jnp.zeros(decay_ref.shape[1:], F32)

    def one_step(t, state):
        u = drive_ref[t]
        new = [decay_ref[n] * state[n] + u for n in range(states)]
        y_ref[t - low] = add_up([coef_ref[n] * new[n] for n in range(states)])
        return tuple(new)

    def make_start(d):
        if start_ref is None:
            return (zero,) * states
        going = starts_ref[d] < low
        return tuple(jnp.where(going, start_ref[n], zero) for n in range(states))

    def finish(d, length, carry):
        if end_ref is not None:

            @pl.when(length > 0)
            def _():
                for n in range(states):
                    end_ref[n] = carry[n]

    run_docs(starts_ref, low, high, one_step, make_start, finish, False)


def from_steps(steps_ref, out_ref):
    length, tiles, _ = steps_ref.shape
    chunk = 256

    def write(i, _):
        r = pl.multiple_of(i * chunk, chunk)
        for j in range(tiles):
            out_ref[pl.ds(r, chunk), j * LANES : (j + 1) * LANES] = steps_ref[
                pl.ds(r, chunk), j, :
            ].astype(BF)
        return 0

    lax.fori_loop(0, length // chunk, write, 0)


def both_parts(own, other, joined, at, sems):
    copies = [
        pltpu.make_async_copy(own, joined.at[at(0)], sems.at[0]),
        pltpu.make_async_copy(other, joined.at[at(1)], sems.at[1]),
    ]
    for copy in copies:
        copy.start()
    return copies


def cols_at(side, cols):
    return lambda k: (
        slice(None),
        pl.ds(pl.multiple_of((side if k == 0 else 1 - side) * cols, cols), cols),
    )


def rows_at(side, rows, *lead):
    return lambda k: lead + (
        pl.ds(pl.multiple_of((side if k == 0 else 1 - side) * rows, rows), rows),
    )


def wait_all(copies):
    for copy in copies:
        copy.wait()


def ssm_forward_kernel(
    starts_ref, side_ref, mine_ref, got_ref, mix_own_ref, mix_other_ref, gain_ref, bias_ref, decay_ref, coef_ref,
    rows_out_ref, normed_out_ref, drive_out_ref, out_ref, end_ref,
    y_ref, mix_ref, rows_ref, normed_ref, drive_ref, sems, out_sems,
):
    length, width = rows_ref.shape
    side = side_ref[0]
    copies = both_parts(
        mine_ref.at[side], got_ref.at[side], rows_ref, rows_at(side, length // 2), sems.at[0]
    ) + both_parts(
        mix_own_ref, mix_other_ref, mix_ref, cols_at(side, width // 2), sems.at[1]
    )
    wait_all(copies)
    chunk = 256

    def project(i, _):
        r = pl.multiple_of(i * chunk, chunk)
        normed = norm_of(
            rows_ref[pl.ds(r, chunk), :].astype(F32), gain_ref[...], bias_ref[...]
        ).astype(BF)
        normed_ref[pl.ds(r, chunk), :] = normed
        for c in range(0, width, 256):
            to_steps(drive_ref, r, dot_plain(normed, mix_ref[:, c : c + 256]), c)
        return 0

    lax.fori_loop(0, length // chunk, project, 0)
    stores = [
        pltpu.make_async_copy(held, out, out_sems.at[k])
        for k, (held, out) in enumerate(
            ((drive_ref, drive_out_ref), (normed_ref, normed_out_ref), (rows_ref, rows_out_ref))
        )
    ]
    for store in stores:
        store.start()
    scan_states(
        starts_ref, 0, length // CUT, drive_ref, decay_ref, coef_ref, y_ref, None, end_ref
    )
    from_steps(y_ref, out_ref)
    wait_all(stores)


def ssm_rest_kernel(
    starts_ref, side_ref, mine_ref, got_ref, drive_ref, decay_ref, coef_ref, start_ref, first_ref,
    out_ref, cot_ref, y_ref, sems,
):
    length = drive_ref.shape[0]
    half = length // 2
    cut = length // CUT
    side = side_ref[0]
    copies = both_parts(
        mine_ref.at[side], got_ref.at[side], cot_ref, rows_at(side, half, 0), sems.at[0]
    ) + both_parts(
        mine_ref.at[1 - side], got_ref.at[1 - side], cot_ref, rows_at(side, half, 1), sems.at[1]
    )
    scan_states(
        starts_ref, cut, length, drive_ref, decay_ref, coef_ref, y_ref, start_ref, None
    )
    out_ref[:cut, :] = first_ref[...]
    from_steps(y_ref, out_ref.at[cut:])
    wait_all(copies)


SMALL = pl.BlockSpec(memory_space=pltpu.SMEM)
WHOLE = pl.BlockSpec(memory_space=pltpu.VMEM)
ANYWHERE = pl.BlockSpec(memory_space=pl.ANY)
COPIES = pltpu.SemaphoreType.DMA((2, 2))


def ssm_forward(starts, side, mine, got, mix_own, mix_other, gain_vec, bias_vec, decay, coef):
    length, width = 2 * mine.shape[1], mine.shape[2]
    tiles = width // LANES
    return pl.pallas_call(
        ssm_forward_kernel,
        out_shape=(
            jax.ShapeDtypeStruct((length, width), BF),
            jax.ShapeDtypeStruct((length, width), BF),
            jax.ShapeDtypeStruct((length, tiles, LANES), F32),
            jax.ShapeDtypeStruct((length // CUT, width), BF),
            jax.ShapeDtypeStruct(decay.shape, F32),
        ),
        in_specs=[SMALL] * 2 + [ANYWHERE] * 4 + [WHOLE] * 4,
        out_specs=(ANYWHERE,) * 3 + (WHOLE,) * 2,
        scratch_shapes=[
            pltpu.VMEM((length // CUT, tiles, LANES), F32),
            pltpu.VMEM((width, width), BF),
            pltpu.VMEM((length, width), BF),
            pltpu.VMEM((length, width), BF),
            pltpu.VMEM((length, tiles, LANES), F32),
            COPIES,
            pltpu.SemaphoreType.DMA((3,)),
        ],
        compiler_params=pltpu.CompilerParams(vmem_limit_bytes=VMEM),
        cost_estimate=pl.CostEstimate(
            flops=12 * length * width * width,
            bytes_accessed=16 * length * width,
            transcendentals=0,
        ),
        name="ssm_forward",
    )(starts, side, mine, got, mix_own, mix_other, gain_vec, bias_vec, decay, coef)


def ssm_rest(starts, side, mine, got, drive, decay, coef, start, first):
    length, tiles, _ = drive.shape
    width = tiles * LANES
    return pl.pallas_call(
        ssm_rest_kernel,
        out_shape=(
            jax.ShapeDtypeStruct((length, width), BF),
            jax.ShapeDtypeStruct((2, length, width), BF),
        ),
        in_specs=[SMALL] * 2 + [ANYWHERE] * 2 + [WHOLE] * 5,
        out_specs=(WHOLE, WHOLE),
        scratch_shapes=[pltpu.VMEM((length - length // CUT, tiles, LANES), F32), COPIES],
        compiler_params=pltpu.CompilerParams(vmem_limit_bytes=VMEM),
        cost_estimate=pl.CostEstimate(
            flops=10 * length * width * width,
            bytes_accessed=16 * length * width,
            transcendentals=0,
        ),
        name="ssm_rest",
    )(starts, side, mine, got, drive, decay, coef, start, first)


def project_kernel(
    side_ref, normed_ref, ssm_ref, left_own_ref, left_other_ref, right_own_ref, right_other_ref,
    query_ref, key_ref, value_ref, rows_ref, weights_ref, held_ref, row_sems, sems, out_sems,
):
    width = normed_ref.shape[1]
    cols = width // 2
    at = cols_at(side_ref[0], cols)
    sources = (
        (left_own_ref, left_other_ref, 0),
        (left_own_ref, left_other_ref, cols),
        (right_own_ref, right_other_ref, 0),
    )
    loads = [
        pltpu.make_async_copy(ref, rows_ref.at[k], row_sems.at[k])
        for k, ref in enumerate((normed_ref, ssm_ref))
    ]
    copies = []
    for k, (own, other, c) in enumerate(sources):
        if k < 2:
            loads[k].start()
        copies.append(
            both_parts(
                own.at[:, c : c + cols], other.at[:, c : c + cols], weights_ref.at[k], at, sems.at[k]
            )
        )
    stores = []
    for k, (row, out_ref) in enumerate(((0, query_ref), (1, key_ref), (1, value_ref))):
        if k < 2:
            loads[k].wait()
        wait_all(copies[k])
        for h, c in enumerate(range(0, width, cols)):
            held_ref[k, :, c : c + cols] = dot_plain(
                rows_ref[row], weights_ref[k, :, c : c + cols]
            ).astype(BF)
            store = pltpu.make_async_copy(
                held_ref.at[k, :, c : c + cols], out_ref.at[:, c : c + cols], out_sems.at[k, h]
            )
            store.start()
            stores.append(store)
    wait_all(stores)


def project(side, normed, ssm_out, left, right):
    length, width = normed.shape
    return pl.pallas_call(
        project_kernel,
        out_shape=(jax.ShapeDtypeStruct((length, width), BF),) * 3,
        in_specs=[SMALL] + [ANYWHERE] * 6,
        out_specs=(ANYWHERE,) * 3,
        scratch_shapes=[
            pltpu.VMEM((2, length, width), BF),
            pltpu.VMEM((3, width, width), BF),
            pltpu.VMEM((3, length, width), BF),
            pltpu.SemaphoreType.DMA((2,)),
            pltpu.SemaphoreType.DMA((3, 2)),
            pltpu.SemaphoreType.DMA((3, 2)),
        ],
        compiler_params=pltpu.CompilerParams(vmem_limit_bytes=VMEM),
        cost_estimate=pl.CostEstimate(
            flops=6 * length * width * width, bytes_accessed=16 * length * width, transcendentals=0
        ),
        name="project",
    )(side, normed, ssm_out, *left, *right)


def adjoint_states(starts_ref, low, drive_ref, g_ref, decay_ref, coef_ref, gm_ref, sum_ref, dsum_ref, given_ref):
    length = g_ref.shape[0]
    part = sum_ref.shape[0]
    zero = jnp.zeros(decay_ref.shape[1:], F32)

    def one_step(t, carry):
        mu, rho, total, dtotal = carry
        u = drive_ref[t]
        g = g_ref[t]
        new_mu, new_rho, new_total, new_dtotal, parts = [], [], [], [], []
        for n in range(part):
            a = decay_ref[low + n]
            r = a * rho[n] + mu[n]
            m = a * mu[n] + g
            new_mu.append(m)
            new_rho.append(r)
            new_total.append(total[n] + u * m)
            new_dtotal.append(dtotal[n] + u * r)
            parts.append(coef_ref[low + n] * m)
        gm = add_up(parts)
        gm_ref[t] = gm if given_ref is None else gm + given_ref[t]
        return tuple(new_mu), tuple(new_rho), tuple(new_total), tuple(new_dtotal)

    for n in range(part):
        sum_ref[n] = zero
        dsum_ref[n] = zero

    def make_start(d):
        zeros = (zero,) * part
        return zeros, zeros, zeros, zeros

    def finish(d, count, carry):
        for n in range(part):
            sum_ref[n] = sum_ref[n] + carry[2][n]
            dsum_ref[n] = dsum_ref[n] + carry[3][n]

    run_docs(starts_ref, 0, length, one_step, make_start, finish, True)


def ssm_backward_kernel(
    starts_ref, side_ref, gkey_in_ref, gvalue_in_ref, left_own_ref, left_other_ref, right_own_ref, right_other_ref,
    drive_in_ref, decay_ref, coef_ref, gmixed_ref, sum_ref, dsum_ref,
    g_ref, gm_ref, wkey_ref, wvalue_ref, gkey_ref, gvalue_ref, drive_ref, sems, in_sems,
):
    length, width = gkey_ref.shape
    cols = width // 2
    loads = [
        pltpu.make_async_copy(source, held, in_sems.at[k])
        for k, (source, held) in enumerate(
            ((gkey_in_ref, gkey_ref), (gvalue_in_ref, gvalue_ref), (drive_in_ref, drive_ref))
        )
    ]
    for load in loads[:2]:
        load.start()
    at = cols_at(side_ref[0], cols)
    copies = both_parts(
        left_own_ref.at[:, cols:], left_other_ref.at[:, cols:], wkey_ref, at, sems.at[0]
    ) + both_parts(
        right_own_ref.at[:, :cols], right_other_ref.at[:, :cols], wvalue_ref, at, sems.at[1]
    )
    loads[2].start()
    wait_all(copies + loads[:2])
    chunk = 256

    def project(i, _):
        r = pl.multiple_of(i * chunk, chunk)
        gkey = gkey_ref[pl.ds(r, chunk), :]
        gvalue = gvalue_ref[pl.ds(r, chunk), :]
        for c in range(0, width, 256):
            to_steps(
                g_ref,
                r,
                dot_last(gkey, wkey_ref[c : c + 256, :])
                + dot_last(gvalue, wvalue_ref[c : c + 256, :]),
                c,
            )
        return 0

    lax.fori_loop(0, length // chunk, project, 0)
    loads[2].wait()
    part = decay_ref.shape[0] // 2
    for k in range(2):
        mine = pl.ds(k * part, part)
        adjoint_states(
            starts_ref, k * part, drive_ref, g_ref, decay_ref, coef_ref, gm_ref,
            sum_ref.at[mine], dsum_ref.at[mine], gm_ref if k else None,
        )
    from_steps(gm_ref, gmixed_ref)


def ssm_backward(starts, side, gkey, gvalue, left, right, drive, decay, coef):
    length, width = gkey.shape
    tiles = width // LANES
    return pl.pallas_call(
        ssm_backward_kernel,
        out_shape=(
            jax.ShapeDtypeStruct((length, width), BF),
            jax.ShapeDtypeStruct(decay.shape, F32),
            jax.ShapeDtypeStruct(decay.shape, F32),
        ),
        in_specs=[SMALL] * 2 + [ANYWHERE] * 7 + [WHOLE] * 2,
        out_specs=(WHOLE,) * 3,
        scratch_shapes=[pltpu.VMEM((length, tiles, LANES), F32)] * 2
        + [pltpu.VMEM((width, width), BF)] * 2
        + [pltpu.VMEM((length, width), BF)] * 2
        + [pltpu.VMEM((length, tiles, LANES), F32), COPIES, pltpu.SemaphoreType.DMA((3,))],
        compiler_params=pltpu.CompilerParams(vmem_limit_bytes=VMEM),
        cost_estimate=pl.CostEstimate(
            flops=40 * length * width * width,
            bytes_accessed=20 * length * width,
            transcendentals=0,
        ),
        name="ssm_backward",
    )(starts, side, gkey, gvalue, *left, *right, drive, decay, coef)


def attention_tiles(length):
    tiles = []
    for first in range(0, length, QTILE):
        block_first = first // BLOCK * BLOCK
        key_first = max(0, block_first - CTX)
        tiles.append((first, key_first, first + QTILE - key_first))
    return tiles


def fill_bias(seg_col_ref, seg_row_ref, bias_ref, tiles):
    at = 0
    for first, key_first, count in tiles:
        same = seg_col_ref[first : first + QTILE, :] == seg_row_ref[:, key_first : key_first + count]
        query_pos = lax.broadcasted_iota(jnp.int32, (QTILE, count), 0) + first
        key_pos = lax.broadcasted_iota(jnp.int32, (QTILE, count), 1) + key_first
        bias_ref[:, at : at + count] = jnp.where(
            same & (key_pos <= query_pos), 0.0, masked_score
        ).astype(F32)
        at += count


EXP_SCALE = HEAD_DIM ** (-0.5) * math.log2(math.e)


def attention_jobs(length):
    jobs = []
    for h in range(HEADS_EACH):
        at = 0
        for first, key_first, count in attention_tiles(length):
            jobs.append(
                (
                    h,
                    slice(h * HEAD_DIM, (h + 1) * HEAD_DIM),
                    slice(first, first + QTILE),
                    slice(key_first, key_first + count),
                    slice(at, at + count),
                )
            )
            at += count
    return jobs


def attention_forward_kernel(
    seg_col_ref, seg_row_ref, query_ref, key_ref, value_ref, out_ref, lse_ref, bias_ref, value_one_ref
):
    length = query_ref.shape[0]

    @pl.when(pl.program_id(0) == 0)
    def _():
        fill_bias(seg_col_ref, seg_row_ref, bias_ref, attention_tiles(length))
        for h in range(HEADS_EACH):
            value_one_ref[h, :, HEAD_DIM:] = jnp.ones((length, HEAD_DIM), BF)

    for h in range(HEADS_EACH):
        value_one_ref[h, :, :HEAD_DIM] = value_ref[:, h * HEAD_DIM : (h + 1) * HEAD_DIM]
    jobs = attention_jobs(length)

    def scores_of(job):
        _, lanes, rows, keys, _ = job
        return dot_last(query_ref[rows, lanes], key_ref[keys, lanes])

    ahead = scores_of(jobs[0])
    for k, (h, lanes, rows, keys, mask) in enumerate(jobs):
        scores = ahead
        if k + 1 < len(jobs):
            ahead = scores_of(jobs[k + 1])
        scores = scores * EXP_SCALE + bias_ref[:, mask]
        top = jnp.max(scores, axis=-1, keepdims=True)
        raised = jnp.exp2(scores - top).astype(BF)
        both = dot_plain(raised, value_one_ref[h, keys, :])
        total = both[:, HEAD_DIM:]
        out_ref[rows, lanes] = (both[:, :HEAD_DIM] / total).astype(BF)
        lse_ref[h, rows, :] = top + jnp.log2(total[:, :1])


def attention_forward(seg_col, seg_row, query, key, value):
    length, width = query.shape
    heads = width // HEAD_DIM
    tiles = attention_tiles(length)
    cols = sum(t[2] for t in tiles)
    head = pl.BlockSpec((length, HEADS_EACH * HEAD_DIM), lambda h: (0, h))
    whole = lambda shape: pl.BlockSpec(shape, lambda h: (0, 0))
    return pl.pallas_call(
        attention_forward_kernel,
        grid=(heads // HEADS_EACH,),
        out_shape=(
            jax.ShapeDtypeStruct((length, width), BF),
            jax.ShapeDtypeStruct((heads, length, 1), F32),
        ),
        in_specs=[whole((length, 1)), whole((1, length)), head, head, head],
        out_specs=(head, pl.BlockSpec((HEADS_EACH, length, 1), lambda h: (h, 0, 0))),
        scratch_shapes=[
            pltpu.VMEM((QTILE, cols), F32),
            pltpu.VMEM((HEADS_EACH, length, 2 * HEAD_DIM), BF),
        ],
        compiler_params=params(),
        cost_estimate=pl.CostEstimate(
            flops=4 * QTILE * cols * width,
            bytes_accessed=8 * length * width,
            transcendentals=QTILE * cols * heads,
        ),
        name="attention_forward",
    )(seg_col, seg_row, query, key, value)


def attention_backward_kernel(
    seg_col_ref, seg_row_ref, query_ref, key_ref, value_ref, lse_ref, gout_ref,
    gquery_ref, gkey_ref, gvalue_ref, bias_ref, gk_ref, gv_ref,
):
    length = query_ref.shape[0]
    scale = HEAD_DIM ** (-0.5)

    @pl.when(pl.program_id(0) == 0)
    def _():
        fill_bias(seg_col_ref, seg_row_ref, bias_ref, attention_tiles(length))

    gk_ref[...] = jnp.zeros_like(gk_ref)
    gv_ref[...] = jnp.zeros_like(gv_ref)
    jobs = attention_jobs(length)

    def scores_of(job):
        _, lanes, rows, keys, _ = job
        return (
            dot_last(query_ref[rows, lanes], key_ref[keys, lanes]),
            dot_last(gout_ref[rows, lanes], value_ref[keys, lanes]),
        )

    ahead = scores_of(jobs[0])
    for k, (h, lanes, rows, keys, mask) in enumerate(jobs):
        scores, gprobs = ahead
        if k + 1 < len(jobs):
            ahead = scores_of(jobs[k + 1])
        gout = gout_ref[rows, lanes]
        probs = jnp.exp2(scores * EXP_SCALE + bias_ref[:, mask] - lse_ref[h, rows, :])
        gv_ref[keys, lanes] = gv_ref[keys, lanes] + dot_first(probs.astype(BF), gout)
        inner = jnp.sum(probs * gprobs, axis=-1, keepdims=True)
        gscores = (probs * (gprobs - inner)).astype(BF)
        gquery_ref[rows, lanes] = (dot_plain(gscores, key_ref[keys, lanes]) * scale).astype(BF)
        gk_ref[keys, lanes] = gk_ref[keys, lanes] + dot_first(gscores, query_ref[rows, lanes])
    gkey_ref[...] = (gk_ref[...] * scale).astype(BF)
    gvalue_ref[...] = gv_ref[...].astype(BF)


def attention_backward(seg_col, seg_row, query, key, value, lse, gout):
    length, width = query.shape
    heads = width // HEAD_DIM
    tiles = attention_tiles(length)
    cols = sum(t[2] for t in tiles)
    head = pl.BlockSpec((length, HEADS_EACH * HEAD_DIM), lambda h: (0, h))
    whole = lambda shape: pl.BlockSpec(shape, lambda h: (0, 0))
    return pl.pallas_call(
        attention_backward_kernel,
        grid=(heads // HEADS_EACH,),
        out_shape=(jax.ShapeDtypeStruct((length, width), BF),) * 3,
        in_specs=[whole((length, 1)), whole((1, length)), head, head, head]
        + [pl.BlockSpec((HEADS_EACH, length, 1), lambda h: (h, 0, 0)), head],
        out_specs=(head,) * 3,
        scratch_shapes=[
            pltpu.VMEM((QTILE, cols), F32),
            pltpu.VMEM((length, HEADS_EACH * HEAD_DIM), F32),
            pltpu.VMEM((length, HEADS_EACH * HEAD_DIM), F32),
        ],
        compiler_params=params(),
        cost_estimate=pl.CostEstimate(
            flops=10 * QTILE * cols * width,
            bytes_accessed=14 * length * width,
            transcendentals=QTILE * cols * heads,
        ),
        name="attention_backward",
    )(seg_col, seg_row, query, key, value, lse, gout)


def norm_backward(grad, values, gain_vec):
    centred = values - jnp.mean(values, axis=-1, keepdims=True)
    inverse = lax.rsqrt(jnp.mean(centred * centred, axis=-1, keepdims=True) + norm_eps)
    xhat = centred * inverse
    dxhat = grad * gain_vec
    back = (
        dxhat
        - jnp.mean(dxhat, axis=-1, keepdims=True)
        - xhat * jnp.mean(dxhat * xhat, axis=-1, keepdims=True)
    ) * inverse
    return back, jnp.sum(grad * xhat, axis=0, keepdims=True), jnp.sum(grad, axis=0, keepdims=True)


def gelu_parts(values):
    below = 0.5 + 0.5 * lax.erf(values * (2.0**-0.5))
    bell = jnp.exp2((-0.5 * math.log2(math.e)) * (values * values))
    return values * below, below + values * (bell * ((2.0 * math.pi) ** -0.5))


FTILE = 512


def feed_forward_kernel(part, blocks, place_ref, own_ref, other_ref, cot_ref, *refs):
    pieces, refs = refs[: sum(b[0] for b in blocks)], refs[sum(b[0] for b in blocks) :]
    ins, refs = refs[: 4 * part], refs[4 * part :]
    outs, grads, refs = refs[:4], refs[4:6], refs[6:]
    normed_ref, cots_ref, up_ref, down_ref, hidden_ref, gpre_ref, sums_ref, total_ref = refs[:8]
    row_sems, weight_sems, out_sems, grad_sems = refs[8:12]
    length, width = own_ref.shape
    units = up_ref.shape[1]
    tile = FTILE
    per = length // tile
    count = 2 * per

    def tile_of(i):
        return pl.ds(pl.multiple_of(i * tile, tile), tile)

    weights = []
    for k, (ref, (number, (places, last))) in enumerate(zip((up_ref, down_ref), blocks)):
        rows = ref.shape[0] // (number * len(places))
        for p in range(number):
            source = pieces[k * blocks[0][0] + p]
            place = place_ref[k] if p == 0 else 1 - place_ref[k]
            for h, at in enumerate(places):
                pltpu.make_async_copy(
                    source.at[pl.ds(h * rows, rows)],
                    ref.at[pl.ds(pl.multiple_of((at + place * last) * rows, rows), rows)],
                    weight_sems.at[k],
                ).start()
        weights.append(pltpu.make_async_copy(ref, ref, weight_sems.at[k]))
    for i in range(count):
        rows = tile_of(i % per)
        source = (own_ref, other_ref)[i // per]
        pltpu.make_async_copy(source.at[rows], normed_ref.at[tile_of(i)], row_sems.at[0, i]).start()
        pltpu.make_async_copy(
            cot_ref.at[i // per, rows], cots_ref.at[tile_of(i)], row_sems.at[1, i]
        ).start()
    if part:
        earlier = [
            pltpu.make_async_copy(ins[k], total_ref.at[k], out_sems.at[k, count])
            for k in range(4)
        ]
        for copy in earlier:
            copy.start()
    wait_all(weights)

    def one(i, _):
        rows = tile_of(i)
        for k, ref in enumerate((normed_ref, cots_ref)):
            pltpu.make_async_copy(ref.at[rows], ref.at[rows], row_sems.at[k, i]).wait()
        for n in range(0, units, tile):
            pre = dot_plain(normed_ref[rows, :], up_ref[:, n : n + tile])
            ghidden = dot_plain(cots_ref[rows, :], down_ref[:, n : n + tile])
            hidden, slope = gelu_parts(pre)
            hidden_ref[rows, n : n + tile] = hidden.astype(BF)
            gpre_ref[rows, n : n + tile] = (ghidden * slope).astype(BF)
        return 0

    lax.fori_loop(0, count, one, 0)

    grad_copies = []
    for k, (first_ref, held_ref) in enumerate(((normed_ref, gpre_ref), (cots_ref, hidden_ref))):

        def three(i, _, k=k, first_ref=first_ref, held_ref=held_ref):
            cols = tile_of(i)
            sums_ref[k, cols, :] = dot_first(first_ref[:, cols], held_ref[...]).astype(BF)
            return 0

        lax.fori_loop(0, width // tile, three, 0)
        copy = pltpu.make_async_copy(
            sums_ref.at[k], grads[k], grad_sems.at[k]
        )
        copy.start()
        grad_copies.append(copy)

    if part:
        wait_all(earlier)
    out_copies = []
    for i in range(count):
        s, rows = i // per, slice(i % per * tile, (i % per + 1) * tile)
        held = slice(i * tile, (i + 1) * tile)
        for k, (held_ref, weight_ref) in enumerate(((hidden_ref, down_ref), (gpre_ref, up_ref))):
            total = dot_last(held_ref[held, :], weight_ref[...])
            if part:
                total = total + total_ref[2 * k + s, rows, :].astype(F32)
            total_ref[2 * k + s, rows, :] = total.astype(BF)
            copy = pltpu.make_async_copy(
                total_ref.at[2 * k + s, rows], outs[2 * k + s].at[rows], out_sems.at[k, i]
            )
            copy.start()
            out_copies.append(copy)
    wait_all(grad_copies + out_copies)


def feed_forward(part, own, other, cot, up, down, earlier):
    length, width = own.shape
    pieces, blocks, places = zip(*(chain.parts() for chain in (up, down)))
    blocks = tuple((len(p), b) for p, b in zip(pieces, blocks))
    pieces = [p for each in pieces for p in each]
    units = pieces[0].shape[1]
    count = 2 * length // FTILE
    dma = pltpu.SemaphoreType.DMA
    return pl.pallas_call(
        functools.partial(feed_forward_kernel, part, blocks),
        out_shape=(jax.ShapeDtypeStruct((length, width), BF),) * 4
        + (jax.ShapeDtypeStruct((width, units), BF),) * 2,
        in_specs=[SMALL] + [ANYWHERE] * (3 + len(pieces) + 4 * part),
        out_specs=(ANYWHERE,) * 6,
        scratch_shapes=[pltpu.VMEM((2 * length, width), BF)] * 2
        + [pltpu.VMEM((width, units), BF)] * 2
        + [pltpu.VMEM((2 * length, units), BF)] * 2
        + [pltpu.VMEM((2, width, units), BF), pltpu.VMEM((4, length, width), BF)]
        + [dma((2, count)), dma((2,)), dma((4, count + 1)), dma((2,))],
        compiler_params=pltpu.CompilerParams(vmem_limit_bytes=VMEM),
        cost_estimate=pl.CostEstimate(
            flops=28 * length * width * units,
            bytes_accessed=48 * length * width,
            transcendentals=4 * length * units,
        ),
        name="feed_forward",
    )(jnp.stack(places), own, other, cot, *pieces, *earlier)


def at_first(joins, sems, side):
    @pl.when(pl.program_id(0) == 0)
    def _():
        copies = []
        for k, (own, other, joined) in enumerate(joins):
            copies += both_parts(own, other, joined, cols_at(side, joined.shape[1] // 2), sems.at[k])
        wait_all(copies)


ROWS = 256


def row_spec(width, lead=None):
    if lead is None:
        return pl.BlockSpec((ROWS, width), lambda i: (i, 0))
    return pl.BlockSpec((None, ROWS, width), lambda i: (lead, i, 0))


def fixed(*shape):
    return pl.BlockSpec(shape, lambda i: (0,) * len(shape))


def middle_kernel(
    side_ref, attended_ref, own_ref, other_ref, rows_ref, gain_ref, bias_ref, middle_ref, normed_ref, out_ref, sems
):
    cols = out_ref.shape[1] // 2
    at_first([(own_ref.at[:, cols:], other_ref.at[:, cols:], out_ref)], sems, side_ref[0])
    middle = rows_ref[...].astype(F32) + dot_last(attended_ref[...], out_ref[...])
    middle_ref[...] = middle
    normed_ref[...] = norm_of(middle, gain_ref[...], bias_ref[...]).astype(BF)


def middle_of(side, attended, right, rows, gain_vec, bias_vec):
    length, width = rows.shape
    row = row_spec(width)
    return pl.pallas_call(
        middle_kernel,
        grid=(length // ROWS,),
        out_shape=(
            jax.ShapeDtypeStruct((length, width), F32),
            jax.ShapeDtypeStruct((length, width), BF),
        ),
        in_specs=[SMALL, row, ANYWHERE, ANYWHERE, row, fixed(1, width), fixed(1, width)],
        out_specs=(row, row),
        scratch_shapes=[pltpu.VMEM((width, width), BF), COPIES],
        compiler_params=params(),
        cost_estimate=pl.CostEstimate(
            flops=2 * length * width * width, bytes_accessed=12 * length * width, transcendentals=0
        ),
        name="middle",
    )(side, attended, *right, rows, gain_vec, bias_vec)


def norm_two_kernel(
    side_ref, mine_ref, theirs_ref, middle_ref, cot_ref, gain_ref, own_ref, other_ref,
    gmiddle_ref, gbranch_ref, gattended_ref, sums_ref, out_ref, sems,
):
    cols = out_ref.shape[1] // 2
    at_first([(own_ref.at[:, cols:], other_ref.at[:, cols:], out_ref)], sems, side_ref[0])
    grad = mine_ref[...].astype(F32) + theirs_ref[...].astype(F32)
    back, gain_sum, bias_sum = norm_backward(grad, middle_ref[...], gain_ref[...])
    gmiddle = cot_ref[...].astype(F32) + back
    gmiddle_ref[...] = gmiddle
    gbranch = gmiddle.astype(BF)
    gbranch_ref[...] = gbranch
    gattended_ref[...] = dot_plain(gbranch, out_ref[...]).astype(BF)
    add_sums(sums_ref, gain_sum, bias_sum)


def add_sums(sums_ref, gain_sum, bias_sum):
    @pl.when(pl.program_id(0) == 0)
    def _():
        sums_ref[...] = jnp.zeros_like(sums_ref)

    sums_ref[0:1, :] = sums_ref[0:1, :] + gain_sum
    sums_ref[1:2, :] = sums_ref[1:2, :] + bias_sum


def norm_two_back(side, mine, theirs, middle, cot, gain_vec, right):
    length, width = middle.shape
    row = row_spec(width)
    return pl.pallas_call(
        norm_two_kernel,
        grid=(length // ROWS,),
        out_shape=(
            jax.ShapeDtypeStruct((length, width), F32),
            jax.ShapeDtypeStruct((length, width), BF),
            jax.ShapeDtypeStruct((length, width), BF),
            jax.ShapeDtypeStruct((2, width), F32),
        ),
        in_specs=[SMALL, row, row, row, row_spec(width, 0), fixed(1, width), ANYWHERE, ANYWHERE],
        out_specs=(row, row, row, fixed(2, width)),
        scratch_shapes=[pltpu.VMEM((width, width), BF), COPIES],
        compiler_params=params(),
        cost_estimate=pl.CostEstimate(
            flops=2 * length * width * width, bytes_accessed=24 * length * width, transcendentals=0
        ),
        name="norm_two_back",
    )(side, mine, theirs, middle, cot, gain_vec, *right)


def norm_one_kernel(
    side_ref, gquery_ref, gmixed_ref, rows_ref, gmiddle_ref, gain_ref,
    left_own_ref, left_other_ref, mix_own_ref, mix_other_ref, grad_ref, sums_ref, query_ref, mix_ref, sems,
):
    cols = query_ref.shape[1] // 2
    at_first(
        [
            (left_own_ref.at[:, :cols], left_other_ref.at[:, :cols], query_ref),
            (mix_own_ref, mix_other_ref, mix_ref),
        ],
        sems,
        side_ref[0],
    )
    grad = dot_last(gquery_ref[...], query_ref[...]) + dot_last(gmixed_ref[...], mix_ref[...])
    back, gain_sum, bias_sum = norm_backward(grad, rows_ref[...].astype(F32), gain_ref[...])
    grad_ref[...] = gmiddle_ref[...] + back
    add_sums(sums_ref, gain_sum, bias_sum)


def norm_one_back(side, gquery, gmixed, rows, gmiddle, gain_vec, left, mix, for_partner):
    length, width = rows.shape
    half = length // 2
    steps = half // ROWS

    def place(side):
        return 1 - side[0] if for_partner else side[0]

    row = pl.BlockSpec((ROWS, width), lambda i, side: (place(side) * steps + i, 0))
    whole = lambda *shape: pl.BlockSpec(shape, lambda i, side: (0,) * len(shape))
    if for_partner:
        out = jax.ShapeDtypeStruct((half, width), F32)
        out_spec = pl.BlockSpec((ROWS, width), lambda i, side: (i, 0))
    else:
        out = jax.ShapeDtypeStruct((2, half, width), F32)
        out_spec = pl.BlockSpec((None, ROWS, width), lambda i, side: (side[0], i, 0))
    return pl.pallas_call(
        norm_one_kernel,
        grid_spec=pltpu.PrefetchScalarGridSpec(
            num_scalar_prefetch=1,
            grid=(steps,),
            in_specs=[row] * 4 + [whole(1, width)] + [ANYWHERE] * 4,
            out_specs=(out_spec, whole(2, width)),
            scratch_shapes=[pltpu.VMEM((width, width), BF)] * 2 + [COPIES],
        ),
        out_shape=(out, jax.ShapeDtypeStruct((2, width), F32)),
        compiler_params=params(),
        cost_estimate=pl.CostEstimate(
            flops=4 * half * width * width, bytes_accessed=20 * half * width, transcendentals=0
        ),
        name="norm_one_back",
    )(side, gquery, gmixed, rows, gmiddle, gain_vec, *left, *mix)


def put_kernel(side_ref, got_ref, given_ref, out_ref):
    out_ref[...] = got_ref[...]


def put(side, got, given):
    half, width = got.shape
    return pl.pallas_call(
        put_kernel,
        grid_spec=pltpu.PrefetchScalarGridSpec(
            num_scalar_prefetch=1,
            grid=(half // ROWS,),
            in_specs=[pl.BlockSpec((ROWS, width), lambda i, side: (i, 0)), ANYWHERE],
            out_specs=pl.BlockSpec((None, ROWS, width), lambda i, side: (1 - side[0], i, 0)),
        ),
        out_shape=jax.ShapeDtypeStruct(given.shape, given.dtype),
        input_output_aliases={2: 0},
        compiler_params=params(),
        name="put",
    )(side, got, given)


def layer_out_kernel(side_ref, middle_ref, own_ref, other_ref, sum_ref, theirs_ref, out_ref):
    side = side_ref[0]
    out_ref[side] = (
        middle_ref[...] + own_ref[...].astype(F32) + theirs_ref[...].astype(F32)
    )
    out_ref[1 - side] = sum_ref[...] + other_ref[...].astype(F32)


def layer_out_of(side, middle, own, other, partner_sum, partner_other):
    length, width = middle.shape
    half = length // 2
    steps = half // ROWS
    mine = pl.BlockSpec((ROWS, width), lambda i, side: (side[0] * steps + i, 0))
    row = pl.BlockSpec((ROWS, width), lambda i, side: (i, 0))
    return pl.pallas_call(
        layer_out_kernel,
        grid_spec=pltpu.PrefetchScalarGridSpec(
            num_scalar_prefetch=1,
            grid=(steps,),
            in_specs=[mine] * 3 + [row] * 2,
            out_specs=pl.BlockSpec((2, ROWS, width), lambda i, side: (0, i, 0)),
        ),
        out_shape=jax.ShapeDtypeStruct((2, half, width), F32),
        compiler_params=params(),
        cost_estimate=pl.CostEstimate(
            flops=4 * half * width, bytes_accessed=24 * half * width, transcendentals=0
        ),
        name="layer_out",
    )(side, middle, own, other, partner_sum, partner_other)


def weight_grads_kernel(count, side_ref, *refs):
    ins, outs, refs = refs[:-6], refs[-6:-4], refs[-4:]
    held_ref, sums_ref, in_sems, out_sems = refs
    lefts = len(ins) - count
    width = held_ref.shape[2]
    cols = width // 2
    side = side_ref[0]
    order = []
    for k in range(count):
        order += [k % lefts, lefts + k]
    order = list(dict.fromkeys(order))
    loads = {
        j: pltpu.make_async_copy(ins[j], held_ref.at[j], in_sems.at[j]) for j in order
    }
    for j in order:
        loads[j].start()
    stores = []
    for k in range(count):
        for j in (k % lefts, lefts + k):
            if j in loads:
                loads.pop(j).wait()
        for which, at in enumerate((1 - side, side)):
            part = held_ref[lefts + k, :, pl.ds(pl.multiple_of(at * cols, cols), cols)]
            sums_ref[which, k] = dot_first(held_ref[k % lefts], part).astype(BF)
            copy = pltpu.make_async_copy(
                sums_ref.at[which, k],
                outs[which].at[:, k * cols : (k + 1) * cols],
                out_sems.at[which, k],
            )
            copy.start()
            stores.append(copy)
    wait_all(stores)


def weight_grads(side, lefts, rights):
    count = len(rights)
    length, width = lefts[0].shape
    cols = width // 2
    many = len(lefts) + count
    return pl.pallas_call(
        functools.partial(weight_grads_kernel, count),
        out_shape=(jax.ShapeDtypeStruct((width, count * cols), BF),) * 2,
        in_specs=[SMALL] + [ANYWHERE] * many,
        out_specs=(ANYWHERE,) * 2,
        scratch_shapes=[
            pltpu.VMEM((many, length, width), BF),
            pltpu.VMEM((2, count, width, cols), BF),
            pltpu.SemaphoreType.DMA((many,)),
            pltpu.SemaphoreType.DMA((2, count)),
        ],
        compiler_params=pltpu.CompilerParams(vmem_limit_bytes=VMEM),
        cost_estimate=pl.CostEstimate(
            flops=2 * count * length * width * width,
            bytes_accessed=6 * count * length * width,
            transcendentals=0,
        ),
        name="weight_grads",
    )(side, *lefts, *rights)


def per_device(
    count,
    layer_in,
    segment_ids,
    w_mix_in,
    w_query,
    w_key,
    w_value,
    w_attn_out,
    w_up,
    w_down,
    norm1_gain,
    norm1_bias,
    norm2_gain,
    norm2_bias,
    ssm_decay,
    ssm_inject,
    ssm_readout,
    out_grad,
):
    index = lax.axis_index("dp")
    side = lax.axis_index("tensor")
    at_side = jnp.reshape(side, (1,))
    half = layer_in.shape[2]
    width = layer_in.shape[3]
    tiles = width // LANES
    states = ssm_decay.shape[0]
    cols = w_query.shape[1]
    parts = 2
    units = w_up.shape[1] // parts
    shard_rows = w_mix_in.shape[0]

    norms = jnp.concatenate([norm1_gain, norm1_bias, norm2_gain, norm2_bias])
    norms = jnp.pad(norms[None], ((0, 7), (0, cols - norms.shape[0])))
    mix = [Gather(jnp.concatenate([w_mix_in, norms], axis=0), count, index, DIRECT)]
    send(mix)
    mine_in, got_in = layer_in[:, 0], pair(layer_in[:, 0])
    coefs = jnp.stack([ssm_decay, ssm_inject, ssm_readout])
    coefs_got = pair(coefs)
    fence(mix)
    attn = [
        Gather(
            jnp.concatenate([w_query, w_key, w_value, w_attn_out.T], axis=1), count, index, X_FIRST
        )
    ]
    turned_down = w_down.T
    ffn = [
        [
            Gather(
                jnp.concatenate(
                    [
                        w_up[:, i * units : (i + 1) * units],
                        turned_down[:, i * units : (i + 1) * units],
                    ],
                    axis=1,
                ),
                count,
                index,
                X_FIRST,
            )
        ]
        for i in range(parts)
    ]
    both_ways = (X_FIRST, Y_FIRST)
    while len(mix[0].left) > 1:
        step(mix)
    send(mix + attn)
    fence(mix + attn)
    mix_all = mix[0].result().reshape(count, shard_rows + 8, cols)
    mix_half = mix_all[:, :shard_rows].reshape(width, cols)
    mix_both = (mix_half, pair(mix_half))
    norms_all = mix_all[:, shard_rows, : 4 * shard_rows].reshape(count, 4, shard_rows)
    norms_all = norms_all.astype(F32).transpose(1, 0, 2).reshape(4, width)
    gain_one, bias_one, gain_two, bias_two = (norms_all[i : i + 1] for i in range(4))
    coefs = jnp.where(
        side == 0,
        jnp.concatenate([coefs, coefs_got], axis=2),
        jnp.concatenate([coefs_got, coefs], axis=2),
    )
    decay, inject, readout = coefs.reshape(3, states, tiles, LANES)
    coef = inject * readout
    segments = lax.dynamic_index_in_dim(segment_ids[:, 0], side, 0, keepdims=False)
    starts = jnp.sum(
        (segments[None, :] < jnp.arange(16, dtype=jnp.int32)[:, None]).astype(jnp.int32), axis=1
    )
    seg_col, seg_row = segments[:, None], segments[None, :]
    while len(attn[0].left) > 2:
        step(attn)
    attn = attn[0].split(both_ways)
    send(attn)

    rows, normed, drive, ssm_first, state_mid = ssm_forward(
        starts, at_side, mine_in, got_in, *mix_both, gain_one, bias_one, decay, coef
    )
    state_mid = fence(attn, state_mid)
    send(attn + ffn[0])
    mine_cot, got_cot = out_grad[:, 0], pair(tie(out_grad, state_mid)[0][:, 0])
    ssm_out, cot = ssm_rest(
        starts, at_side, mine_cot, got_cot, drive, decay, coef, state_mid, ssm_first
    )
    ssm_out = fence(attn + ffn[0], ssm_out)
    left, right = ((h, pair(h)) for h in (m.result() for m in attn))
    while len(ffn[0][0].left) > 2:
        step(ffn[0])
    ffn[0] = ffn[0][0].split(both_ways, True)
    send(ffn[0] + ffn[1])
    query, key, value = project(at_side, normed, ssm_out, left, right)
    query = fence(ffn[0], query)
    send(ffn[0])
    attended, lse = attention_forward(seg_col, seg_row, query, key, value)
    attended = fence(ffn[0] + ffn[1], attended)
    while len(ffn[1][0].left) > 2:
        step(ffn[1])
    ffn[1] = ffn[1][0].split(both_ways, True)
    send(ffn[1])
    middle, normed_two = middle_of(at_side, attended, right, rows, gain_two, bias_two)

    middle, normed_two = fence(ffn[1], middle, normed_two)
    send(ffn[1])

    def scatters(left, right, singly=False):
        return [
            Scatter(left, count, index, X_FIRST, singly),
            Scatter(right, count, index, Y_FIRST, singly),
        ]

    normed_other = pair(normed_two)
    *both, grad_up, grad_down = feed_forward(
        0, normed_two, normed_other, cot, *ffn[0], ()
    )
    both, grad_up, grad_down = fence(ffn[1], both, grad_up, grad_down)
    sums_one = scatters(grad_up, grad_down)
    send(sums_one)
    own, other, gown, gother, grad_up, grad_down = feed_forward(
        1, normed_two, normed_other, cot, *ffn[1], both
    )
    own, other, gown, gother, grad_up, grad_down = fence(
        sums_one, own, other, gown, gother, grad_up, grad_down
    )
    send(sums_one)
    sums_two = scatters(grad_up, grad_down, True)

    grad_middle, grad_branch, grad_attended, norm_two_sums = norm_two_back(
        at_side, gown, pair(gother), middle, cot, gain_two, right
    )
    grad_attended = fence(sums_one, grad_attended)
    join_chains(sums_one)
    send(sums_one + sums_two)
    grad_query, grad_key, grad_value = attention_backward(
        seg_col, seg_row, query, key, value, lse, grad_attended
    )
    grad_query, grad_key, grad_value = fence(
        sums_one + sums_two, grad_query, grad_key, grad_value
    )
    send(sums_two)

    def pair_sum(theirs, mine):
        return (mine.astype(F32) + pair(theirs).astype(F32)).astype(BF)

    grads_left = weight_grads(at_side, (normed, grad_branch), (grad_query, attended))
    grads_left, ssm_out = tie(grads_left, ssm_out)
    grads_right = weight_grads(at_side, (ssm_out,), (grad_key, grad_value))
    sums_left = pair_sum(*grads_left)
    grads_right = fence(sums_two, grads_right)
    sums_attn = [
        Scatter(
            jnp.concatenate([sums_left, pair_sum(*grads_right)], axis=1), count, index, DIRECT
        )
    ]
    join_chains(sums_two)
    send(sums_attn + sums_two)
    grad_mixed, state_sum, state_dsum = ssm_backward(
        starts, at_side, grad_key, grad_value, left, right, drive, decay, coef
    )
    grad_mixed = fence(sums_attn + sums_two, grad_mixed)
    send(sums_attn)
    grads_mix = weight_grads(at_side, (normed,), (grad_mixed,))
    grads_mix, grad_mixed = tie(grads_mix, grad_mixed)
    sums_mix = [Scatter(pair_sum(*grads_mix), count, index, DIRECT)]
    sums_mix[0].values, grad_mixed = tie(sums_mix[0].values, grad_mixed)
    send(sums_mix)
    for_partner, norm_one_first = norm_one_back(
        at_side, grad_query, grad_mixed, rows, grad_middle, gain_one, left, mix_both, True
    )
    for_partner, norm_one_first, grad_mixed = fence(
        sums_mix + sums_attn, for_partner, norm_one_first, grad_mixed
    )
    send(sums_mix + sums_two)
    got_grad = pair(for_partner)
    in_grad, norm_one_second = norm_one_back(
        at_side, grad_query, grad_mixed, rows, grad_middle, gain_one, left, mix_both, False
    )
    in_grad, norm_one_second, middle, own, other = fence(
        sums_mix + sums_two, in_grad, norm_one_second, middle, own, other
    )

    state_sums = jnp.concatenate([state_sum, state_dsum]).reshape(
        2 * states, width
    )
    sums = jnp.concatenate(
        [
            lax.dynamic_slice_in_dim(state_sums, (1 - side) * cols, cols, 1),
            (norm_one_first + norm_one_second).reshape(-1, cols),
            norm_two_sums.reshape(-1, cols),
        ]
    )
    mine = lax.dynamic_slice_in_dim(state_sums, side * cols, cols, 1)
    small = [Total(jnp.concatenate([mine, sums[2 * states :]]) + pair(sums), count)]
    send(small)
    in_half = (1 - side) * half
    partner_sum = pair(
        lax.dynamic_slice_in_dim(middle, in_half, half, 0)
        + lax.dynamic_slice_in_dim(own, in_half, half, 0).astype(F32)
    )
    partner_other = pair(lax.dynamic_slice_in_dim(other, in_half, half, 0))
    in_grad = put(at_side, got_grad, in_grad)
    in_grad, middle = fence(small, in_grad, middle)
    send(small)
    layer_out = layer_out_of(at_side, middle, own, other, partner_sum, partner_other)
    layer_out = fence(small, layer_out)
    complete(sums_mix + small + sums_attn + sums_one + sums_two)
    small = small[0].values
    total, dtotal = small[:states], small[states : 2 * states]
    norm_sums = lax.dynamic_slice_in_dim(
        small[2 * states :].reshape(4, width), index * shard_rows, shard_rows, 1
    )
    shard_attn = sums_attn[0].result()
    shards = [sums_one[0].result(), sums_two[0].result()]
    return (
        layer_out[:, None],
        in_grad[:, None],
        sums_mix[0].result(),
        shard_attn[:, :cols],
        shard_attn[:, 2 * cols : 3 * cols],
        shard_attn[:, 3 * cols :],
        shard_attn[:, cols : 2 * cols].T,
        jnp.concatenate([v[:, :units] for v in shards], axis=1),
        jnp.concatenate([v[:, units:] for v in shards], axis=1).T,
        norm_sums[0],
        norm_sums[1],
        norm_sums[2],
        norm_sums[3],
        ssm_inject * ssm_readout * dtotal,
        ssm_readout * total,
        ssm_inject * total,
    )


def solution(mesh):
    return jax.shard_map(
        functools.partial(per_device, mesh.shape["dp"]),
        mesh=mesh,
        in_specs=(
            P(None, "dp", "tensor", None),
            P(None, "dp", None),
            P("dp", "tensor"),
            P("dp", "tensor"),
            P("dp", "tensor"),
            P("dp", "tensor"),
            P("tensor", "dp"),
            P("dp", "tensor"),
            P("tensor", "dp"),
            P("dp"),
            P("dp"),
            P("dp"),
            P("dp"),
            P(None, "tensor"),
            P(None, "tensor"),
            P(None, "tensor"),
            P(None, "dp", "tensor", None),
        ),
        out_specs=(
            P(None, "dp", "tensor", None),
            P(None, "dp", "tensor", None),
            P("dp", "tensor"),
            P("dp", "tensor"),
            P("dp", "tensor"),
            P("dp", "tensor"),
            P("tensor", "dp"),
            P("dp", "tensor"),
            P("tensor", "dp"),
            P("dp"),
            P("dp"),
            P("dp"),
            P("dp"),
            P(None, "tensor"),
            P(None, "tensor"),
            P(None, "tensor"),
        ),
        check_vma=False,
    )
```
